32 devices in a mesh: req: 8 (over z, y), tp: 4 (over x, core).
Axes of the slice: x: 2, y: 2, z: 4, core: 2. Of those that a mesh axis runs over, the one named last changes fastest.
Arguments:
- drafts: bfloat16 [16, 64, 1536], P('req'), may hold values from -27 to 27, as said below
- gain_attn: float32 [1536], replicated, may hold values from 0.1 to 1.9
- w_query: bfloat16 [1536, 1536], P(None, 'tp'), may hold values from -0.15625 to 0.15625
- key_value_weight: bfloat16 [1536, 512], replicated, may hold values from -0.15625 to 0.15625
- w_output: bfloat16 [1536, 1536], P('tp'), may hold values from -0.5 to 0.5
- cache: bfloat16 [16, 2, 2, 3072, 128], P('req'), may hold values from -130 to 130, as said below
- lengths: int32 [16], P('req'), may hold values from 1 to 3072, 16384 in all
- tree_mask: int32 [16, 64, 64], P('req'), may hold values from 0 to 1, as said below
- depths: int32 [16, 64], P('req'), may hold values from 0 to 63, as said below
- gain_moe: float32 [1536], replicated, may hold values from 0.1 to 1.9
- w_router: bfloat16 [1536, 32], replicated, may hold values from -0.15625 to 0.15625
- expert_ids: int32 [16, 64, 4], P('req'), may hold values from 0 to 31, all different within a row; in each aligned block of 128 rows (0 to 127, 128 to 255, ..., all dimensions but the last counted through in order) at most 32 rows name the same one
- w_in: bfloat16 [64, 1536, 2, 384], P('req'), may hold values from -0.15625 to 0.15625
- w_out: bfloat16 [64, 384, 1536], P('req'), may hold values from -0.21875 to 0.21875
- slots: int32 [16, 64], P('req'), may hold values from -1 to 15, as said below
- order: int32 [16], P('req'), may hold values from 0 to 15, each once
Outputs:
- tree_out: bfloat16 [16, 64, 1536], P('req', None, 'tp')
- accepted: bfloat16 [16, 16, 1536], P('req', None, 'tp')
The draws below stay inside these ranges and needn't reach their ends.
Inputs may be any that keep to these rules, and one draw needn't show every extreme that they name: `drafts`: values lie within this range. `cache`: values lie within this range. `tree_mask`: each request's tokens form a tree rooted at token 0, the parent of token t being one of tokens t - 4 to t - 1; entry [s, i, j] is 1 exactly when j is i or an ancestor of i. `depths`: depth of each token in its tree, agreeing with tree_mask; the root has depth 0. In every draw some request's tree is a single chain. In each request the tokens on the path from the root to one token of depth d carry slots 0 to d (their depths), with d + 1 <= 16; all other tokens carry -1. In every draw some request fills all 16 slots. `expert_ids`: each token names 4 different experts; among the tokens of one device no expert is named by more than 32 tokens. `order`: each request is served in exactly one serving slot.
All inputs are finite; a program needn't handle non-finite values. No bound on the sum of `lengths` on one device may be relied on, other than what follows from the above.
Results may differ from the reference program's by a relative error of at most 0.011.
Values may be sent and summed in bfloat16 or wider, within the bound.
No kernel may reach another device: no remote copies, remote signals or barrier semaphores. Data moves between devices by JAX's collectives and lax.ppermute only.
A program may use at most 128 MiB of HBM per device.

```python
import math
import jax
import jax.numpy as jnp
import numpy as np
from jax import lax

MODEL_WIDTH = 1536
QUERY_HEADS = 12
KEY_VALUE_HEADS = 2
HEAD_SIZE = 128
EXPERTS = 32
FF = 768
TOPK = 4
TREE = 64
KEEP = 16
REQ_DEV = 2
CACHE_LONGEST = 3072
REQUEST_TOTAL = 16
CAP = 32
N_REQ = 8


def draw_drafts(key, part):
    key_a, random_key_second, random_key_third = jax.random.split(jax.random.fold_in(key, 3), 3)
    row_scale = jnp.exp(jax.random.uniform(key_a, (REQUEST_TOTAL, TREE, 1), jnp.float32, jnp.log(0.3), jnp.log(3.0)))
    col_scale = jnp.exp(jax.random.uniform(random_key_second, (MODEL_WIDTH,), jnp.float32, jnp.log(0.3), jnp.log(3.0)))
    noise = jnp.clip(jax.random.normal(random_key_third, (REQUEST_TOTAL, TREE, MODEL_WIDTH), jnp.float32), -3.0, 3.0)
    return (noise * row_scale * col_scale).astype(jnp.bfloat16)


def draw_cache(key, part):
    key_a = jax.random.fold_in(jax.random.fold_in(key, 5), 0)
    array_shape = (REQUEST_TOTAL, 2, KEY_VALUE_HEADS, CACHE_LONGEST, HEAD_SIZE)
    values = jnp.clip(jax.random.normal(key_a, array_shape, jnp.float32), -4.0, 4.0)
    return values.astype(jnp.bfloat16)


def tree_parts(key):
    key_a, random_key_second, random_key_third, key_d = jax.random.split(jax.random.fold_in(key, 11), 4)
    index = jnp.arange(TREE, dtype=jnp.int32)
    row_ids = jnp.arange(REQUEST_TOTAL, dtype=jnp.int32)
    forced = jax.random.randint(random_key_third, (), 0, REQUEST_TOTAL)
    lowest = jnp.maximum(index - 4, 0)
    span = jnp.maximum(index - lowest, 1)
    parent = lowest[None, :] + jax.random.randint(key_a, (REQUEST_TOTAL, TREE), 0, 1 << 20) % span[None, :]
    chain = jnp.maximum(index - 1, 0)
    parent = jnp.where((row_ids == forced)[:, None], chain[None, :], parent)
    depth0 = jnp.zeros((REQUEST_TOTAL, TREE), jnp.int32)
    ancest0 = jnp.zeros((REQUEST_TOTAL, TREE, TREE), jnp.int32).at[:, 0, 0].set(1)

    def grow(node, carry):
        depth, ancest = carry
        parents = parent[:, node]
        new_depth = depth[row_ids, parents] + 1
        new_row = jnp.maximum(ancest[row_ids, parents], (index == node).astype(jnp.int32)[None, :])
        return (depth.at[:, node].set(new_depth), ancest.at[:, node].set(new_row))
    depth, ancest = lax.fori_loop(1, TREE, grow, (depth0, ancest0))
    target = jax.random.randint(random_key_second, (REQUEST_TOTAL,), KEEP // 2, KEEP)
    target = jnp.where(row_ids == forced, KEEP - 1, target)
    score = jnp.where(depth == target[:, None], jax.random.randint(key_d, (REQUEST_TOTAL, TREE), 0, 1 << 16) * TREE + index[None, :] + 1, 0)
    leaf = jnp.argmax(score, axis=1)
    on_path = ancest[row_ids, leaf]
    slot_vals = jnp.where(on_path > 0, depth, -1)
    return (ancest, depth, slot_vals)


def draw_tree_mask(key, part):
    return tree_parts(key)[0]


def draw_depths(key, part):
    return tree_parts(key)[1]


def draw_slots(key, part):
    return tree_parts(key)[2]


def level_of(stream_key, dims, shards, least, largest):
    def one(position, parts):
        heights = jax.random.uniform(jax.random.fold_in(jax.random.fold_in(stream_key, 6), position), (parts,), jnp.float32, least / len(shards), largest / len(shards))
        return jnp.repeat(jnp.exp(heights), dims[position] // parts).reshape((-1,) + (1,) * (len(dims) - position - 1))

    factor_of = one(*shards[0])
    for cut in shards[1:]:
        factor_of = factor_of * one(*cut)
    return factor_of


def length_profile(number_of, total, reach, slope):
    weights = [(1 << 20) // math.isqrt(grade ** slope) + 1 for grade in range(2, number_of + 1)]
    surplus, holding = total - reach - (number_of - 1), [1] * (number_of - 1)
    while surplus > 0:
        movable = [i for i in range(number_of - 1) if holding[i] < reach]
        mass, left = sum([weights[i] for i in movable]), surplus
        for i in movable:
            more = min(reach - holding[i], max(1, left * weights[i] // mass), surplus)
            holding[i] = holding[i] + more
            surplus = surplus - more
    return np.array([reach] + holding)


def uneven(stream_key, amount, total, bound, lean):
    if amount == 2:
        one = jax.random.randint(stream_key, (), max(1, total - bound), min(bound, total - 1) + 1)
        return jnp.stack([one, total - one])
    tallies = jnp.asarray(length_profile(amount, total, bound, lean), jnp.int32)
    couples = (amount - 1) // 2
    donor, taker = tallies[1:1 + 2 * couples:2], tallies[2:2 + 2 * couples:2]
    margin = jnp.minimum(donor - 1, bound - taker)
    passed = jax.random.randint(jax.random.fold_in(stream_key, 1), (couples,), 0, 1 << 20) % (margin + 1)
    tallies = tallies.at[1:1 + 2 * couples:2].set(donor - passed).at[2:2 + 2 * couples:2].set(taker + passed)
    return tallies[jax.random.permutation(jax.random.fold_in(stream_key, 2), amount)]


def routed_block(own_key, own, number, rows, count, top, reach, slope):
    order = jax.random.permutation(own_key, count)
    crowded, usual = shares(count, rows * top, reach, slope, True), shares(count, rows * top, reach, slope, False)
    places = jnp.arange(count)

    def named(tallies, turn):
        used = int((tallies > 0).sum())
        fixed = max(1, used // 4)
        shifted = fixed + (places - fixed + turn * (used - fixed)) % max(1, count - fixed)
        return jnp.zeros((count,), jnp.int32).at[order[jnp.where(places < fixed, places, shifted)]].set(jnp.asarray(tallies, jnp.int32))

    tallies = jnp.where(number % 4 == 0, named(crowded, number // 4), named(usual, number - number // 4 - 1))
    mixed = jax.random.permutation(jax.random.fold_in(own, 3), count)
    donor, receiver = mixed[0:count // 2 * 2:2], mixed[1:count // 2 * 2:2]
    room = jnp.minimum(tallies[donor] - 1, reach - tallies[receiver]) // 2
    room = jnp.where((donor == order[0]) | (receiver == order[0]) | (tallies[receiver] == 0), 0, jnp.maximum(room, 0))
    shifted = jax.random.randint(jax.random.fold_in(own, 4), (count // 2,), 0, 1 << 20) % (room + 1)
    tallies = tallies.at[donor].add(-shifted).at[receiver].add(shifted)
    items = jnp.searchsorted(jnp.cumsum(tallies), jnp.arange(rows * top), side="right").astype(jnp.int32)
    table = items.reshape(top, rows).T
    table = table[jax.random.permutation(jax.random.fold_in(own, 1), rows)]
    turn = jax.random.randint(jax.random.fold_in(own, 2), (rows, 1), 0, top)
    return jnp.take_along_axis(table, (jnp.arange(top)[None, :] + turn) % top, axis=1)


def shares(amount, total, most, slope, full):
    portions = [(1 << 20) // math.isqrt(standing ** slope) + 1 for standing in range(1, amount + 1)]
    largest = most if full else min(most, max(-(-total // amount), total * portions[0] // sum(portions)))
    least = 1 if total - largest >= amount - 1 else 0
    holding, spare = [largest] + [least] * (amount - 1), total - largest - least * (amount - 1)
    while spare > 0:
        free = [i for i in range(1, amount) if holding[i] < largest] or [i for i in range(1, amount) if holding[i] < most]
        pool, budget = sum([portions[i] for i in free]), spare
        for i in free:
            addition = min(most - holding[i], max(1, budget * portions[i] // pool), spare)
            holding[i] = holding[i] + addition
            spare = spare - addition
    return np.array(holding)


def normal_values(rng, dims, deviation, most, cuts=(), kind=jnp.bfloat16):
    drawn = deviation * jax.random.normal(rng, dims, jnp.float32)
    if cuts:
        drawn = drawn * level_of(rng, dims, cuts, -0.22, 0.18)
    return jnp.clip(drawn, -most, most).astype(kind)


def setup_inputs(seed: int = 0) -> dict:
    streams_of = jax.random.split(jax.random.key(seed), 17)
    drafts = draw_drafts(jax.random.fold_in(streams_of[16], 71), 0)
    gain_attn = jnp.clip(1.0 + 0.18 * jax.random.normal(streams_of[1], (MODEL_WIDTH,), jnp.float32), 0.1, 1.9)
    w_query = normal_values(streams_of[2], (MODEL_WIDTH, QUERY_HEADS * HEAD_SIZE), MODEL_WIDTH ** -0.5, 0.15625, ((1, 4),))
    key_value_weight = normal_values(streams_of[3], (MODEL_WIDTH, 2 * KEY_VALUE_HEADS * HEAD_SIZE), MODEL_WIDTH ** -0.5, 0.15625)
    w_output = normal_values(streams_of[4], (QUERY_HEADS * HEAD_SIZE, MODEL_WIDTH), HEAD_SIZE ** -0.5, 0.5, ((0, 4),))
    cache = draw_cache(jax.random.fold_in(streams_of[16], 71), 0)
    lengths = uneven(streams_of[6], REQUEST_TOTAL, REQUEST_TOTAL * CACHE_LONGEST // 3, CACHE_LONGEST, 2).astype(jnp.int32)
    tree_mask = draw_tree_mask(jax.random.fold_in(streams_of[16], 71), 0)
    depths = draw_depths(jax.random.fold_in(streams_of[16], 71), 0)
    gain_moe = jnp.clip(1.0 + 0.18 * jax.random.normal(streams_of[9], (MODEL_WIDTH,), jnp.float32), 0.1, 1.9)
    w_router = normal_values(streams_of[10], (MODEL_WIDTH, EXPERTS), MODEL_WIDTH ** -0.5, 0.15625)
    expert_ids_keys = jax.random.split(jax.random.fold_in(streams_of[11], 1), REQUEST_TOTAL * TREE // (REQ_DEV * TREE))
    expert_ids_turns = jax.random.permutation(jax.random.fold_in(streams_of[11], 3), REQUEST_TOTAL * TREE // (REQ_DEV * TREE))
    expert_ids = jax.vmap(lambda own, number: routed_block(jax.random.fold_in(streams_of[11], 2), own, number, REQ_DEV * TREE, EXPERTS, TOPK, CAP, 2))(expert_ids_keys, expert_ids_turns).reshape((REQUEST_TOTAL, TREE, TOPK))
    w_in = normal_values(streams_of[12], (2 * EXPERTS, MODEL_WIDTH, 2, FF // 2), MODEL_WIDTH ** -0.5, 0.15625, ((0, 8),))
    w_out = normal_values(streams_of[13], (2 * EXPERTS, FF // 2, MODEL_WIDTH), FF ** -0.5, 0.21875, ((0, 8),))
    slots = draw_slots(jax.random.fold_in(streams_of[16], 71), 0)
    order = jax.random.permutation(streams_of[15], REQUEST_TOTAL).astype(jnp.int32)
    return {"drafts": drafts, "gain_attn": gain_attn, "w_query": w_query, "key_value_weight": key_value_weight, "w_output": w_output, "cache": cache, "lengths": lengths, "tree_mask": tree_mask, "depths": depths, "gain_moe": gain_moe, "w_router": w_router, "expert_ids": expert_ids, "w_in": w_in, "w_out": w_out, "slots": slots, "order": order}


EPSILON = 1e-06
THETA = 1000000.0

def rms_norm(values, gain_vec):
    return values * lax.rsqrt(lax.optimization_barrier(jnp.mean(values * values, axis=-1, keepdims=True)) + EPSILON) * gain_vec

def rotary(values, positions):
    half_dim = values.shape[-1] // 2
    freqs = jnp.exp(-jnp.log(THETA) * jnp.arange(half_dim, dtype=jnp.float32) / half_dim)
    angles = positions.astype(jnp.float32)[..., None] * freqs
    cosine = jnp.cos(angles)
    sine = jnp.sin(angles)
    first = values[..., :half_dim]
    second = values[..., half_dim:]
    return jnp.concatenate([first * cosine - second * sine, second * cosine + first * sine], axis=-1)

def reference(drafts, gain_attn, w_query, key_value_weight, w_output, cache, lengths, tree_mask, depths, gain_moe, w_router, expert_ids, w_in, w_out, slots, order):
    request_list, draft_tree, width = drafts.shape
    cache_len = cache.shape[3]
    head_group = QUERY_HEADS // KEY_VALUE_HEADS
    scale = HEAD_SIZE ** (-0.5)
    inputs = drafts.astype(jnp.float32).reshape(request_list * draft_tree, width)
    normalized_input = rms_norm(inputs, gain_attn).astype(jnp.bfloat16)
    positions = lengths[:, None] + depths
    query_all = jnp.dot(normalized_input, w_query, preferred_element_type=jnp.float32).reshape(request_list, draft_tree, QUERY_HEADS, HEAD_SIZE)
    key_value = jnp.dot(normalized_input, key_value_weight, preferred_element_type=jnp.float32).reshape(request_list, draft_tree, 2, KEY_VALUE_HEADS, HEAD_SIZE)
    query_all = rotary(query_all, positions[:, :, None]).astype(jnp.bfloat16)
    key_new = rotary(key_value[:, :, 0], positions[:, :, None]).astype(jnp.bfloat16)
    val_new = key_value[:, :, 1].astype(jnp.bfloat16)

    def attend(pack):
        query_request, k_req, v_req, c_req, limit, allowed = pack
        query_heads_rows = query_request.astype(jnp.float32).reshape(draft_tree, KEY_VALUE_HEADS, head_group, HEAD_SIZE)
        cache_scores = jnp.einsum('tkgd,kcd->kgtc', query_heads_rows, c_req[0].astype(jnp.float32)) * scale
        tree_scores = jnp.einsum('tkgd,skd->kgts', query_heads_rows, k_req.astype(jnp.float32)) * scale
        inside = jnp.arange(cache_len) < limit
        cache_scores = jnp.where(inside[None, None, None, :], cache_scores, -jnp.inf)
        tree_scores = jnp.where((allowed > 0)[None, None], tree_scores, -jnp.inf)
        peak = jnp.maximum(lax.optimization_barrier(jnp.max(cache_scores, axis=-1)), lax.optimization_barrier(jnp.max(tree_scores, axis=-1)))
        cache_w = jnp.exp(cache_scores - peak[..., None])
        tree_w = jnp.exp(tree_scores - peak[..., None])
        totals = lax.optimization_barrier(jnp.sum(cache_w, axis=-1)) + lax.optimization_barrier(jnp.sum(tree_w, axis=-1))
        cache_p = cache_w.astype(jnp.bfloat16).astype(jnp.float32)
        tree_p = tree_w.astype(jnp.bfloat16).astype(jnp.float32)
        mixed = jnp.einsum('kgtc,kcd->kgtd', cache_p, c_req[1].astype(jnp.float32))
        mixed = mixed + jnp.einsum('kgts,skd->kgtd', tree_p, v_req.astype(jnp.float32))
        mixed = mixed / totals[..., None]
        return mixed.transpose(2, 0, 1, 3).reshape(draft_tree, QUERY_HEADS * HEAD_SIZE).astype(jnp.bfloat16)
    heads = lax.map(attend, (query_all, key_new, val_new, cache, lengths, tree_mask))
    attn = jnp.dot(heads.reshape(request_list * draft_tree, QUERY_HEADS * HEAD_SIZE), w_output, preferred_element_type=jnp.float32)
    resid = inputs + attn
    normed2 = rms_norm(resid, gain_moe).astype(jnp.bfloat16)
    logits = jnp.dot(normed2, w_router, preferred_element_type=jnp.float32)
    ids = expert_ids.reshape(request_list * draft_tree, TOPK)
    chosen = jax.nn.sigmoid(jnp.take_along_axis(logits, ids, axis=1))
    gates = (chosen / lax.optimization_barrier(jnp.sum(chosen, axis=1, keepdims=True))).astype(jnp.bfloat16)
    half_ff = FF // 2
    gate_up = w_in.reshape(EXPERTS, 2, width, 2, half_ff).transpose(0, 2, 3, 1, 4).reshape(EXPERTS, width, 2, FF)
    down = w_out.reshape(EXPERTS, FF, width)
    most_rows = N_REQ * CAP

    def expert_step(carry, expert):
        hits = jnp.any(ids == expert, axis=1)
        picked = jnp.nonzero(hits, size=most_rows, fill_value=0)[0]
        valid = jnp.arange(most_rows) < jnp.sum(hits.astype(jnp.int32))
        rows_in = normed2[picked]
        weights_in = lax.dynamic_index_in_dim(gate_up, expert, 0, keepdims=False)
        weights_down = lax.dynamic_index_in_dim(down, expert, 0, keepdims=False)
        gate = jnp.dot(rows_in, weights_in[:, 0], preferred_element_type=jnp.float32)
        upper = jnp.dot(rows_in, weights_in[:, 1], preferred_element_type=jnp.float32)
        act = (jax.nn.relu(gate) * upper).astype(jnp.bfloat16)
        output = jnp.zeros((most_rows, width), jnp.float32)
        for half_index in range(2):
            piece_out = jnp.dot(act[:, half_index * half_ff:(half_index + 1) * half_ff], weights_down[half_index * half_ff:(half_index + 1) * half_ff], preferred_element_type=jnp.float32)
            rounded = lax.optimization_barrier(piece_out.astype(jnp.bfloat16))
            output = output + rounded.astype(jnp.float32)
        token_gate = lax.optimization_barrier(jnp.sum(jnp.where(ids == expert, gates.astype(jnp.float32), 0.0), axis=1))
        row_gate = jnp.where(valid, token_gate[picked], 0.0)
        return (carry.at[picked].add(row_gate[:, None] * output), None)
    mixture, unused = lax.scan(expert_step, jnp.zeros((request_list * draft_tree, width), jnp.float32), jnp.arange(EXPERTS).astype(jnp.int32))
    tree_out = (resid + mixture).astype(jnp.bfloat16).reshape(request_list, draft_tree, width)
    dest_req = jnp.broadcast_to(order[:, None], slots.shape)
    dest_slot = jnp.where(slots >= 0, slots, KEEP)
    accepted = jnp.zeros((request_list, KEEP, width), jnp.bfloat16).at[dest_req, dest_slot].set(tree_out, mode='drop')
    return (tree_out, accepted)
```

```python
import functools

import jax
import jax.numpy as jnp
from jax import lax
from jax.experimental import pallas as pl
from jax.experimental.pallas import tpu as pltpu
from jax.sharding import PartitionSpec as P

KEEP = 16
CAP = 32


EPSILON = 1e-06
THETA = 1000000.0
LOG2E = 1.4426950408889634
BLOCK = 512


def rms_norm(values, gain_vec):
    return (
        values * lax.rsqrt(jnp.mean(values * values, axis=-1, keepdims=True) + EPSILON) * gain_vec
    )


def column_of(row):
    count = row.shape[1]
    at_row = lax.broadcasted_iota(jnp.int32, (count, count), 0)
    at_col = lax.broadcasted_iota(jnp.int32, (count, count), 1)
    return jnp.sum(jnp.where(at_row == at_col, row, 0.0), axis=1, keepdims=True)


def attention_kernel(
    lengths_ref,
    place_ref,
    drafts_ref,
    gain_ref,
    freqs_ref,
    depths_ref,
    mask_ref,
    wq_hbm,
    wkv_hbm,
    wo_hbm,
    cache_hbm,
    mine_ref,
    theirs_ref,
    wq,
    wk,
    wv,
    wo,
    keys,
    vals,
    scores,
    weight_sem,
    cache_sem,
):
    req_dev, tree, width = drafts_ref.shape
    head_dim = cache_hbm.shape[-1]
    kv_heads = cache_hbm.shape[2]
    local_heads = wq.shape[1] // head_dim
    block = scores.shape[2]
    kv_head = place_ref[0]
    first = place_ref[1]

    def column_copy(target, which, sem):
        start = pl.multiple_of((which * kv_heads + kv_head) * head_dim, head_dim)
        return pltpu.make_async_copy(wkv_hbm.at[:, pl.ds(start, head_dim)], target, sem)

    def cache_copy(request, which, index):
        rows = pl.ds(pl.multiple_of(index * block, block), block)
        target = vals if which else keys
        return pltpu.make_async_copy(
            cache_hbm.at[request, which, kv_head, rows],
            target.at[request, rows],
            cache_sem.at[request, which, index],
        )

    copy_q = pltpu.make_async_copy(wq_hbm, wq, weight_sem.at[0])
    copy_k = column_copy(wk, 0, weight_sem.at[1])
    copy_v = column_copy(wv, 1, weight_sem.at[2])
    copy_o = pltpu.make_async_copy(wo_hbm, wo, weight_sem.at[3])
    copy_q.start()
    copy_k.start()
    copy_v.start()
    limits = [lengths_ref[request] for request in range(req_dev)]
    counts = [(limit + block - 1) // block for limit in limits]
    for request in range(req_dev):
        for which in range(2):

            @pl.loop(0, counts[request])
            def _(index, request=request, which=which):
                cache_copy(request, which, index).start()

    copy_o.start()

    inputs = drafts_ref[...].astype(jnp.float32).reshape(req_dev * tree, width)
    normed = rms_norm(inputs, gain_ref[...]).astype(jnp.bfloat16)
    at = [
        column_of(depths_ref[request : request + 1, :].astype(jnp.float32))
        + limits[request].astype(jnp.float32)
        for request in range(req_dev)
    ]
    angles = jnp.concatenate(at, axis=0) * freqs_ref[...]
    cosine = jnp.cos(angles)
    lane = lax.broadcasted_iota(jnp.int32, angles.shape, 1)
    sine = jnp.sin(angles) * jnp.where(lane < head_dim // 2, -1.0, 1.0)

    def turned(vectors):
        return (vectors * cosine + pltpu.roll(vectors, head_dim // 2, 1) * sine).astype(jnp.bfloat16)

    copy_q.wait()
    query_all = jnp.dot(normed, wq[...], preferred_element_type=jnp.float32)
    queries = [
        turned(query_all[:, head * head_dim : (head + 1) * head_dim]) for head in range(local_heads)
    ]
    copy_k.wait()
    key_new = turned(jnp.dot(normed, wk[...], preferred_element_type=jnp.float32))
    copy_v.wait()
    val_new = jnp.dot(normed, wv[...], preferred_element_type=jnp.float32).astype(jnp.bfloat16)
    slope = LOG2E * head_dim ** (-0.5)
    rows = local_heads * tree
    contract = (((1,), (1,)), ((), ()))

    def lanes_down(values, step):
        parts = [values[:, i : i + 128] for i in range(0, values.shape[1], 128)]
        return functools.reduce(step, parts)

    mixed = []
    for request in range(req_dev):
        span = slice(request * tree, (request + 1) * tree)
        own = jnp.concatenate([q[span] for q in queries], axis=0)
        allowed = jnp.concatenate([mask_ref[request]] * local_heads, axis=0) > 0
        tree_scores = lax.dot_general(
            own, key_new[span], contract, preferred_element_type=jnp.float32
        )
        tree_scores = jnp.where(allowed, tree_scores, -jnp.inf)
        limit = limits[request]

        def score_step(index, best, request=request, own=own, limit=limit):
            cache_copy(request, 0, index).wait()
            offset = pl.multiple_of(index * block, block)
            found = lax.dot_general(
                own,
                keys[request, pl.ds(offset, block)],
                contract,
                preferred_element_type=jnp.float32,
            )
            inside = offset + lax.broadcasted_iota(jnp.int32, found.shape, 1) < limit
            found = jnp.where(inside, found, -jnp.inf)
            scores[index] = found
            return jnp.maximum(best, lanes_down(found, jnp.maximum))

        best = lax.fori_loop(
            0, counts[request], score_step, jnp.full((rows, 128), -jnp.inf, jnp.float32)
        )
        peak = jnp.maximum(
            jnp.max(best, axis=1, keepdims=True), jnp.max(tree_scores, axis=1, keepdims=True)
        )
        tree_weights = jnp.exp2((tree_scores - peak) * slope)
        start = (
            jnp.zeros((rows, 128), jnp.float32),
            jnp.dot(
                tree_weights.astype(jnp.bfloat16), val_new[span], preferred_element_type=jnp.float32
            ),
        )

        def sum_step(index, carry, request=request, peak=peak):
            total, accum = carry
            cache_copy(request, 1, index).wait()
            offset = pl.multiple_of(index * block, block)
            weights = jnp.exp2((scores[index] - peak) * slope)
            accum = accum + jnp.dot(
                weights.astype(jnp.bfloat16),
                vals[request, pl.ds(offset, block)],
                preferred_element_type=jnp.float32,
            )
            return total + lanes_down(weights, jnp.add), accum

        total, accum = lax.fori_loop(0, counts[request], sum_step, start)
        total = jnp.sum(total, axis=1, keepdims=True) + jnp.sum(tree_weights, axis=1, keepdims=True)
        mixed.append((accum / total).astype(jnp.bfloat16))

    copy_o.wait()
    for request in range(req_dev):
        heads = jnp.concatenate(
            [mixed[request][head * tree : (head + 1) * tree] for head in range(local_heads)], axis=1
        )
        part = jnp.dot(heads, wo[...], preferred_element_type=jnp.float32).astype(jnp.bfloat16)

        @pl.when(first == request)
        def _(part=part):
            mine_ref[...] = part

        @pl.when(first != request)
        def _(part=part):
            theirs_ref[...] = part


def attention_part(
    drafts, gain, w_query, key_value_weight, w_output, cache, lengths, tree_mask, depths, place
):
    req_dev, tree, width = drafts.shape
    head_dim = cache.shape[-1]
    longest = cache.shape[3]
    block = min(BLOCK, longest)
    local = w_query.shape[1]
    half_dim = head_dim // 2
    freqs = jnp.exp(-jnp.log(THETA) * jnp.arange(half_dim, dtype=jnp.float32) / half_dim)
    freqs = jnp.tile(freqs, 2).reshape(1, head_dim)
    whole = pl.BlockSpec(memory_space=pltpu.VMEM)
    scalar = pl.BlockSpec(memory_space=pltpu.SMEM)
    anywhere = pl.BlockSpec(memory_space=pl.ANY)
    bf16 = jnp.bfloat16
    return pl.pallas_call(
        attention_kernel,
        out_shape=[jax.ShapeDtypeStruct((tree, width), bf16)] * 2,
        in_specs=[scalar] * 2 + [whole] * 5 + [anywhere] * 4,
        out_specs=[whole] * 2,
        scratch_shapes=[
            pltpu.VMEM((width, local), bf16),
            pltpu.VMEM((width, head_dim), bf16),
            pltpu.VMEM((width, head_dim), bf16),
            pltpu.VMEM((local, width), bf16),
            pltpu.VMEM((req_dev, longest, head_dim), bf16),
            pltpu.VMEM((req_dev, longest, head_dim), bf16),
            pltpu.VMEM((longest // block, local // head_dim * tree, block), jnp.float32),
            pltpu.SemaphoreType.DMA((4,)),
            pltpu.SemaphoreType.DMA((req_dev, 2, longest // block)),
        ],
        compiler_params=pltpu.CompilerParams(vmem_limit_bytes=32 * 1024 * 1024),
        name="attention",
    )(
        lengths,
        place,
        drafts,
        gain.reshape(1, width),
        freqs,
        depths,
        tree_mask,
        w_query,
        key_value_weight,
        w_output,
        cache,
    )


def dispatch_kernel(
    place_ref, half_ref, other_ref, drafts_ref, gain_ref, matrix_ref, sent_ref, normed_ref, resid
):
    tree = half_ref.shape[0]
    first = place_ref[1]
    resid[pl.ds(first, 1)] = half_ref[...].astype(jnp.float32)[None]
    resid[pl.ds(1 - first, 1)] = other_ref[...].astype(jnp.float32)[None]
    values = drafts_ref[...].astype(jnp.float32) + resid[...]
    normed = rms_norm(values, gain_ref[...][None]).astype(jnp.bfloat16)
    normed = normed.reshape(normed_ref.shape)
    normed_ref[...] = normed
    sent_ref[...] = jnp.dot(
        matrix_ref[...], normed, preferred_element_type=jnp.float32
    ).astype(jnp.bfloat16)


def dispatch_rows(half, other, drafts, gain, matrix, place):
    req_dev, tree, width = drafts.shape
    whole = pl.BlockSpec(memory_space=pltpu.VMEM)
    scalar = pl.BlockSpec(memory_space=pltpu.SMEM)
    return pl.pallas_call(
        dispatch_kernel,
        out_shape=[
            jax.ShapeDtypeStruct((matrix.shape[0], width), jnp.bfloat16),
            jax.ShapeDtypeStruct((req_dev * tree, width), jnp.bfloat16),
        ],
        in_specs=[scalar] + [whole] * 5,
        out_specs=[whole] * 2,
        scratch_shapes=[pltpu.VMEM((req_dev, tree, width), jnp.float32)],
        compiler_params=pltpu.CompilerParams(vmem_limit_bytes=32 * 1024 * 1024),
        name="dispatch",
    )(place, half, other, drafts, gain.reshape(1, width), matrix)


def expert_kernel(place_ref, rows_ref, w_in_hbm, w_out_hbm, out_ref, wi, wo, in_sem, out_sem):
    halves = wi.shape[0]
    copies = []
    for half in range(halves):
        for which in range(2):
            copy = pltpu.make_async_copy(
                w_in_hbm.at[half, which], wi.at[half, which], in_sem.at[half, which]
            )
            copy.start()
            copies.append(copy)
    downs = []
    for half in range(halves):
        copy = pltpu.make_async_copy(
            w_out_hbm.at[place_ref[2] * halves + half], wo.at[half], out_sem.at[half]
        )
        copy.start()
        downs.append(copy)
    rows = rows_ref[...]
    acts = []
    for half in range(halves):
        copies[2 * half].wait()
        gate = jnp.dot(rows, wi[half, 0], preferred_element_type=jnp.float32)
        copies[2 * half + 1].wait()
        upper = jnp.dot(rows, wi[half, 1], preferred_element_type=jnp.float32)
        acts.append((jnp.maximum(gate, 0.0) * upper).astype(jnp.bfloat16))
    for half in range(halves):
        downs[half].wait()
    groups, ranks, share, quarter = out_ref.shape
    for rank in range(ranks):
        columns = slice(rank * quarter, (rank + 1) * quarter)
        made = jnp.dot(acts[0], wo[0, :, columns], preferred_element_type=jnp.float32)
        for half in range(1, halves):
            made = made + jnp.dot(
                acts[half], wo[half, :, columns], preferred_element_type=jnp.float32
            )
        out_ref[:, rank] = made.astype(jnp.bfloat16).reshape(groups, share, quarter)


def expert_rows(rows, w_in_own, w_out, place, groups, ranks):
    count, width = rows.shape
    halves, _, _, hidden = w_in_own.shape
    quarter = width // ranks
    whole = pl.BlockSpec(memory_space=pltpu.VMEM)
    scalar = pl.BlockSpec(memory_space=pltpu.SMEM)
    anywhere = pl.BlockSpec(memory_space=pl.ANY)
    return pl.pallas_call(
        expert_kernel,
        out_shape=jax.ShapeDtypeStruct((groups, ranks, count // groups, quarter), jnp.bfloat16),
        in_specs=[scalar, whole, anywhere, anywhere],
        out_specs=whole,
        scratch_shapes=[
            pltpu.VMEM((halves, 2, width, hidden), jnp.bfloat16),
            pltpu.VMEM((halves, hidden, width), jnp.bfloat16),
            pltpu.SemaphoreType.DMA((halves, 2)),
            pltpu.SemaphoreType.DMA((halves,)),
        ],
        compiler_params=pltpu.CompilerParams(vmem_limit_bytes=32 * 1024 * 1024),
        name="experts",
    )(place, rows, w_in_own, w_out)


def combine_kernel(
    order_ref, rows_ref, targets_ref, gates_ref, resid_ref, slots_ref, tree_ref, posted_ref
):
    req_dev, tree, quarter = tree_ref.shape
    keep = posted_ref.shape[1]
    tokens = req_dev * tree
    places = lax.broadcasted_iota(jnp.int32, (tokens, rows_ref.shape[0]), 1)
    matrix = jnp.zeros(places.shape, jnp.float32)
    for pick in range(targets_ref.shape[1]):
        matrix = matrix + jnp.where(
            places == targets_ref[:, pick : pick + 1], gates_ref[:, pick : pick + 1], 0.0
        )
    mixture = jnp.dot(
        matrix.astype(jnp.bfloat16), rows_ref[...], preferred_element_type=jnp.float32
    )
    done = (resid_ref[...] + mixture).astype(jnp.bfloat16)
    tree_ref[...] = done.reshape(tree_ref.shape)
    posted_ref[...] = jnp.zeros_like(posted_ref)
    for request in range(req_dev):
        wanted = lax.broadcasted_iota(jnp.int32, (keep, tree), 0)
        chosen = (slots_ref[request : request + 1, :] == wanted).astype(jnp.bfloat16)
        kept = jnp.dot(
            chosen, done[request * tree : (request + 1) * tree], preferred_element_type=jnp.float32
        )
        posted_ref[pl.ds(order_ref[request], 1)] = kept.astype(jnp.bfloat16)[None]


def combine_rows(rows, targets, gates, resid, slots, order, requests):
    tokens, quarter = resid.shape
    req_dev, tree = slots.shape
    whole = pl.BlockSpec(memory_space=pltpu.VMEM)
    scalar = pl.BlockSpec(memory_space=pltpu.SMEM)
    return pl.pallas_call(
        combine_kernel,
        out_shape=[
            jax.ShapeDtypeStruct((req_dev, tree, quarter), jnp.bfloat16),
            jax.ShapeDtypeStruct((requests, KEEP, quarter), jnp.bfloat16),
        ],
        in_specs=[scalar] + [whole] * 5,
        out_specs=[whole] * 2,
        compiler_params=pltpu.CompilerParams(vmem_limit_bytes=32 * 1024 * 1024),
        name="combine",
    )(order, rows, targets, gates, resid, slots)


def on_device(
    drafts,
    gain_attn,
    w_query,
    key_value_weight,
    w_output,
    cache,
    lengths,
    tree_mask,
    depths,
    gain_moe,
    w_router,
    expert_ids,
    w_in,
    w_out,
    slots,
    order,
):
    req_dev, draft_tree, width = drafts.shape
    head_dim = cache.shape[-1]
    kv_heads = cache.shape[2]
    local_heads = w_query.shape[1] // head_dim
    tp_count = lax.axis_size("tp")
    req_count = lax.axis_size("req")
    tp_rank = lax.axis_index("tp")
    head_group = local_heads * tp_count // kv_heads
    kv_head = tp_rank * local_heads // head_group
    tokens = req_dev * draft_tree
    experts = w_router.shape[1]
    pieces = w_in.shape[0]
    quarter = width // tp_count
    first = tp_rank % 2
    place = jnp.stack([kv_head, first, tp_rank]).astype(jnp.int32)

    ids = expert_ids.reshape(tokens, -1)
    picks = ids[:, :, None] == jnp.arange(experts)[None, None, :]
    counts = jnp.sum(picks.astype(jnp.int32), axis=1)
    slot_expert = jnp.cumsum(counts, axis=0) - counts
    slot_pick = jnp.sum(jnp.where(picks, slot_expert[:, None, :], 0), axis=-1)
    held = jnp.where(counts == 1, slot_expert, -1).T
    by_expert = pieces == 2 * tp_count
    if by_expert:
        share = CAP
        held = lax.dynamic_index_in_dim(
            held.reshape(req_count, tp_count, tokens), tp_rank, 1, keepdims=False
        )
        slot_ids = jnp.arange(share)
        targets = ids * CAP + slot_pick
    else:
        share = CAP // tp_count
        held = jnp.repeat(held, 2, axis=0)
        slot_ids = tp_rank * share + jnp.arange(share)
        piece = 2 * ids[:, :, None] + jnp.arange(2)
        lane = (piece // pieces) * tp_count + (slot_pick // share)[:, :, None]
        targets = (lane * pieces + piece % pieces) * share + (slot_pick % share)[:, :, None]
        targets = targets.reshape(tokens, -1)
    matrix = (held[:, None, :] == slot_ids[None, :, None]).astype(jnp.bfloat16)
    matrix = matrix.reshape(-1, tokens)

    mine, theirs = attention_part(
        drafts,
        gain_attn,
        w_query,
        key_value_weight,
        w_output,
        cache,
        lengths,
        tree_mask,
        depths,
        place,
    )
    near = [(i, i ^ 1) for i in range(tp_count)]
    far = [(i, i ^ 2) for i in range(tp_count)]

    def added(left, right):
        return (left.astype(jnp.float32) + right.astype(jnp.float32)).astype(jnp.bfloat16)

    chip = added(mine, lax.ppermute(theirs, "tp", near))
    half = added(chip, lax.ppermute(chip, "tp", far))
    other = lax.ppermute(half, "tp", near)

    sent, normed2 = dispatch_rows(half, other, drafts, gain_moe, matrix, place)
    arrived = lax.all_to_all(
        sent.reshape(req_count, -1, width), "req", split_axis=0, concat_axis=0, tiled=True
    )

    logits = jnp.dot(normed2, w_router, preferred_element_type=jnp.float32)
    chosen = jax.nn.sigmoid(jnp.sum(jnp.where(picks, logits[:, None, :], 0.0), axis=-1))
    gates = (chosen / jnp.sum(chosen, axis=1, keepdims=True)).astype(jnp.bfloat16)
    gates = gates.astype(jnp.float32)
    start = tp_rank * quarter
    own_attn = jnp.where(
        first == 0,
        jnp.concatenate([half, other], axis=0),
        jnp.concatenate([other, half], axis=0),
    )
    own_resid = lax.dynamic_slice_in_dim(
        drafts.reshape(tokens, width), start, quarter, 1
    ).astype(jnp.float32) + lax.dynamic_slice_in_dim(own_attn, start, quarter, 1).astype(
        jnp.float32
    )

    if by_expert:
        own_in = lax.dynamic_slice_in_dim(w_in, tp_rank * 2, 2, 0).transpose(0, 2, 1, 3)
        produced = expert_rows(
            arrived.reshape(-1, width), own_in, w_out, place, req_count, tp_count
        )
    else:
        gates = jnp.repeat(gates, 2, axis=1)
        rows_in = arrived.reshape(req_count, pieces, share, width)
        rows_in = rows_in.transpose(1, 0, 2, 3).reshape(pieces, req_count * share, width)
        gate_up = jnp.einsum("prd,pdgf->prgf", rows_in, w_in, preferred_element_type=jnp.float32)
        act = (jax.nn.relu(gate_up[:, :, 0]) * gate_up[:, :, 1]).astype(jnp.bfloat16)
        produced = jnp.einsum(
            "prf,pfd->prd", act, w_out, preferred_element_type=jnp.float32
        ).astype(jnp.bfloat16)
        produced = produced.reshape(pieces, req_count, share, tp_count, quarter)
        produced = produced.transpose(1, 3, 0, 2, 4)
    returned = lax.all_to_all(
        produced.reshape(req_count * tp_count, -1, quarter),
        ("req", "tp"),
        split_axis=0,
        concat_axis=0,
        tiled=True,
    )
    tree_out, posted = combine_rows(
        returned.reshape(-1, quarter),
        targets,
        gates,
        own_resid,
        slots,
        order,
        req_count * req_dev,
    )
    received = lax.all_to_all(
        posted.reshape(req_count, req_dev, KEEP, quarter),
        "req",
        split_axis=0,
        concat_axis=0,
        tiled=True,
    )
    accepted = jnp.sum(received.astype(jnp.float32), axis=0).astype(jnp.bfloat16)
    return (tree_out, accepted)


def solution(mesh):
    placed = (
        P("req", None, None),
        P(),
        P(None, "tp"),
        P(),
        P("tp", None),
        P("req", None, None, None, None),
        P("req"),
        P("req", None, None),
        P("req", None),
        P(),
        P(),
        P("req", None, None),
        P("req", None, None, None),
        P("req", None, None),
        P("req", None),
        P("req"),
    )
    return jax.shard_map(
        on_device,
        mesh=mesh,
        in_specs=placed,
        out_specs=(P("req", None, "tp"), P("req", None, "tp")),
        check_vma=False,
    )
```

```python
import functools

import jax
import jax.numpy as jnp
from jax import lax
from jax.experimental import pallas as pl
from jax.experimental.pallas import tpu as pltpu
from jax.sharding import PartitionSpec as P

KEEP = 16
CAP = 32


EPSILON = 1e-06
THETA = 1000000.0
LOG2E = 1.4426950408889634
BLOCK = 512
WHOLE_VMEM = 60 * 1024 * 1024
SOME_VMEM = 32 * 1024 * 1024


def rms_norm(values, gain_vec):
    return (
        values * lax.rsqrt(jnp.mean(values * values, axis=-1, keepdims=True) + EPSILON) * gain_vec
    )


def column_of(row):
    count = row.shape[1]
    at_row = lax.broadcasted_iota(jnp.int32, (count, count), 0)
    at_col = lax.broadcasted_iota(jnp.int32, (count, count), 1)
    return jnp.sum(jnp.where(at_row == at_col, row, 0.0), axis=1, keepdims=True)


def attention_kernel(
    lengths_ref,
    place_ref,
    gain_ref,
    freqs_ref,
    depths_ref,
    mask_ref,
    drafts_hbm,
    wq_hbm,
    wkv_hbm,
    wo_hbm,
    cache_hbm,
    mine_ref,
    theirs_ref,
    drafts,
    wq,
    wk,
    wv,
    wo,
    keys,
    vals,
    scores,
    weight_sem,
    cache_sem,
):
    req_dev, tree, width = drafts.shape
    head_dim = cache_hbm.shape[-1]
    kv_heads = cache_hbm.shape[2]
    local_heads = wq.shape[1] // head_dim
    block = scores.shape[2]
    kv_head = place_ref[0]
    first = place_ref[1]

    def column_copy(target, which, sem):
        start = pl.multiple_of((which * kv_heads + kv_head) * head_dim, head_dim)
        return pltpu.make_async_copy(wkv_hbm.at[:, pl.ds(start, head_dim)], target, sem)

    def cache_copy(request, which, index):
        rows = pl.ds(pl.multiple_of(index * block, block), block)
        target = vals if which else keys
        return pltpu.make_async_copy(
            cache_hbm.at[request, which, kv_head, rows],
            target.at[request, rows],
            cache_sem.at[request, which, index],
        )

    copy_d = pltpu.make_async_copy(drafts_hbm, drafts, weight_sem.at[4])
    copy_d.start()
    copy_q = pltpu.make_async_copy(wq_hbm, wq, weight_sem.at[0])
    copy_k = column_copy(wk, 0, weight_sem.at[1])
    copy_v = column_copy(wv, 1, weight_sem.at[2])
    copy_o = pltpu.make_async_copy(wo_hbm, wo, weight_sem.at[3])
    copy_q.start()
    copy_k.start()
    copy_v.start()
    limits = [lengths_ref[request] for request in range(req_dev)]
    counts = [(limit + block - 1) // block for limit in limits]
    for request in range(req_dev):
        for which in range(2):

            @pl.loop(0, counts[request])
            def _(index, request=request, which=which):
                cache_copy(request, which, index).start()

    copy_o.start()

    copy_d.wait()
    inputs = drafts[...].astype(jnp.float32).reshape(req_dev * tree, width)
    normed = rms_norm(inputs, gain_ref[...][None, :]).astype(jnp.bfloat16)
    at = [
        column_of(depths_ref[request : request + 1, :].astype(jnp.float32))
        + limits[request].astype(jnp.float32)
        for request in range(req_dev)
    ]
    angles = jnp.concatenate(at, axis=0) * freqs_ref[...]
    cosine = jnp.cos(angles)
    lane = lax.broadcasted_iota(jnp.int32, angles.shape, 1)
    sine = jnp.sin(angles) * jnp.where(lane < head_dim // 2, -1.0, 1.0)

    def turned(vectors):
        return (vectors * cosine + pltpu.roll(vectors, head_dim // 2, 1) * sine).astype(jnp.bfloat16)

    copy_q.wait()
    query_all = jnp.dot(normed, wq[...], preferred_element_type=jnp.float32)
    queries = [
        turned(query_all[:, head * head_dim : (head + 1) * head_dim]) for head in range(local_heads)
    ]
    copy_k.wait()
    key_new = turned(jnp.dot(normed, wk[...], preferred_element_type=jnp.float32))
    copy_v.wait()
    val_new = jnp.dot(normed, wv[...], preferred_element_type=jnp.float32).astype(jnp.bfloat16)
    slope = LOG2E * head_dim ** (-0.5)
    rows = local_heads * tree
    contract = (((1,), (1,)), ((), ()))

    def lanes_down(values, step):
        parts = [values[:, i : i + 128] for i in range(0, values.shape[1], 128)]
        return functools.reduce(step, parts)

    mixed = []
    for request in range(req_dev):
        span = slice(request * tree, (request + 1) * tree)
        own = jnp.concatenate([q[span] for q in queries], axis=0)
        allowed = jnp.concatenate([mask_ref[request]] * local_heads, axis=0) > 0
        tree_scores = lax.dot_general(
            own, key_new[span], contract, preferred_element_type=jnp.float32
        )
        tree_scores = jnp.where(allowed, tree_scores, -jnp.inf)
        limit = limits[request]

        def score_step(index, best, request=request, own=own, limit=limit):
            cache_copy(request, 0, index).wait()
            offset = pl.multiple_of(index * block, block)
            found = lax.dot_general(
                own,
                keys[request, pl.ds(offset, block)],
                contract,
                preferred_element_type=jnp.float32,
            )
            inside = offset + lax.broadcasted_iota(jnp.int32, found.shape, 1) < limit
            found = jnp.where(inside, found, -jnp.inf)
            scores[index] = found
            return jnp.maximum(best, lanes_down(found, jnp.maximum))

        best = lax.fori_loop(
            0, counts[request], score_step, jnp.full((rows, 128), -jnp.inf, jnp.float32)
        )
        peak = jnp.maximum(
            jnp.max(best, axis=1, keepdims=True), jnp.max(tree_scores, axis=1, keepdims=True)
        )
        tree_weights = jnp.exp2((tree_scores - peak) * slope)
        start = (
            jnp.zeros((rows, 128), jnp.float32),
            jnp.dot(
                tree_weights.astype(jnp.bfloat16), val_new[span], preferred_element_type=jnp.float32
            ),
        )

        def sum_step(index, carry, request=request, peak=peak):
            total, accum = carry
            cache_copy(request, 1, index).wait()
            offset = pl.multiple_of(index * block, block)
            weights = jnp.exp2((scores[index] - peak) * slope)
            accum = accum + jnp.dot(
                weights.astype(jnp.bfloat16),
                vals[request, pl.ds(offset, block)],
                preferred_element_type=jnp.float32,
            )
            return total + lanes_down(weights, jnp.add), accum

        total, accum = lax.fori_loop(0, counts[request], sum_step, start)
        total = jnp.sum(total, axis=1, keepdims=True) + jnp.sum(tree_weights, axis=1, keepdims=True)
        mixed.append((accum / total).astype(jnp.bfloat16))

    copy_o.wait()
    for request in range(req_dev):
        heads = jnp.concatenate(
            [mixed[request][head * tree : (head + 1) * tree] for head in range(local_heads)], axis=1
        )
        part = jnp.dot(heads, wo[...], preferred_element_type=jnp.float32).astype(jnp.bfloat16)

        @pl.when(first == request)
        def _(part=part):
            mine_ref[...] = part

        @pl.when(first != request)
        def _(part=part):
            theirs_ref[...] = part


def attention_part(
    drafts, gain, w_query, key_value_weight, w_output, cache, lengths, tree_mask, depths, place
):
    req_dev, tree, width = drafts.shape
    head_dim = cache.shape[-1]
    longest = cache.shape[3]
    block = min(BLOCK, longest)
    local = w_query.shape[1]
    half_dim = head_dim // 2
    freqs = jnp.exp(-jnp.log(THETA) * jnp.arange(half_dim, dtype=jnp.float32) / half_dim)
    freqs = jnp.tile(freqs, 2).reshape(1, head_dim)
    whole = pl.BlockSpec(memory_space=pltpu.VMEM)
    scalar = pl.BlockSpec(memory_space=pltpu.SMEM)
    anywhere = pl.BlockSpec(memory_space=pl.ANY)
    bf16 = jnp.bfloat16
    return pl.pallas_call(
        attention_kernel,
        out_shape=[jax.ShapeDtypeStruct((tree, width), bf16)] * 2,
        in_specs=[scalar] * 2 + [whole] * 4 + [anywhere] * 5,
        out_specs=[whole] * 2,
        scratch_shapes=[
            pltpu.VMEM((req_dev, tree, width), bf16),
            pltpu.VMEM((width, local), bf16),
            pltpu.VMEM((width, head_dim), bf16),
            pltpu.VMEM((width, head_dim), bf16),
            pltpu.VMEM((local, width), bf16),
            pltpu.VMEM((req_dev, longest, head_dim), bf16),
            pltpu.VMEM((req_dev, longest, head_dim), bf16),
            pltpu.VMEM((longest // block, local // head_dim * tree, block), jnp.float32),
            pltpu.SemaphoreType.DMA((5,)),
            pltpu.SemaphoreType.DMA((req_dev, 2, longest // block)),
        ],
        compiler_params=pltpu.CompilerParams(vmem_limit_bytes=WHOLE_VMEM),
        name="attention",
    )(
        lengths,
        place,
        gain,
        freqs,
        depths,
        tree_mask,
        drafts,
        w_query,
        key_value_weight,
        w_output,
        cache,
    )


def dispatch_kernel(
    place_ref,
    half_ref,
    other_ref,
    drafts_ref,
    gain_ref,
    held_ref,
    router_ref,
    logits_ref,
    *rest,
):
    sent_refs, resid = rest[:-1], rest[-1]
    first = place_ref[1]
    resid[pl.ds(first, 1)] = half_ref[...].astype(jnp.float32)[None]
    resid[pl.ds(1 - first, 1)] = other_ref[...].astype(jnp.float32)[None]
    values = drafts_ref[...].astype(jnp.float32) + resid[...]
    normed = rms_norm(values, gain_ref[...][None, None, :]).astype(jnp.bfloat16)
    normed = normed.reshape(-1, normed.shape[-1])
    for step, sent_ref in enumerate(sent_refs):
        slots = lax.broadcasted_iota(
            jnp.int32, (sent_ref.shape[0], held_ref.shape[1]), 0
        )
        row = held_ref[pl.ds(place_ref[3] ^ step, 1), :]
        matrix = (row == slots).astype(jnp.bfloat16)
        sent_ref[...] = jnp.dot(matrix, normed, preferred_element_type=jnp.float32).astype(
            jnp.bfloat16
        )
    logits_ref[...] = lax.dot_general(
        normed, router_ref[...], (((1,), (1,)), ((), ())), preferred_element_type=jnp.float32
    )


def dispatch_rows(half, other, drafts, gain, held, router, place):
    req_dev, tree, width = drafts.shape
    tokens = req_dev * tree
    whole = pl.BlockSpec(memory_space=pltpu.VMEM)
    scalar = pl.BlockSpec(memory_space=pltpu.SMEM)
    logits, *sent = pl.pallas_call(
        dispatch_kernel,
        out_shape=[jax.ShapeDtypeStruct((tokens, router.shape[0]), jnp.float32)]
        + [jax.ShapeDtypeStruct((CAP, width), jnp.bfloat16)] * held.shape[0],
        in_specs=[scalar] + [whole] * 6,
        out_specs=[whole] * (1 + held.shape[0]),
        scratch_shapes=[pltpu.VMEM((req_dev, tree, width), jnp.float32)],
        compiler_params=pltpu.CompilerParams(vmem_limit_bytes=SOME_VMEM),
        name="dispatch",
    )(place, half, other, drafts, gain, held, router)
    return logits, sent


def expert_kernel(place_ref, w_in_hbm, w_out_hbm, *rest):
    *row_refs, out_ref, rows, wi, wo, in_sem, out_sem = rest
    halves = wi.shape[0]
    in_copies = []
    for half in range(halves):
        for which in range(2):
            copy = pltpu.make_async_copy(
                w_in_hbm.at[half, which], wi.at[half, which], in_sem.at[half, which]
            )
            copy.start()
            in_copies.append(copy)
    out_copies = []
    for half in range(halves):
        copy = pltpu.make_async_copy(
            w_out_hbm.at[place_ref[2] * halves + half], wo.at[half], out_sem.at[half]
        )
        copy.start()
        out_copies.append(copy)
    share = row_refs[0].shape[0]
    for step, row_ref in enumerate(row_refs):
        start = pl.multiple_of((place_ref[3] ^ step) * share, share)
        rows[pl.ds(start, share)] = row_ref[...]
    taken = rows[...]
    acts = []
    for half in range(halves):
        in_copies[2 * half].wait()
        gate = jnp.dot(taken, wi[half, 0], preferred_element_type=jnp.float32)
        in_copies[2 * half + 1].wait()
        upper = jnp.dot(taken, wi[half, 1], preferred_element_type=jnp.float32)
        acts.append((jnp.maximum(gate, 0.0) * upper).astype(jnp.bfloat16))
    for copy in out_copies:
        copy.wait()
    groups, ranks, _, quarter = out_ref.shape
    for rank in range(ranks):
        columns = slice(rank * quarter, (rank + 1) * quarter)
        made = jnp.dot(acts[0], wo[0, :, columns], preferred_element_type=jnp.float32)
        for half in range(1, halves):
            made = made + jnp.dot(
                acts[half], wo[half, :, columns], preferred_element_type=jnp.float32
            )
        out_ref[:, rank] = made.astype(jnp.bfloat16).reshape(groups, share, quarter)


def expert_rows(rows, w_in_own, w_out, place, ranks):
    share, width = rows[0].shape
    groups = len(rows)
    halves, _, _, hidden = w_in_own.shape
    quarter = width // ranks
    whole = pl.BlockSpec(memory_space=pltpu.VMEM)
    scalar = pl.BlockSpec(memory_space=pltpu.SMEM)
    anywhere = pl.BlockSpec(memory_space=pl.ANY)
    return pl.pallas_call(
        expert_kernel,
        out_shape=jax.ShapeDtypeStruct((groups, ranks, share, quarter), jnp.bfloat16),
        in_specs=[scalar] + [anywhere] * 2 + [whole] * groups,
        out_specs=whole,
        scratch_shapes=[
            pltpu.VMEM((groups * share, width), jnp.bfloat16),
            pltpu.VMEM((halves, 2, width, hidden), jnp.bfloat16),
            pltpu.VMEM((halves, hidden, width), jnp.bfloat16),
            pltpu.SemaphoreType.DMA((halves, 2)),
            pltpu.SemaphoreType.DMA((halves,)),
        ],
        compiler_params=pltpu.CompilerParams(vmem_limit_bytes=WHOLE_VMEM),
        name="experts",
    )(place, w_in_own, w_out, *rows)


def combine_kernel(
    order_ref, rows_ref, targets_ref, gates_ref, resid_ref, slots_ref, tree_ref, posted_ref
):
    req_dev, tree, quarter = tree_ref.shape
    keep = posted_ref.shape[1]
    tokens = req_dev * tree
    places = lax.broadcasted_iota(jnp.int32, (tokens, rows_ref.shape[0]), 1)
    matrix = jnp.zeros(places.shape, jnp.float32)
    for pick in range(targets_ref.shape[1]):
        matrix = matrix + jnp.where(
            places == targets_ref[:, pick : pick + 1], gates_ref[:, pick : pick + 1], 0.0
        )
    mixture = jnp.dot(
        matrix.astype(jnp.bfloat16), rows_ref[...], preferred_element_type=jnp.float32
    )
    done = (resid_ref[...] + mixture).astype(jnp.bfloat16)
    tree_ref[...] = done.reshape(tree_ref.shape)
    posted_ref[...] = jnp.zeros_like(posted_ref)
    for request in range(req_dev):
        wanted = lax.broadcasted_iota(jnp.int32, (keep, tree), 0)
        chosen = (slots_ref[request : request + 1, :] == wanted).astype(jnp.bfloat16)
        kept = jnp.dot(
            chosen, done[request * tree : (request + 1) * tree], preferred_element_type=jnp.float32
        )
        posted_ref[pl.ds(order_ref[request], 1)] = kept.astype(jnp.bfloat16)[None]


def combine_rows(rows, targets, gates, resid, slots, order, requests):
    tokens, quarter = resid.shape
    req_dev, tree = slots.shape
    whole = pl.BlockSpec(memory_space=pltpu.VMEM)
    scalar = pl.BlockSpec(memory_space=pltpu.SMEM)
    return pl.pallas_call(
        combine_kernel,
        out_shape=[
            jax.ShapeDtypeStruct((req_dev, tree, quarter), jnp.bfloat16),
            jax.ShapeDtypeStruct((requests, KEEP, quarter), jnp.bfloat16),
        ],
        in_specs=[scalar] + [whole] * 5,
        out_specs=[whole] * 2,
        compiler_params=pltpu.CompilerParams(vmem_limit_bytes=SOME_VMEM),
        name="combine",
    )(order, rows, targets, gates, resid, slots)


def on_device(
    drafts,
    gain_attn,
    w_query,
    key_value_weight,
    w_output,
    cache,
    lengths,
    tree_mask,
    depths,
    gain_moe,
    w_router,
    expert_ids,
    w_in,
    w_out,
    slots,
    order,
):
    req_dev, draft_tree, width = drafts.shape
    head_dim = cache.shape[-1]
    kv_heads = cache.shape[2]
    local_heads = w_query.shape[1] // head_dim
    tp_count = lax.axis_size("tp")
    req_count = lax.axis_size("req")
    tp_rank = lax.axis_index("tp")
    head_group = local_heads * tp_count // kv_heads
    kv_head = tp_rank * local_heads // head_group
    tokens = req_dev * draft_tree
    experts = w_router.shape[1]
    pieces = w_in.shape[0]
    quarter = width // tp_count
    first = tp_rank % 2
    place = jnp.stack([kv_head, first, tp_rank, lax.axis_index("req")]).astype(jnp.int32)

    ids = expert_ids.reshape(tokens, -1)
    picks = ids[:, :, None] == jnp.arange(experts)[None, None, :]
    counts = jnp.sum(picks.astype(jnp.int32), axis=1)
    slot_expert = jnp.cumsum(counts, axis=0) - counts
    slot_pick = jnp.sum(jnp.where(picks, slot_expert[:, None, :], 0), axis=-1)
    held = jnp.where(counts == 1, slot_expert, -1).T
    by_expert = pieces == 2 * tp_count
    if by_expert:
        share = CAP
        held = lax.dynamic_index_in_dim(
            held.reshape(req_count, tp_count, tokens), tp_rank, 1, keepdims=False
        )
        targets = ids * CAP + slot_pick
    else:
        share = CAP // tp_count
        held = jnp.repeat(held, 2, axis=0)
        slot_ids = tp_rank * share + jnp.arange(share)
        piece = 2 * ids[:, :, None] + jnp.arange(2)
        lane = (piece // pieces) * tp_count + (slot_pick // share)[:, :, None]
        targets = (lane * pieces + piece % pieces) * share + (slot_pick % share)[:, :, None]
        targets = targets.reshape(tokens, -1)
        matrix = (held[:, None, :] == slot_ids[None, :, None]).astype(jnp.bfloat16)
        matrix = matrix.reshape(-1, tokens)

    mine, theirs = attention_part(
        drafts,
        gain_attn,
        w_query,
        key_value_weight,
        w_output,
        cache,
        lengths,
        tree_mask,
        depths,
        place,
    )
    near = [(i, i ^ 1) for i in range(tp_count)]
    far = [(i, i ^ 2) for i in range(tp_count)]

    def added(left, right):
        return (left.astype(jnp.float32) + right.astype(jnp.float32)).astype(jnp.bfloat16)

    chip = added(mine, lax.ppermute(theirs, "tp", near))
    half = added(chip, lax.ppermute(chip, "tp", far))
    other = lax.ppermute(half, "tp", near)

    if by_expert:
        logits, sent = dispatch_rows(
            half, other, drafts, gain_moe, held, w_router.T, place
        )
        arrived = [sent[0]] + [
            lax.ppermute(sent[step], "req", [(i, i ^ step) for i in range(req_count)])
            for step in range(1, req_count)
        ]
    else:
        resid = jnp.where(first == 0, jnp.stack([half, other]), jnp.stack([other, half]))
        resid = (drafts.astype(jnp.float32) + resid.astype(jnp.float32)).reshape(tokens, width)
        normed2 = rms_norm(resid, gain_moe).astype(jnp.bfloat16)
        logits = jnp.dot(normed2, w_router, preferred_element_type=jnp.float32)
        sent = jnp.dot(matrix, normed2, preferred_element_type=jnp.float32).astype(jnp.bfloat16)
        arrived = lax.all_to_all(
            sent.reshape(req_count, -1, width), "req", split_axis=0, concat_axis=0, tiled=True
        )

    chosen = jax.nn.sigmoid(jnp.sum(jnp.where(picks, logits[:, None, :], 0.0), axis=-1))
    gates = (chosen / jnp.sum(chosen, axis=1, keepdims=True)).astype(jnp.bfloat16)
    gates = gates.astype(jnp.float32)
    start = tp_rank * quarter
    own_attn = jnp.where(
        first == 0,
        jnp.concatenate([half, other], axis=0),
        jnp.concatenate([other, half], axis=0),
    )
    own_resid = lax.dynamic_slice_in_dim(
        drafts.reshape(tokens, width), start, quarter, 1
    ).astype(jnp.float32) + lax.dynamic_slice_in_dim(own_attn, start, quarter, 1).astype(
        jnp.float32
    )

    if by_expert:
        own_in = lax.dynamic_slice_in_dim(w_in, tp_rank * 2, 2, 0).transpose(0, 2, 1, 3)
        produced = expert_rows(arrived, own_in, w_out, place, tp_count)
    else:
        gates = jnp.repeat(gates, 2, axis=1)
        rows_in = arrived.reshape(req_count, pieces, share, width)
        rows_in = rows_in.transpose(1, 0, 2, 3).reshape(pieces, req_count * share, width)
        gate_up = jnp.einsum("prd,pdgf->prgf", rows_in, w_in, preferred_element_type=jnp.float32)
        act = (jax.nn.relu(gate_up[:, :, 0]) * gate_up[:, :, 1]).astype(jnp.bfloat16)
        produced = jnp.einsum(
            "prf,pfd->prd", act, w_out, preferred_element_type=jnp.float32
        ).astype(jnp.bfloat16)
        produced = produced.reshape(pieces, req_count, share, tp_count, quarter)
        produced = produced.transpose(1, 3, 0, 2, 4)
    returned = lax.all_to_all(
        produced.reshape(req_count * tp_count, -1, quarter),
        ("req", "tp"),
        split_axis=0,
        concat_axis=0,
        tiled=True,
    )
    tree_out, posted = combine_rows(
        returned.reshape(-1, quarter),
        targets,
        gates,
        own_resid,
        slots,
        order,
        req_count * req_dev,
    )
    received = lax.all_to_all(
        posted.reshape(req_count, req_dev, KEEP, quarter),
        "req",
        split_axis=0,
        concat_axis=0,
        tiled=True,
    )
    accepted = jnp.sum(received.astype(jnp.float32), axis=0).astype(jnp.bfloat16)
    return (tree_out, accepted)


def solution(mesh):
    placed = (
        P("req", None, None),
        P(),
        P(None, "tp"),
        P(),
        P("tp", None),
        P("req", None, None, None, None),
        P("req"),
        P("req", None, None),
        P("req", None),
        P(),
        P(),
        P("req", None, None),
        P("req", None, None, None),
        P("req", None, None),
        P("req", None),
        P("req"),
    )
    return jax.shard_map(
        on_device,
        mesh=mesh,
        in_specs=placed,
        out_specs=(P("req", None, "tp"), P("req", None, "tp")),
        check_vma=False,
    )
```

```python
import functools

import jax
import jax.numpy as jnp
from jax import lax
from jax.experimental import pallas as pl
from jax.experimental.pallas import tpu as pltpu
from jax.sharding import PartitionSpec as P

KEEP = 16
CAP = 32


EPSILON = 1e-06
THETA = 1000000.0
LOG2E = 1.4426950408889634
BLOCK = 1536
WHOLE_VMEM = 60 * 1024 * 1024
SOME_VMEM = 20 * 1024 * 1024


def rms_norm(values, gain_vec):
    return (
        values * lax.rsqrt(jnp.mean(values * values, axis=-1, keepdims=True) + EPSILON) * gain_vec
    )


def column_of(row):
    count = row.shape[1]
    at_row = lax.broadcasted_iota(jnp.int32, (count, count), 0)
    at_col = lax.broadcasted_iota(jnp.int32, (count, count), 1)
    return jnp.sum(jnp.where(at_row == at_col, row, 0.0), axis=1, keepdims=True)


def attention_kernel(
    tp_count,
    lengths_ref,
    gain_hbm,
    depths_hbm,
    mask_hbm,
    drafts_hbm,
    wq_hbm,
    wkv_hbm,
    wo_hbm,
    cache_hbm,
    mine_ref,
    theirs_ref,
    gain_ref,
    depths_ref,
    mask_ref,
    drafts,
    wq,
    wk,
    wv,
    wo,
    keys,
    vals,
    scores,
    weight_sem,
    cache_sem,
):
    req_dev, tree, width = drafts.shape
    head_dim = cache_hbm.shape[-1]
    kv_heads = cache_hbm.shape[2]
    local_heads = wq.shape[1] // head_dim
    block = scores.shape[2]
    tp_rank = lax.axis_index("tp")
    kv_head = tp_rank * local_heads // (local_heads * tp_count // kv_heads)
    first = lax.rem(tp_rank, 2)

    def column_copy(target, which, sem):
        start = pl.multiple_of((which * kv_heads + kv_head) * head_dim, head_dim)
        return pltpu.make_async_copy(wkv_hbm.at[:, pl.ds(start, head_dim)], target, sem)

    def cache_copy(request, which, index):
        rows = pl.ds(pl.multiple_of(index * block, block), block)
        target = vals if which else keys
        return pltpu.make_async_copy(
            cache_hbm.at[request, which, kv_head, rows],
            target.at[request, rows],
            cache_sem.at[request, which, index],
        )

    copy_d = pltpu.make_async_copy(drafts_hbm, drafts, weight_sem.at[4])
    copy_d.start()
    small = [
        pltpu.make_async_copy(gain_hbm, gain_ref, weight_sem.at[5]),
        pltpu.make_async_copy(depths_hbm, depths_ref, weight_sem.at[6]),
        pltpu.make_async_copy(mask_hbm, mask_ref, weight_sem.at[7]),
    ]
    for copy in small:
        copy.start()
    copy_q = pltpu.make_async_copy(wq_hbm, wq, weight_sem.at[0])
    copy_k = column_copy(wk, 0, weight_sem.at[1])
    copy_v = column_copy(wv, 1, weight_sem.at[2])
    copy_o = pltpu.make_async_copy(wo_hbm, wo, weight_sem.at[3])
    copy_q.start()
    copy_k.start()
    copy_v.start()
    limits = [lengths_ref[request] for request in range(req_dev)]
    counts = [(limit + block - 1) // block for limit in limits]
    for request in range(req_dev):
        for which in range(2):

            @pl.loop(0, counts[request])
            def _(index, request=request, which=which):
                cache_copy(request, which, index).start()

    copy_o.start()

    copy_d.wait()
    small[0].wait()
    inputs = drafts[...].astype(jnp.float32).reshape(req_dev * tree, width)
    normed = rms_norm(inputs, gain_ref[...][None, :]).astype(jnp.bfloat16)
    small[1].wait()
    small[2].wait()
    at = [
        column_of(depths_ref[request : request + 1, :].astype(jnp.float32))
        + limits[request].astype(jnp.float32)
        for request in range(req_dev)
    ]
    lane = lax.broadcasted_iota(jnp.int32, (req_dev * tree, head_dim), 1)
    half_dim = head_dim // 2
    freqs = jnp.exp(
        -jnp.log(THETA) * lax.rem(lane, half_dim).astype(jnp.float32) / half_dim
    )
    angles = jnp.concatenate(at, axis=0) * freqs
    cosine = jnp.cos(angles)
    sine = jnp.sin(angles) * jnp.where(lane < head_dim // 2, -1.0, 1.0)

    def turned(vectors):
        return (vectors * cosine + pltpu.roll(vectors, head_dim // 2, 1) * sine).astype(jnp.bfloat16)

    copy_q.wait()
    query_all = jnp.dot(normed, wq[...], preferred_element_type=jnp.float32)
    queries = [
        turned(query_all[:, head * head_dim : (head + 1) * head_dim]) for head in range(local_heads)
    ]
    copy_k.wait()
    key_new = turned(jnp.dot(normed, wk[...], preferred_element_type=jnp.float32))
    copy_v.wait()
    val_new = jnp.dot(normed, wv[...], preferred_element_type=jnp.float32).astype(jnp.bfloat16)
    slope = LOG2E * head_dim ** (-0.5)
    rows = local_heads * tree
    contract = (((1,), (1,)), ((), ()))

    def lanes_down(values, step):
        parts = [values[:, i : i + 128] for i in range(0, values.shape[1], 128)]
        return functools.reduce(step, parts)

    mixed = []
    for request in range(req_dev):
        span = slice(request * tree, (request + 1) * tree)
        own = jnp.concatenate([q[span] for q in queries], axis=0)
        allowed = jnp.concatenate([mask_ref[request]] * local_heads, axis=0) > 0
        tree_scores = lax.dot_general(
            own, key_new[span], contract, preferred_element_type=jnp.float32
        )
        tree_scores = jnp.where(allowed, tree_scores, -jnp.inf)
        limit = limits[request]

        def score_step(index, best, request=request, own=own, limit=limit):
            cache_copy(request, 0, index).wait()
            offset = pl.multiple_of(index * block, block)
            found = lax.dot_general(
                own,
                keys[request, pl.ds(offset, block)],
                contract,
                preferred_element_type=jnp.float32,
            )
            inside = offset + lax.broadcasted_iota(jnp.int32, found.shape, 1) < limit
            found = jnp.where(inside, found, -jnp.inf)
            scores[index] = found
            return jnp.maximum(best, lanes_down(found, jnp.maximum))

        best = lax.fori_loop(
            0, counts[request], score_step, jnp.full((rows, 128), -jnp.inf, jnp.float32)
        )
        peak = jnp.maximum(
            jnp.max(best, axis=1, keepdims=True), jnp.max(tree_scores, axis=1, keepdims=True)
        )
        tree_weights = jnp.exp2((tree_scores - peak) * slope)
        start = (
            jnp.zeros((rows, 128), jnp.float32),
            jnp.dot(
                tree_weights.astype(jnp.bfloat16), val_new[span], preferred_element_type=jnp.float32
            ),
        )

        def sum_step(index, carry, request=request, peak=peak):
            total, accum = carry
            cache_copy(request, 1, index).wait()
            offset = pl.multiple_of(index * block, block)
            weights = jnp.exp2((scores[index] - peak) * slope)
            accum = accum + jnp.dot(
                weights.astype(jnp.bfloat16),
                vals[request, pl.ds(offset, block)],
                preferred_element_type=jnp.float32,
            )
            return total + lanes_down(weights, jnp.add), accum

        total, accum = lax.fori_loop(0, counts[request], sum_step, start)
        total = jnp.sum(total, axis=1, keepdims=True) + jnp.sum(tree_weights, axis=1, keepdims=True)
        mixed.append((accum / total).astype(jnp.bfloat16))

    copy_o.wait()
    for request in range(req_dev):
        heads = jnp.concatenate(
            [mixed[request][head * tree : (head + 1) * tree] for head in range(local_heads)], axis=1
        )
        part = jnp.dot(heads, wo[...], preferred_element_type=jnp.float32).astype(jnp.bfloat16)

        @pl.when(first == request)
        def _(part=part):
            mine_ref[...] = part

        @pl.when(first != request)
        def _(part=part):
            theirs_ref[...] = part


def attention_part(
    drafts, gain, w_query, key_value_weight, w_output, cache, lengths, tree_mask, depths, tp_count
):
    req_dev, tree, width = drafts.shape
    head_dim = cache.shape[-1]
    longest = cache.shape[3]
    block = min(BLOCK, longest)
    local = w_query.shape[1]
    whole = pl.BlockSpec(memory_space=pltpu.VMEM)
    scalar = pl.BlockSpec(memory_space=pltpu.SMEM)
    anywhere = pl.BlockSpec(memory_space=pl.ANY)
    bf16 = jnp.bfloat16
    return pl.pallas_call(
        functools.partial(attention_kernel, tp_count),
        out_shape=[jax.ShapeDtypeStruct((tree, width), bf16)] * 2,
        in_specs=[scalar] + [anywhere] * 8,
        out_specs=[whole] * 2,
        scratch_shapes=[
            pltpu.VMEM((width,), jnp.float32),
            pltpu.VMEM((req_dev, tree), jnp.int32),
            pltpu.VMEM((req_dev, tree, tree), jnp.int32),
            pltpu.VMEM((req_dev, tree, width), bf16),
            pltpu.VMEM((width, local), bf16),
            pltpu.VMEM((width, head_dim), bf16),
            pltpu.VMEM((width, head_dim), bf16),
            pltpu.VMEM((local, width), bf16),
            pltpu.VMEM((req_dev, longest, head_dim), bf16),
            pltpu.VMEM((req_dev, longest, head_dim), bf16),
            pltpu.VMEM((longest // block, local // head_dim * tree, block), jnp.float32),
            pltpu.SemaphoreType.DMA((8,)),
            pltpu.SemaphoreType.DMA((req_dev, 2, longest // block)),
        ],
        compiler_params=pltpu.CompilerParams(vmem_limit_bytes=WHOLE_VMEM),
        name="attention",
    )(
        lengths,
        gain,
        depths,
        tree_mask,
        drafts,
        w_query,
        key_value_weight,
        w_output,
        cache,
    )


def dispatch_kernel(
    place_ref,
    half_ref,
    other_ref,
    drafts_ref,
    gain_ref,
    held_ref,
    router_ref,
    logits_ref,
    *rest,
):
    sent_refs, resid = rest[:-1], rest[-1]
    first = place_ref[1]
    resid[pl.ds(first, 1)] = half_ref[...].astype(jnp.float32)[None]
    resid[pl.ds(1 - first, 1)] = other_ref[...].astype(jnp.float32)[None]
    values = drafts_ref[...].astype(jnp.float32) + resid[...]
    normed = rms_norm(values, gain_ref[...][None, None, :]).astype(jnp.bfloat16)
    normed = normed.reshape(-1, normed.shape[-1])
    for step, sent_ref in enumerate(sent_refs):
        slots = lax.broadcasted_iota(
            jnp.int32, (sent_ref.shape[0], held_ref.shape[1]), 0
        )
        row = held_ref[pl.ds(place_ref[3] ^ step, 1), :]
        matrix = (row == slots).astype(jnp.bfloat16)
        sent_ref[...] = jnp.dot(matrix, normed, preferred_element_type=jnp.float32).astype(
            jnp.bfloat16
        )
    logits_ref[...] = lax.dot_general(
        normed, router_ref[...], (((1,), (1,)), ((), ())), preferred_element_type=jnp.float32
    )


def dispatch_rows(half, other, drafts, gain, held, router, place):
    req_dev, tree, width = drafts.shape
    tokens = req_dev * tree
    whole = pl.BlockSpec(memory_space=pltpu.VMEM)
    scalar = pl.BlockSpec(memory_space=pltpu.SMEM)
    logits, *sent = pl.pallas_call(
        dispatch_kernel,
        out_shape=[jax.ShapeDtypeStruct((tokens, router.shape[0]), jnp.float32)]
        + [jax.ShapeDtypeStruct((CAP, width), jnp.bfloat16)] * held.shape[0],
        in_specs=[scalar] + [whole] * 6,
        out_specs=[whole] * (1 + held.shape[0]),
        scratch_shapes=[pltpu.VMEM((req_dev, tree, width), jnp.float32)],
        compiler_params=pltpu.CompilerParams(vmem_limit_bytes=SOME_VMEM),
        name="dispatch",
    )(place, half, other, drafts, gain, held, router)
    return logits, sent


def fetch_kernel(place_ref, w_in_hbm, w_out_hbm, wi, wo, in_sem, out_sem):
    halves = wi.shape[0]
    inward = pltpu.make_async_copy(w_in_hbm, wi, in_sem)
    outward = pltpu.make_async_copy(
        w_out_hbm.at[pl.ds(place_ref[2] * halves, halves)], wo, out_sem
    )
    inward.start()
    outward.start()
    inward.wait()
    outward.wait()


def fetched(w_in_own, w_out, place):
    halves = w_in_own.shape[0]
    whole = pl.BlockSpec(memory_space=pltpu.VMEM)
    scalar = pl.BlockSpec(memory_space=pltpu.SMEM)
    anywhere = pl.BlockSpec(memory_space=pl.ANY)
    return pl.pallas_call(
        fetch_kernel,
        out_shape=[
            jax.ShapeDtypeStruct(w_in_own.shape, w_in_own.dtype),
            jax.ShapeDtypeStruct((halves,) + w_out.shape[1:], w_out.dtype),
        ],
        in_specs=[scalar, anywhere, anywhere],
        out_specs=[whole] * 2,
        scratch_shapes=[pltpu.SemaphoreType.DMA, pltpu.SemaphoreType.DMA],
        compiler_params=pltpu.CompilerParams(vmem_limit_bytes=SOME_VMEM),
        name="fetch",
    )(place, w_in_own, w_out)


def expert_kernel(place_ref, wi, wo, *rest):
    *row_refs, out_ref, rows = rest
    share = row_refs[0].shape[0]
    for step, row_ref in enumerate(row_refs):
        start = pl.multiple_of((place_ref[3] ^ step) * share, share)
        rows[pl.ds(start, share)] = row_ref[...]
    taken = rows[...]
    acts = []
    for half in range(wi.shape[0]):
        gate = jnp.dot(taken, wi[half, 0], preferred_element_type=jnp.float32)
        upper = jnp.dot(taken, wi[half, 1], preferred_element_type=jnp.float32)
        acts.append((jnp.maximum(gate, 0.0) * upper).astype(jnp.bfloat16))
    acts = jnp.concatenate(acts, axis=1)
    groups, ranks, _, quarter = out_ref.shape
    for rank in range(ranks):
        columns = slice(rank * quarter, (rank + 1) * quarter)
        made = jnp.dot(acts, wo[:, columns], preferred_element_type=jnp.float32)
        out_ref[:, rank] = made.astype(jnp.bfloat16).reshape(groups, share, quarter)


def expert_rows(rows, w_in_own, w_out_own, place, ranks):
    share, width = rows[0].shape
    groups = len(rows)
    whole = pl.BlockSpec(memory_space=pltpu.VMEM)
    scalar = pl.BlockSpec(memory_space=pltpu.SMEM)
    return pl.pallas_call(
        expert_kernel,
        out_shape=jax.ShapeDtypeStruct((groups, ranks, share, width // ranks), jnp.bfloat16),
        in_specs=[scalar] + [whole] * (2 + groups),
        out_specs=whole,
        scratch_shapes=[pltpu.VMEM((groups * share, width), jnp.bfloat16)],
        compiler_params=pltpu.CompilerParams(vmem_limit_bytes=SOME_VMEM),
        name="experts",
    )(place, w_in_own, w_out_own, *rows)


def combine_kernel(
    order_ref, rows_ref, targets_ref, gates_ref, resid_ref, slots_ref, tree_ref, posted_ref
):
    req_dev, tree, quarter = tree_ref.shape
    keep = posted_ref.shape[1]
    tokens = req_dev * tree
    places = lax.broadcasted_iota(jnp.int32, (tokens, rows_ref.shape[0]), 1)
    matrix = jnp.zeros(places.shape, jnp.float32)
    for pick in range(targets_ref.shape[1]):
        matrix = matrix + jnp.where(
            places == targets_ref[:, pick : pick + 1], gates_ref[:, pick : pick + 1], 0.0
        )
    mixture = jnp.dot(
        matrix.astype(jnp.bfloat16), rows_ref[...], preferred_element_type=jnp.float32
    )
    done = (resid_ref[...] + mixture).astype(jnp.bfloat16)
    tree_ref[...] = done.reshape(tree_ref.shape)
    posted_ref[...] = jnp.zeros_like(posted_ref)
    for request in range(req_dev):
        wanted = lax.broadcasted_iota(jnp.int32, (keep, tree), 0)
        chosen = (slots_ref[request : request + 1, :] == wanted).astype(jnp.bfloat16)
        kept = jnp.dot(
            chosen, done[request * tree : (request + 1) * tree], preferred_element_type=jnp.float32
        )
        posted_ref[pl.ds(order_ref[request], 1)] = kept.astype(jnp.bfloat16)[None]


def combine_rows(rows, targets, gates, resid, slots, order, requests):
    tokens, quarter = resid.shape
    req_dev, tree = slots.shape
    whole = pl.BlockSpec(memory_space=pltpu.VMEM)
    scalar = pl.BlockSpec(memory_space=pltpu.SMEM)
    return pl.pallas_call(
        combine_kernel,
        out_shape=[
            jax.ShapeDtypeStruct((req_dev, tree, quarter), jnp.bfloat16),
            jax.ShapeDtypeStruct((requests, KEEP, quarter), jnp.bfloat16),
        ],
        in_specs=[scalar] + [whole] * 5,
        out_specs=[whole] * 2,
        compiler_params=pltpu.CompilerParams(vmem_limit_bytes=SOME_VMEM),
        name="combine",
    )(order, rows, targets, gates, resid, slots)


def on_device(
    drafts,
    gain_attn,
    w_query,
    key_value_weight,
    w_output,
    cache,
    lengths,
    tree_mask,
    depths,
    gain_moe,
    w_router,
    expert_ids,
    w_in,
    w_out,
    slots,
    order,
):
    req_dev, draft_tree, width = drafts.shape
    head_dim = cache.shape[-1]
    kv_heads = cache.shape[2]
    local_heads = w_query.shape[1] // head_dim
    tp_count = lax.axis_size("tp")
    req_count = lax.axis_size("req")
    tp_rank = lax.axis_index("tp")
    head_group = local_heads * tp_count // kv_heads
    kv_head = tp_rank * local_heads // head_group
    tokens = req_dev * draft_tree
    experts = w_router.shape[1]
    pieces = w_in.shape[0]
    quarter = width // tp_count
    first = tp_rank % 2
    place = jnp.stack([kv_head, first, tp_rank, lax.axis_index("req")]).astype(jnp.int32)

    ids = expert_ids.reshape(tokens, -1)
    picks = ids[:, :, None] == jnp.arange(experts)[None, None, :]
    counts = jnp.sum(picks.astype(jnp.int32), axis=1)
    slot_expert = jnp.cumsum(counts, axis=0) - counts
    slot_pick = jnp.sum(jnp.where(picks, slot_expert[:, None, :], 0), axis=-1)
    held = jnp.where(counts == 1, slot_expert, -1).T
    by_expert = pieces == 2 * tp_count
    if by_expert:
        share = CAP
        held = lax.dynamic_index_in_dim(
            held.reshape(req_count, tp_count, tokens), tp_rank, 1, keepdims=False
        )
        targets = ids * CAP + slot_pick
    else:
        share = CAP // tp_count
        held = jnp.repeat(held, 2, axis=0)
        slot_ids = tp_rank * share + jnp.arange(share)
        piece = 2 * ids[:, :, None] + jnp.arange(2)
        lane = (piece // pieces) * tp_count + (slot_pick // share)[:, :, None]
        targets = (lane * pieces + piece % pieces) * share + (slot_pick % share)[:, :, None]
        targets = targets.reshape(tokens, -1)
        matrix = (held[:, None, :] == slot_ids[None, :, None]).astype(jnp.bfloat16)
        matrix = matrix.reshape(-1, tokens)

    mine, theirs = attention_part(
        drafts,
        gain_attn,
        w_query,
        key_value_weight,
        w_output,
        cache,
        lengths,
        tree_mask,
        depths,
        tp_count,
    )
    near = [(i, i ^ 1) for i in range(tp_count)]
    far = [(i, i ^ 2) for i in range(tp_count)]

    def added(left, right):
        return (left.astype(jnp.float32) + right.astype(jnp.float32)).astype(jnp.bfloat16)

    chip = added(mine, lax.ppermute(theirs, "tp", near))
    half = added(chip, lax.ppermute(chip, "tp", far))
    other = lax.ppermute(half, "tp", near)

    if by_expert:
        logits, sent = dispatch_rows(
            half, other, drafts, gain_moe, held, w_router.T, place
        )
        arrived = [sent[0]] + [
            lax.ppermute(sent[step], "req", [(i, i ^ step) for i in range(req_count)])
            for step in range(1, req_count)
        ]
    else:
        resid = jnp.where(first == 0, jnp.stack([half, other]), jnp.stack([other, half]))
        resid = (drafts.astype(jnp.float32) + resid.astype(jnp.float32)).reshape(tokens, width)
        normed2 = rms_norm(resid, gain_moe).astype(jnp.bfloat16)
        logits = jnp.dot(normed2, w_router, preferred_element_type=jnp.float32)
        sent = jnp.dot(matrix, normed2, preferred_element_type=jnp.float32).astype(jnp.bfloat16)
        arrived = lax.all_to_all(
            sent.reshape(req_count, -1, width), "req", split_axis=0, concat_axis=0, tiled=True
        )

    chosen = jax.nn.sigmoid(jnp.sum(jnp.where(picks, logits[:, None, :], 0.0), axis=-1))
    gates = (chosen / jnp.sum(chosen, axis=1, keepdims=True)).astype(jnp.bfloat16)
    gates = gates.astype(jnp.float32)
    start = tp_rank * quarter
    own_attn = jnp.where(
        first == 0,
        jnp.concatenate([half, other], axis=0),
        jnp.concatenate([other, half], axis=0),
    )
    own_resid = lax.dynamic_slice_in_dim(
        drafts.reshape(tokens, width), start, quarter, 1
    ).astype(jnp.float32) + lax.dynamic_slice_in_dim(own_attn, start, quarter, 1).astype(
        jnp.float32
    )

    if by_expert:
        own_in = lax.dynamic_slice_in_dim(w_in, tp_rank * 2, 2, 0).transpose(0, 2, 1, 3)
        own_in, own_out = fetched(own_in, w_out, place)
        produced = expert_rows(arrived, own_in, own_out.reshape(-1, width), place, tp_count)
    else:
        gates = jnp.repeat(gates, 2, axis=1)
        rows_in = arrived.reshape(req_count, pieces, share, width)
        rows_in = rows_in.transpose(1, 0, 2, 3).reshape(pieces, req_count * share, width)
        gate_up = jnp.einsum("prd,pdgf->prgf", rows_in, w_in, preferred_element_type=jnp.float32)
        act = (jax.nn.relu(gate_up[:, :, 0]) * gate_up[:, :, 1]).astype(jnp.bfloat16)
        produced = jnp.einsum(
            "prf,pfd->prd", act, w_out, preferred_element_type=jnp.float32
        ).astype(jnp.bfloat16)
        produced = produced.reshape(pieces, req_count, share, tp_count, quarter)
        produced = produced.transpose(1, 3, 0, 2, 4)
    returned = lax.all_to_all(
        produced.reshape(req_count * tp_count, -1, quarter),
        ("req", "tp"),
        split_axis=0,
        concat_axis=0,
        tiled=True,
    )
    tree_out, posted = combine_rows(
        returned.reshape(-1, quarter),
        targets,
        gates,
        own_resid,
        slots,
        order,
        req_count * req_dev,
    )
    received = lax.all_to_all(
        posted.reshape(req_count, req_dev, KEEP, quarter),
        "req",
        split_axis=0,
        concat_axis=0,
        tiled=True,
    )
    accepted = jnp.sum(received.astype(jnp.float32), axis=0).astype(jnp.bfloat16)
    return (tree_out, accepted)


def solution(mesh):
    placed = (
        P("req", None, None),
        P(),
        P(None, "tp"),
        P(),
        P("tp", None),
        P("req", None, None, None, None),
        P("req"),
        P("req", None, None),
        P("req", None),
        P(),
        P(),
        P("req", None, None),
        P("req", None, None, None),
        P("req", None, None),
        P("req", None),
        P("req"),
    )
    return jax.shard_map(
        on_device,
        mesh=mesh,
        in_specs=placed,
        out_specs=(P("req", None, "tp"), P("req", None, "tp")),
        check_vma=False,
    )
```

```python
import functools

import jax
import jax.numpy as jnp
from jax import lax
from jax.experimental import pallas as pl
from jax.experimental.pallas import tpu as pltpu
from jax.sharding import PartitionSpec as P

KEEP = 16
CAP = 32
REQ_DEV = 2
TOPK = 4


EPSILON = 1e-06
THETA = 1000000.0
LOG2E = 1.4426950408889634
BLOCK = 1536
WHOLE_VMEM = 60 * 1024 * 1024
SOME_VMEM = 20 * 1024 * 1024


def rms_norm(values, gain_vec):
    return (
        values * lax.rsqrt(jnp.mean(values * values, axis=-1, keepdims=True) + EPSILON) * gain_vec
    )


def column_of(row):
    count = row.shape[1]
    at_row = lax.broadcasted_iota(jnp.int32, (count, count), 0)
    at_col = lax.broadcasted_iota(jnp.int32, (count, count), 1)
    return jnp.sum(jnp.where(at_row == at_col, row, 0.0), axis=1, keepdims=True)


def attention_kernel(
    tp_count,
    lengths_ref,
    gain_hbm,
    depths_hbm,
    mask_hbm,
    drafts_hbm,
    wq_hbm,
    wkv_hbm,
    wo_hbm,
    cache_hbm,
    mine_ref,
    theirs_ref,
    gain_ref,
    depths_ref,
    mask_ref,
    drafts,
    wq,
    wk,
    wv,
    wo,
    keys,
    vals,
    scores,
    weight_sem,
    cache_sem,
):
    req_dev, tree, width = drafts.shape
    head_dim = cache_hbm.shape[-1]
    kv_heads = cache_hbm.shape[2]
    local_heads = wq.shape[1] // head_dim
    block = scores.shape[2]
    tp_rank = lax.axis_index("tp")
    kv_head = tp_rank * local_heads // (local_heads * tp_count // kv_heads)
    first = lax.rem(tp_rank, 2)

    def column_copy(target, which, sem):
        start = pl.multiple_of((which * kv_heads + kv_head) * head_dim, head_dim)
        return pltpu.make_async_copy(wkv_hbm.at[:, pl.ds(start, head_dim)], target, sem)

    def cache_copy(request, which, index):
        rows = pl.ds(pl.multiple_of(index * block, block), block)
        target = vals if which else keys
        return pltpu.make_async_copy(
            cache_hbm.at[request, which, kv_head, rows],
            target.at[request, rows],
            cache_sem.at[request, which, index],
        )

    copy_d = pltpu.make_async_copy(drafts_hbm, drafts, weight_sem.at[4])
    copy_d.start()
    small = [
        pltpu.make_async_copy(gain_hbm, gain_ref, weight_sem.at[5]),
        pltpu.make_async_copy(depths_hbm, depths_ref, weight_sem.at[6]),
        pltpu.make_async_copy(mask_hbm, mask_ref, weight_sem.at[7]),
    ]
    for copy in small:
        copy.start()
    copy_q = pltpu.make_async_copy(wq_hbm, wq, weight_sem.at[0])
    copy_k = column_copy(wk, 0, weight_sem.at[1])
    copy_v = column_copy(wv, 1, weight_sem.at[2])
    copy_o = pltpu.make_async_copy(wo_hbm, wo, weight_sem.at[3])
    copy_q.start()
    copy_k.start()
    copy_v.start()
    limits = [lengths_ref[request] for request in range(req_dev)]
    counts = [(limit + block - 1) // block for limit in limits]
    for request in range(req_dev):
        for which in range(2):

            @pl.loop(0, counts[request])
            def _(index, request=request, which=which):
                cache_copy(request, which, index).start()

    copy_o.start()

    copy_d.wait()
    small[0].wait()
    inputs = drafts[...].astype(jnp.float32).reshape(req_dev * tree, width)
    normed = rms_norm(inputs, gain_ref[...][None, :]).astype(jnp.bfloat16)
    small[1].wait()
    small[2].wait()
    at = [
        column_of(depths_ref[request : request + 1, :].astype(jnp.float32))
        + limits[request].astype(jnp.float32)
        for request in range(req_dev)
    ]
    lane = lax.broadcasted_iota(jnp.int32, (req_dev * tree, head_dim), 1)
    half_dim = head_dim // 2
    freqs = jnp.exp(
        -jnp.log(THETA) * lax.rem(lane, half_dim).astype(jnp.float32) / half_dim
    )
    angles = jnp.concatenate(at, axis=0) * freqs
    cosine = jnp.cos(angles)
    sine = jnp.sin(angles) * jnp.where(lane < head_dim // 2, -1.0, 1.0)

    def turned(vectors):
        return (vectors * cosine + pltpu.roll(vectors, head_dim // 2, 1) * sine).astype(jnp.bfloat16)

    copy_q.wait()
    query_all = jnp.dot(normed, wq[...], preferred_element_type=jnp.float32)
    queries = [
        turned(query_all[:, head * head_dim : (head + 1) * head_dim]) for head in range(local_heads)
    ]
    copy_k.wait()
    key_new = turned(jnp.dot(normed, wk[...], preferred_element_type=jnp.float32))
    copy_v.wait()
    val_new = jnp.dot(normed, wv[...], preferred_element_type=jnp.float32).astype(jnp.bfloat16)
    slope = LOG2E * head_dim ** (-0.5)
    rows = local_heads * tree
    contract = (((1,), (1,)), ((), ()))

    def lanes_down(values, step):
        parts = [values[:, i : i + 128] for i in range(0, values.shape[1], 128)]
        return functools.reduce(step, parts)

    mixed = []
    for request in range(req_dev):
        span = slice(request * tree, (request + 1) * tree)
        own = jnp.concatenate([q[span] for q in queries], axis=0)
        allowed = jnp.concatenate([mask_ref[request]] * local_heads, axis=0) > 0
        tree_scores = lax.dot_general(
            own, key_new[span], contract, preferred_element_type=jnp.float32
        )
        tree_scores = jnp.where(allowed, tree_scores, -jnp.inf)
        limit = limits[request]

        def score_step(index, best, request=request, own=own, limit=limit):
            cache_copy(request, 0, index).wait()
            offset = pl.multiple_of(index * block, block)
            found = lax.dot_general(
                own,
                keys[request, pl.ds(offset, block)],
                contract,
                preferred_element_type=jnp.float32,
            )
            inside = offset + lax.broadcasted_iota(jnp.int32, found.shape, 1) < limit
            found = jnp.where(inside, found, -jnp.inf)
            scores[index] = found
            return jnp.maximum(best, lanes_down(found, jnp.maximum))

        best = lax.fori_loop(
            0, counts[request], score_step, jnp.full((rows, 128), -jnp.inf, jnp.float32)
        )
        peak = jnp.maximum(
            jnp.max(best, axis=1, keepdims=True), jnp.max(tree_scores, axis=1, keepdims=True)
        )
        tree_weights = jnp.exp2((tree_scores - peak) * slope)
        start = (
            jnp.zeros((rows, 128), jnp.float32),
            jnp.dot(
                tree_weights.astype(jnp.bfloat16), val_new[span], preferred_element_type=jnp.float32
            ),
        )

        def sum_step(index, carry, request=request, peak=peak):
            total, accum = carry
            cache_copy(request, 1, index).wait()
            offset = pl.multiple_of(index * block, block)
            weights = jnp.exp2((scores[index] - peak) * slope)
            accum = accum + jnp.dot(
                weights.astype(jnp.bfloat16),
                vals[request, pl.ds(offset, block)],
                preferred_element_type=jnp.float32,
            )
            return total + lanes_down(weights, jnp.add), accum

        total, accum = lax.fori_loop(0, counts[request], sum_step, start)
        total = jnp.sum(total, axis=1, keepdims=True) + jnp.sum(tree_weights, axis=1, keepdims=True)
        mixed.append((accum / total).astype(jnp.bfloat16))

    copy_o.wait()
    for request in range(req_dev):
        heads = jnp.concatenate(
            [mixed[request][head * tree : (head + 1) * tree] for head in range(local_heads)], axis=1
        )
        part = jnp.dot(heads, wo[...], preferred_element_type=jnp.float32).astype(jnp.bfloat16)

        @pl.when(first == request)
        def _(part=part):
            mine_ref[...] = part

        @pl.when(first != request)
        def _(part=part):
            theirs_ref[...] = part


def attention_part(
    drafts, gain, w_query, key_value_weight, w_output, cache, lengths, tree_mask, depths, tp_count
):
    req_dev, tree, width = drafts.shape
    head_dim = cache.shape[-1]
    longest = cache.shape[3]
    block = min(BLOCK, longest)
    local = w_query.shape[1]
    whole = pl.BlockSpec(memory_space=pltpu.VMEM)
    scalar = pl.BlockSpec(memory_space=pltpu.SMEM)
    anywhere = pl.BlockSpec(memory_space=pl.ANY)
    bf16 = jnp.bfloat16
    return pl.pallas_call(
        functools.partial(attention_kernel, tp_count),
        out_shape=[jax.ShapeDtypeStruct((tree, width), bf16)] * 2,
        in_specs=[scalar] + [anywhere] * 8,
        out_specs=[whole] * 2,
        scratch_shapes=[
            pltpu.VMEM((width,), jnp.float32),
            pltpu.VMEM((req_dev, tree), jnp.int32),
            pltpu.VMEM((req_dev, tree, tree), jnp.int32),
            pltpu.VMEM((req_dev, tree, width), bf16),
            pltpu.VMEM((width, local), bf16),
            pltpu.VMEM((width, head_dim), bf16),
            pltpu.VMEM((width, head_dim), bf16),
            pltpu.VMEM((local, width), bf16),
            pltpu.VMEM((req_dev, longest, head_dim), bf16),
            pltpu.VMEM((req_dev, longest, head_dim), bf16),
            pltpu.VMEM((longest // block, local // head_dim * tree, block), jnp.float32),
            pltpu.SemaphoreType.DMA((8,)),
            pltpu.SemaphoreType.DMA((req_dev, 2, longest // block)),
        ],
        compiler_params=pltpu.CompilerParams(vmem_limit_bytes=WHOLE_VMEM),
        name="attention",
    )(
        lengths,
        gain,
        depths,
        tree_mask,
        drafts,
        w_query,
        key_value_weight,
        w_output,
        cache,
    )


def dispatch_kernel(
    place_ref,
    half_ref,
    other_ref,
    drafts_ref,
    gain_ref,
    held_ref,
    router_ref,
    logits_ref,
    *rest,
):
    sent_refs, resid = rest[:-1], rest[-1]
    first = place_ref[1]
    resid[pl.ds(first, 1)] = half_ref[...].astype(jnp.float32)[None]
    resid[pl.ds(1 - first, 1)] = other_ref[...].astype(jnp.float32)[None]
    values = drafts_ref[...].astype(jnp.float32) + resid[...]
    normed = rms_norm(values, gain_ref[...][None, None, :]).astype(jnp.bfloat16)
    normed = normed.reshape(-1, normed.shape[-1])
    for step, sent_ref in enumerate(sent_refs):
        slots = lax.broadcasted_iota(
            jnp.int32, (sent_ref.shape[0], held_ref.shape[1]), 0
        )
        row = held_ref[pl.ds(place_ref[3] ^ step, 1), :]
        matrix = (row == slots).astype(jnp.bfloat16)
        sent_ref[...] = jnp.dot(matrix, normed, preferred_element_type=jnp.float32).astype(
            jnp.bfloat16
        )
    logits_ref[...] = lax.dot_general(
        normed, router_ref[...], (((1,), (1,)), ((), ())), preferred_element_type=jnp.float32
    )


def dispatch_rows(half, other, drafts, gain, held, router, place):
    req_dev, tree, width = drafts.shape
    tokens = req_dev * tree
    whole = pl.BlockSpec(memory_space=pltpu.VMEM)
    scalar = pl.BlockSpec(memory_space=pltpu.SMEM)
    logits, *sent = pl.pallas_call(
        dispatch_kernel,
        out_shape=[jax.ShapeDtypeStruct((tokens, router.shape[0]), jnp.float32)]
        + [jax.ShapeDtypeStruct((CAP, width), jnp.bfloat16)] * held.shape[0],
        in_specs=[scalar] + [whole] * 6,
        out_specs=[whole] * (1 + held.shape[0]),
        scratch_shapes=[pltpu.VMEM((req_dev, tree, width), jnp.float32)],
        compiler_params=pltpu.CompilerParams(vmem_limit_bytes=SOME_VMEM),
        name="dispatch",
    )(place, half, other, drafts, gain, held, router)
    return logits, sent


def fetch_kernel(place_ref, w_in_hbm, w_out_hbm, wi, wo, in_sem, out_sem):
    halves = wi.shape[0]
    inward = pltpu.make_async_copy(w_in_hbm, wi, in_sem)
    outward = pltpu.make_async_copy(
        w_out_hbm.at[pl.ds(place_ref[2] * halves, halves)], wo, out_sem
    )
    inward.start()
    outward.start()
    inward.wait()
    outward.wait()


def fetched(w_in_own, w_out, place):
    halves = w_in_own.shape[0]
    whole = pl.BlockSpec(memory_space=pltpu.VMEM)
    scalar = pl.BlockSpec(memory_space=pltpu.SMEM)
    anywhere = pl.BlockSpec(memory_space=pl.ANY)
    return pl.pallas_call(
        fetch_kernel,
        out_shape=[
            jax.ShapeDtypeStruct(w_in_own.shape, w_in_own.dtype),
            jax.ShapeDtypeStruct((halves,) + w_out.shape[1:], w_out.dtype),
        ],
        in_specs=[scalar, anywhere, anywhere],
        out_specs=[whole] * 2,
        scratch_shapes=[pltpu.SemaphoreType.DMA, pltpu.SemaphoreType.DMA],
        compiler_params=pltpu.CompilerParams(vmem_limit_bytes=SOME_VMEM),
        name="fetch",
    )(place, w_in_own, w_out)


def expert_kernel(place_ref, wi, wo, *rest):
    *row_refs, out_ref, rows = rest
    share = row_refs[0].shape[0]
    for step, row_ref in enumerate(row_refs):
        start = pl.multiple_of((place_ref[4] ^ step) * share, share)
        rows[pl.ds(start, share)] = row_ref[...]
    taken = rows[...]
    acts = []
    for half in range(wi.shape[0]):
        gate = jnp.dot(taken, wi[half, 0], preferred_element_type=jnp.float32)
        upper = jnp.dot(taken, wi[half, 1], preferred_element_type=jnp.float32)
        acts.append((jnp.maximum(gate, 0.0) * upper).astype(jnp.bfloat16))
    acts = jnp.concatenate(acts, axis=1)
    groups, ranks, sides, _, quarter = out_ref.shape
    for rank in range(ranks):
        columns = slice(rank * quarter, (rank + 1) * quarter)
        made = jnp.dot(acts, wo[:, columns], preferred_element_type=jnp.float32)
        made = made.astype(jnp.bfloat16).reshape(sides, groups, share, quarter)
        for side in range(sides):
            out_ref[:, rank, side] = made[side]


def expert_rows(rows, w_in_own, w_out_own, place, ranks):
    share, width = rows[0].shape
    groups = len(rows)
    whole = pl.BlockSpec(memory_space=pltpu.VMEM)
    scalar = pl.BlockSpec(memory_space=pltpu.SMEM)
    return pl.pallas_call(
        expert_kernel,
        out_shape=jax.ShapeDtypeStruct(
            (groups // 2, ranks, 2, share, width // ranks), jnp.bfloat16
        ),
        in_specs=[scalar] + [whole] * (2 + groups),
        out_specs=whole,
        scratch_shapes=[pltpu.VMEM((groups * share, width), jnp.bfloat16)],
        compiler_params=pltpu.CompilerParams(vmem_limit_bytes=SOME_VMEM),
        name="experts",
    )(place, w_in_own, w_out_own, *rows)


def combine_kernel(
    order_ref, rows_ref, targets_ref, gates_ref, resid_ref, slots_ref, tree_ref, posted_ref
):
    req_dev, tree, quarter = tree_ref.shape
    keep = posted_ref.shape[1]
    tokens = req_dev * tree
    places = lax.broadcasted_iota(jnp.int32, (tokens, rows_ref.shape[0]), 1)
    matrix = jnp.zeros(places.shape, jnp.float32)
    for pick in range(targets_ref.shape[1]):
        matrix = matrix + jnp.where(
            places == targets_ref[:, pick : pick + 1], gates_ref[:, pick : pick + 1], 0.0
        )
    mixture = jnp.dot(
        matrix.astype(jnp.bfloat16), rows_ref[...], preferred_element_type=jnp.float32
    )
    done = (resid_ref[...] + mixture).astype(jnp.bfloat16)
    tree_ref[...] = done.reshape(tree_ref.shape)
    posted_ref[...] = jnp.zeros_like(posted_ref)
    for request in range(req_dev):
        wanted = lax.broadcasted_iota(jnp.int32, (keep, tree), 0)
        chosen = (slots_ref[request : request + 1, :] == wanted).astype(jnp.bfloat16)
        kept = jnp.dot(
            chosen, done[request * tree : (request + 1) * tree], preferred_element_type=jnp.float32
        )
        posted_ref[pl.ds(order_ref[request], 1)] = kept.astype(jnp.bfloat16)[None]


def combine_rows(rows, targets, gates, resid, slots, order, requests):
    tokens, quarter = resid.shape
    req_dev, tree = slots.shape
    whole = pl.BlockSpec(memory_space=pltpu.VMEM)
    scalar = pl.BlockSpec(memory_space=pltpu.SMEM)
    return pl.pallas_call(
        combine_kernel,
        out_shape=[
            jax.ShapeDtypeStruct((req_dev, tree, quarter), jnp.bfloat16),
            jax.ShapeDtypeStruct((requests, KEEP, quarter), jnp.bfloat16),
        ],
        in_specs=[scalar] + [whole] * 5,
        out_specs=[whole] * 2,
        compiler_params=pltpu.CompilerParams(vmem_limit_bytes=SOME_VMEM),
        name="combine",
    )(order, rows, targets, gates, resid, slots)


def mixture(place_ref, rows_ref, pack_ref, side):
    experts, _, quarter = rows_ref.shape
    pack = jnp.transpose(pack_ref[...])
    first = place_ref[5] * (experts * CAP)
    places = lax.broadcasted_iota(jnp.int32, (pack.shape[0], experts * CAP), 1) + first
    matrix = jnp.zeros(places.shape, jnp.float32)
    for pick in range(TOPK):
        target = pack[:, pick : pick + 1].astype(jnp.int32)
        gate = pack[:, TOPK + pick : TOPK + pick + 1]
        matrix = matrix + jnp.where(places == target, gate, 0.0)
    rows = rows_ref[:, side * CAP : (side + 1) * CAP].reshape(experts * CAP, quarter)
    return jnp.dot(matrix.astype(jnp.bfloat16), rows, preferred_element_type=jnp.float32)


def relay_kernel(place_ref, rows_ref, partner_ref, relay_ref):
    relay_ref[...] = mixture(place_ref, rows_ref, partner_ref, 1).astype(jnp.bfloat16)


def relayed(place, rows, partner):
    whole = pl.BlockSpec(memory_space=pltpu.VMEM)
    scalar = pl.BlockSpec(memory_space=pltpu.SMEM)
    return pl.pallas_call(
        relay_kernel,
        out_shape=jax.ShapeDtypeStruct((partner.shape[1], rows.shape[2]), jnp.bfloat16),
        in_specs=[scalar] + [whole] * 2,
        out_specs=whole,
        compiler_params=pltpu.CompilerParams(vmem_limit_bytes=SOME_VMEM),
        name="relay",
    )(place, rows, partner)


def gather_kernel(
    place_ref, rows_ref, own_ref, partner_ref, resid_ref, relay_ref, sum_ref, posted_ref
):
    requests, keep, quarter = posted_ref.shape
    tokens = own_ref.shape[1]
    tree = tokens // REQ_DEV
    own_sum = resid_ref[...] + mixture(place_ref, rows_ref, own_ref, 0)
    sum_ref[...] = own_sum
    posted = [jnp.zeros((keep, quarter), jnp.float32)] * requests
    for pack_ref, done in (
        (own_ref, own_sum.astype(jnp.bfloat16)),
        (partner_ref, relay_ref[...]),
    ):
        slots = pack_ref[2 * TOPK : 2 * TOPK + 1, :].astype(jnp.int32)
        chosen = lax.broadcasted_iota(jnp.int32, (keep, tokens), 0) == slots
        homes = pack_ref[2 * TOPK + 1 : 2 * TOPK + 2, :].astype(jnp.int32)
        for request in range(REQ_DEV):
            start = request * tree
            rows = jnp.dot(
                chosen[:, start : start + tree].astype(jnp.bfloat16),
                done[start : start + tree],
                preferred_element_type=jnp.float32,
            )
            home = homes[:, start : start + 1]
            posted = [jnp.where(home == place, rows, held) for place, held in enumerate(posted)]
    for place in range(requests):
        posted_ref[place] = posted[place].astype(jnp.bfloat16)


def gathered(place, rows, own, partner, resid, relay, requests):
    tokens, quarter = resid.shape
    whole = pl.BlockSpec(memory_space=pltpu.VMEM)
    scalar = pl.BlockSpec(memory_space=pltpu.SMEM)
    return pl.pallas_call(
        gather_kernel,
        out_shape=[
            jax.ShapeDtypeStruct((tokens, quarter), jnp.float32),
            jax.ShapeDtypeStruct((requests, KEEP, quarter), jnp.bfloat16),
        ],
        in_specs=[scalar] + [whole] * 5,
        out_specs=[whole] * 2,
        compiler_params=pltpu.CompilerParams(vmem_limit_bytes=SOME_VMEM),
        name="gather",
    )(place, rows, own, partner, resid, relay)


def finish_kernel(sum_ref, other_ref, received_ref, tree_ref, accepted_ref):
    done = (sum_ref[...] + other_ref[...].astype(jnp.float32)).astype(jnp.bfloat16)
    tree_ref[...] = done.reshape(tree_ref.shape)
    total = received_ref[0].astype(jnp.float32)
    for source in range(1, received_ref.shape[0]):
        total = total + received_ref[source].astype(jnp.float32)
    accepted_ref[...] = total.astype(jnp.bfloat16)


def finished(own_sum, other_sum, received):
    tokens, quarter = own_sum.shape
    req_dev = received.shape[1]
    whole = pl.BlockSpec(memory_space=pltpu.VMEM)
    return pl.pallas_call(
        finish_kernel,
        out_shape=[
            jax.ShapeDtypeStruct((req_dev, tokens // req_dev, quarter), jnp.bfloat16),
            jax.ShapeDtypeStruct(received.shape[1:], jnp.bfloat16),
        ],
        in_specs=[whole] * 3,
        out_specs=[whole] * 2,
        compiler_params=pltpu.CompilerParams(vmem_limit_bytes=SOME_VMEM),
        name="finish",
    )(own_sum, other_sum, received)


def on_device(
    drafts,
    gain_attn,
    w_query,
    key_value_weight,
    w_output,
    cache,
    lengths,
    tree_mask,
    depths,
    gain_moe,
    w_router,
    expert_ids,
    w_in,
    w_out,
    slots,
    order,
):
    req_dev, draft_tree, width = drafts.shape
    head_dim = cache.shape[-1]
    kv_heads = cache.shape[2]
    local_heads = w_query.shape[1] // head_dim
    tp_count = lax.axis_size("tp")
    req_count = lax.axis_size("req")
    tp_rank = lax.axis_index("tp")
    head_group = local_heads * tp_count // kv_heads
    kv_head = tp_rank * local_heads // head_group
    tokens = req_dev * draft_tree
    experts = w_router.shape[1]
    pieces = w_in.shape[0]
    quarter = width // tp_count
    first = tp_rank % 2
    req_rank = lax.axis_index("req")
    side = req_count // 2
    place = jnp.stack(
        [kv_head, first, tp_rank, req_rank, req_rank % side, req_rank // side]
    ).astype(jnp.int32)

    ids = expert_ids.reshape(tokens, -1)
    picks = ids[:, :, None] == jnp.arange(experts)[None, None, :]
    counts = jnp.sum(picks.astype(jnp.int32), axis=1)
    slot_expert = jnp.cumsum(counts, axis=0) - counts
    slot_pick = jnp.sum(jnp.where(picks, slot_expert[:, None, :], 0), axis=-1)
    held = jnp.where(counts == 1, slot_expert, -1).T
    by_expert = pieces == 2 * tp_count and req_count == 8 and req_dev == REQ_DEV
    if by_expert:
        share = CAP
        held = lax.dynamic_index_in_dim(
            held.reshape(req_count, tp_count, tokens), tp_rank, 1, keepdims=False
        )
        targets = ids * CAP + slot_pick
    else:
        share = CAP // tp_count
        held = jnp.repeat(held, 2, axis=0)
        slot_ids = tp_rank * share + jnp.arange(share)
        piece = 2 * ids[:, :, None] + jnp.arange(2)
        lane = (piece // pieces) * tp_count + (slot_pick // share)[:, :, None]
        targets = (lane * pieces + piece % pieces) * share + (slot_pick % share)[:, :, None]
        targets = targets.reshape(tokens, -1)
        matrix = (held[:, None, :] == slot_ids[None, :, None]).astype(jnp.bfloat16)
        matrix = matrix.reshape(-1, tokens)

    mine, theirs = attention_part(
        drafts,
        gain_attn,
        w_query,
        key_value_weight,
        w_output,
        cache,
        lengths,
        tree_mask,
        depths,
        tp_count,
    )
    near = [(i, i ^ 1) for i in range(tp_count)]
    far = [(i, i ^ 2) for i in range(tp_count)]

    def added(left, right):
        return (left.astype(jnp.float32) + right.astype(jnp.float32)).astype(jnp.bfloat16)

    chip = added(mine, lax.ppermute(theirs, "tp", near))
    half = added(chip, lax.ppermute(chip, "tp", far))
    other = lax.ppermute(half, "tp", near)

    if by_expert:
        logits, sent = dispatch_rows(
            half, other, drafts, gain_moe, held, w_router.T, place
        )
        arrived = [sent[0]] + [
            lax.ppermute(sent[step], "req", [(i, i ^ step) for i in range(req_count)])
            for step in range(1, req_count)
        ]
    else:
        resid = jnp.where(first == 0, jnp.stack([half, other]), jnp.stack([other, half]))
        resid = (drafts.astype(jnp.float32) + resid.astype(jnp.float32)).reshape(tokens, width)
        normed2 = rms_norm(resid, gain_moe).astype(jnp.bfloat16)
        logits = jnp.dot(normed2, w_router, preferred_element_type=jnp.float32)
        sent = jnp.dot(matrix, normed2, preferred_element_type=jnp.float32).astype(jnp.bfloat16)
        arrived = lax.all_to_all(
            sent.reshape(req_count, -1, width), "req", split_axis=0, concat_axis=0, tiled=True
        )

    chosen = jax.nn.sigmoid(jnp.sum(jnp.where(picks, logits[:, None, :], 0.0), axis=-1))
    gates = (chosen / jnp.sum(chosen, axis=1, keepdims=True)).astype(jnp.bfloat16)
    gates = gates.astype(jnp.float32)
    start = tp_rank * quarter
    own_attn = jnp.where(
        first == 0,
        jnp.concatenate([half, other], axis=0),
        jnp.concatenate([other, half], axis=0),
    )
    own_resid = lax.dynamic_slice_in_dim(
        drafts.reshape(tokens, width), start, quarter, 1
    ).astype(jnp.float32) + lax.dynamic_slice_in_dim(own_attn, start, quarter, 1).astype(
        jnp.float32
    )

    if by_expert:
        own_in = lax.dynamic_slice_in_dim(w_in, tp_rank * 2, 2, 0).transpose(0, 2, 1, 3)
        own_in, own_out = fetched(own_in, w_out, place)
        produced = expert_rows(arrived, own_in, own_out.reshape(-1, width), place, tp_count)
    else:
        gates = jnp.repeat(gates, 2, axis=1)
        rows_in = arrived.reshape(req_count, pieces, share, width)
        rows_in = rows_in.transpose(1, 0, 2, 3).reshape(pieces, req_count * share, width)
        gate_up = jnp.einsum("prd,pdgf->prgf", rows_in, w_in, preferred_element_type=jnp.float32)
        act = (jax.nn.relu(gate_up[:, :, 0]) * gate_up[:, :, 1]).astype(jnp.bfloat16)
        produced = jnp.einsum(
            "prf,pfd->prd", act, w_out, preferred_element_type=jnp.float32
        ).astype(jnp.bfloat16)
        produced = produced.reshape(pieces, req_count, share, tp_count, quarter)
        produced = produced.transpose(1, 3, 0, 2, 4)
    if by_expert:
        across = [(i, i ^ side) for i in range(req_count)]
        halves = [
            list(range(i * side * tp_count, (i + 1) * side * tp_count)) for i in range(2)
        ]
        own = jnp.concatenate(
            [
                targets.astype(jnp.float32).T,
                gates.T,
                slots.reshape(1, tokens).astype(jnp.float32),
                jnp.repeat(order, draft_tree).reshape(1, tokens).astype(jnp.float32),
                jnp.zeros((6, tokens), jnp.float32),
            ],
            axis=0,
        )
        partner = lax.ppermute(own, "req", across)
        returned = lax.all_to_all(
            produced.reshape(side * tp_count, -1, quarter),
            ("req", "tp"),
            split_axis=0,
            concat_axis=0,
            axis_index_groups=halves,
            tiled=True,
        )
        relay = relayed(place, returned, partner)
        other_sum = lax.ppermute(relay, "req", across)
        own_sum, posted = gathered(
            place, returned, own, partner, own_resid, relay, req_count * req_dev
        )
    else:
        returned = lax.all_to_all(
            produced.reshape(req_count * tp_count, -1, quarter),
            ("req", "tp"),
            split_axis=0,
            concat_axis=0,
            tiled=True,
        )
        tree_out, posted = combine_rows(
            returned.reshape(-1, quarter),
            targets,
            gates,
            own_resid,
            slots,
            order,
            req_count * req_dev,
        )
    received = lax.all_to_all(
        posted.reshape(req_count, req_dev, KEEP, quarter),
        "req",
        split_axis=0,
        concat_axis=0,
        tiled=True,
    )
    if by_expert:
        tree_out, accepted = finished(own_sum, other_sum, received)
    else:
        accepted = jnp.sum(received.astype(jnp.float32), axis=0).astype(jnp.bfloat16)
    return (tree_out, accepted)


def solution(mesh):
    placed = (
        P("req", None, None),
        P(),
        P(None, "tp"),
        P(),
        P("tp", None),
        P("req", None, None, None, None),
        P("req"),
        P("req", None, None),
        P("req", None),
        P(),
        P(),
        P("req", None, None),
        P("req", None, None, None),
        P("req", None, None),
        P("req", None),
        P("req"),
    )
    return jax.shard_map(
        on_device,
        mesh=mesh,
        in_specs=placed,
        out_specs=(P("req", None, "tp"), P("req", None, "tp")),
        check_vma=False,
    )
```

```python
import functools

import jax
import jax.numpy as jnp
from jax import lax
from jax.experimental import pallas as pl
from jax.experimental.pallas import tpu as pltpu
from jax.sharding import PartitionSpec as P

KEEP = 16
CAP = 32
REQ_DEV = 2
TOPK = 4
TURNS = (1, 2, 4, 5, 6, 7, 3, 0)


EPSILON = 1e-06
THETA = 1000000.0
LOG2E = 1.4426950408889634
BLOCK = 1536
WHOLE_VMEM = 60 * 1024 * 1024
SOME_VMEM = 20 * 1024 * 1024


def rms_norm(values, gain_vec):
    return (
        values * lax.rsqrt(jnp.mean(values * values, axis=-1, keepdims=True) + EPSILON) * gain_vec
    )


def column_of(row):
    count = row.shape[1]
    at_row = lax.broadcasted_iota(jnp.int32, (count, count), 0)
    at_col = lax.broadcasted_iota(jnp.int32, (count, count), 1)
    return jnp.sum(jnp.where(at_row == at_col, row, 0.0), axis=1, keepdims=True)


def attention_kernel(
    tp_count,
    lengths_ref,
    gain_hbm,
    depths_hbm,
    mask_hbm,
    drafts_hbm,
    wq_hbm,
    wkv_hbm,
    wo_hbm,
    cache_hbm,
    mine_ref,
    theirs_ref,
    gain_ref,
    depths_ref,
    mask_ref,
    drafts,
    wq,
    wk,
    wv,
    wo,
    keys,
    vals,
    scores,
    weight_sem,
    cache_sem,
):
    req_dev, tree, width = drafts.shape
    head_dim = cache_hbm.shape[-1]
    kv_heads = cache_hbm.shape[2]
    local_heads = wq.shape[1] // head_dim
    block = scores.shape[2]
    tp_rank = lax.axis_index("tp")
    kv_head = tp_rank * local_heads // (local_heads * tp_count // kv_heads)
    first = lax.rem(tp_rank, 2)

    def column_copy(target, which, sem):
        start = pl.multiple_of((which * kv_heads + kv_head) * head_dim, head_dim)
        return pltpu.make_async_copy(wkv_hbm.at[:, pl.ds(start, head_dim)], target, sem)

    def cache_copy(request, which, index):
        rows = pl.ds(pl.multiple_of(index * block, block), block)
        target = vals if which else keys
        return pltpu.make_async_copy(
            cache_hbm.at[request, which, kv_head, rows],
            target.at[request, rows],
            cache_sem.at[request, which, index],
        )

    copy_d = pltpu.make_async_copy(drafts_hbm, drafts, weight_sem.at[4])
    copy_d.start()
    small = [
        pltpu.make_async_copy(gain_hbm, gain_ref, weight_sem.at[5]),
        pltpu.make_async_copy(depths_hbm, depths_ref, weight_sem.at[6]),
        pltpu.make_async_copy(mask_hbm, mask_ref, weight_sem.at[7]),
    ]
    for copy in small:
        copy.start()
    copy_q = pltpu.make_async_copy(wq_hbm, wq, weight_sem.at[0])
    copy_k = column_copy(wk, 0, weight_sem.at[1])
    copy_v = column_copy(wv, 1, weight_sem.at[2])
    copy_o = pltpu.make_async_copy(wo_hbm, wo, weight_sem.at[3])
    copy_q.start()
    copy_k.start()
    copy_v.start()
    limits = [lengths_ref[request] for request in range(req_dev)]
    counts = [(limit + block - 1) // block for limit in limits]
    for request in range(req_dev):
        for which in range(2):

            @pl.loop(0, counts[request])
            def _(index, request=request, which=which):
                cache_copy(request, which, index).start()

    copy_o.start()

    copy_d.wait()
    small[0].wait()
    inputs = drafts[...].astype(jnp.float32).reshape(req_dev * tree, width)
    normed = rms_norm(inputs, gain_ref[...][None, :]).astype(jnp.bfloat16)
    small[1].wait()
    small[2].wait()
    at = [
        column_of(depths_ref[request : request + 1, :].astype(jnp.float32))
        + limits[request].astype(jnp.float32)
        for request in range(req_dev)
    ]
    lane = lax.broadcasted_iota(jnp.int32, (req_dev * tree, head_dim), 1)
    half_dim = head_dim // 2
    freqs = jnp.exp(
        -jnp.log(THETA) * lax.rem(lane, half_dim).astype(jnp.float32) / half_dim
    )
    angles = jnp.concatenate(at, axis=0) * freqs
    cosine = jnp.cos(angles)
    sine = jnp.sin(angles) * jnp.where(lane < head_dim // 2, -1.0, 1.0)

    def turned(vectors):
        return (vectors * cosine + pltpu.roll(vectors, head_dim // 2, 1) * sine).astype(jnp.bfloat16)

    copy_q.wait()
    query_all = jnp.dot(normed, wq[...], preferred_element_type=jnp.float32)
    queries = [
        turned(query_all[:, head * head_dim : (head + 1) * head_dim]) for head in range(local_heads)
    ]
    copy_k.wait()
    key_new = turned(jnp.dot(normed, wk[...], preferred_element_type=jnp.float32))
    copy_v.wait()
    val_new = jnp.dot(normed, wv[...], preferred_element_type=jnp.float32).astype(jnp.bfloat16)
    slope = LOG2E * head_dim ** (-0.5)
    rows = local_heads * tree
    contract = (((1,), (1,)), ((), ()))

    def lanes_down(values, step):
        parts = [values[:, i : i + 128] for i in range(0, values.shape[1], 128)]
        return functools.reduce(step, parts)

    mixed = []
    for request in range(req_dev):
        span = slice(request * tree, (request + 1) * tree)
        own = jnp.concatenate([q[span] for q in queries], axis=0)
        allowed = jnp.concatenate([mask_ref[request]] * local_heads, axis=0) > 0
        tree_scores = lax.dot_general(
            own, key_new[span], contract, preferred_element_type=jnp.float32
        )
        tree_scores = jnp.where(allowed, tree_scores, -jnp.inf)
        limit = limits[request]

        def score_step(index, best, request=request, own=own, limit=limit):
            cache_copy(request, 0, index).wait()
            offset = pl.multiple_of(index * block, block)
            found = lax.dot_general(
                own,
                keys[request, pl.ds(offset, block)],
                contract,
                preferred_element_type=jnp.float32,
            )
            inside = offset + lax.broadcasted_iota(jnp.int32, found.shape, 1) < limit
            found = jnp.where(inside, found, -jnp.inf)
            scores[index] = found
            return jnp.maximum(best, lanes_down(found, jnp.maximum))

        best = lax.fori_loop(
            0, counts[request], score_step, jnp.full((rows, 128), -jnp.inf, jnp.float32)
        )
        peak = jnp.maximum(
            jnp.max(best, axis=1, keepdims=True), jnp.max(tree_scores, axis=1, keepdims=True)
        )
        tree_weights = jnp.exp2((tree_scores - peak) * slope)
        start = (
            jnp.zeros((rows, 128), jnp.float32),
            jnp.dot(
                tree_weights.astype(jnp.bfloat16), val_new[span], preferred_element_type=jnp.float32
            ),
        )

        def sum_step(index, carry, request=request, peak=peak):
            total, accum = carry
            cache_copy(request, 1, index).wait()
            offset = pl.multiple_of(index * block, block)
            weights = jnp.exp2((scores[index] - peak) * slope)
            accum = accum + jnp.dot(
                weights.astype(jnp.bfloat16),
                vals[request, pl.ds(offset, block)],
                preferred_element_type=jnp.float32,
            )
            return total + lanes_down(weights, jnp.add), accum

        total, accum = lax.fori_loop(0, counts[request], sum_step, start)
        total = jnp.sum(total, axis=1, keepdims=True) + jnp.sum(tree_weights, axis=1, keepdims=True)
        mixed.append((accum / total).astype(jnp.bfloat16))

    copy_o.wait()
    heads = jnp.concatenate(
        [
            jnp.concatenate(
                [found[head * tree : (head + 1) * tree] for head in range(local_heads)], axis=1
            )
            for found in mixed
        ],
        axis=0,
    )
    part = jnp.dot(heads, wo[...], preferred_element_type=jnp.float32).astype(jnp.bfloat16)
    part = part.reshape(req_dev, tree, width)
    for request in range(req_dev):

        @pl.when(first == request)
        def _(request=request):
            mine_ref[...] = part[request]

        @pl.when(first != request)
        def _(request=request):
            theirs_ref[...] = part[request]


def attention_part(
    drafts, gain, w_query, key_value_weight, w_output, cache, lengths, tree_mask, depths, tp_count
):
    req_dev, tree, width = drafts.shape
    head_dim = cache.shape[-1]
    longest = cache.shape[3]
    block = min(BLOCK, longest)
    local = w_query.shape[1]
    whole = pl.BlockSpec(memory_space=pltpu.VMEM)
    scalar = pl.BlockSpec(memory_space=pltpu.SMEM)
    anywhere = pl.BlockSpec(memory_space=pl.ANY)
    bf16 = jnp.bfloat16
    return pl.pallas_call(
        functools.partial(attention_kernel, tp_count),
        out_shape=[jax.ShapeDtypeStruct((tree, width), bf16)] * 2,
        in_specs=[scalar] + [anywhere] * 8,
        out_specs=[whole] * 2,
        scratch_shapes=[
            pltpu.VMEM((width,), jnp.float32),
            pltpu.VMEM((req_dev, tree), jnp.int32),
            pltpu.VMEM((req_dev, tree, tree), jnp.int32),
            pltpu.VMEM((req_dev, tree, width), bf16),
            pltpu.VMEM((width, local), bf16),
            pltpu.VMEM((width, head_dim), bf16),
            pltpu.VMEM((width, head_dim), bf16),
            pltpu.VMEM((local, width), bf16),
            pltpu.VMEM((req_dev, longest, head_dim), bf16),
            pltpu.VMEM((req_dev, longest, head_dim), bf16),
            pltpu.VMEM((longest // block, local // head_dim * tree, block), jnp.float32),
            pltpu.SemaphoreType.DMA((8,)),
            pltpu.SemaphoreType.DMA((req_dev, 2, longest // block)),
        ],
        compiler_params=pltpu.CompilerParams(vmem_limit_bytes=WHOLE_VMEM),
        name="attention",
    )(
        lengths,
        gain,
        depths,
        tree_mask,
        drafts,
        w_query,
        key_value_weight,
        w_output,
        cache,
    )


def dispatch_kernel(
    place_ref,
    half_ref,
    other_ref,
    drafts_ref,
    gain_ref,
    held_ref,
    router_ref,
    logits_ref,
    *rest,
):
    sent_refs, resid = rest[:-1], rest[-1]
    first = place_ref[1]
    resid[pl.ds(first, 1)] = half_ref[...].astype(jnp.float32)[None]
    resid[pl.ds(1 - first, 1)] = other_ref[...].astype(jnp.float32)[None]
    values = drafts_ref[...].astype(jnp.float32) + resid[...]
    normed = rms_norm(values, gain_ref[...][None, None, :]).astype(jnp.bfloat16)
    normed = normed.reshape(-1, normed.shape[-1])
    for step, sent_ref in enumerate(sent_refs):
        slots = lax.broadcasted_iota(
            jnp.int32, (sent_ref.shape[0], held_ref.shape[1]), 0
        )
        row = held_ref[pl.ds(place_ref[3] ^ step, 1), :]
        matrix = (row == slots).astype(jnp.bfloat16)
        sent_ref[...] = jnp.dot(matrix, normed, preferred_element_type=jnp.float32).astype(
            jnp.bfloat16
        )
    logits_ref[...] = lax.dot_general(
        normed, router_ref[...], (((1,), (1,)), ((), ())), preferred_element_type=jnp.float32
    )


def dispatch_rows(half, other, drafts, gain, held, router, place):
    req_dev, tree, width = drafts.shape
    tokens = req_dev * tree
    whole = pl.BlockSpec(memory_space=pltpu.VMEM)
    scalar = pl.BlockSpec(memory_space=pltpu.SMEM)
    logits, *sent = pl.pallas_call(
        dispatch_kernel,
        out_shape=[jax.ShapeDtypeStruct((tokens, router.shape[0]), jnp.float32)]
        + [jax.ShapeDtypeStruct((CAP, width), jnp.bfloat16)] * held.shape[0],
        in_specs=[scalar] + [whole] * 6,
        out_specs=[whole] * (1 + held.shape[0]),
        scratch_shapes=[pltpu.VMEM((req_dev, tree, width), jnp.float32)],
        compiler_params=pltpu.CompilerParams(vmem_limit_bytes=SOME_VMEM),
        name="dispatch",
    )(place, half, other, drafts, gain, held, router)
    return logits, sent


def fetch_kernel(place_ref, w_in_hbm, w_out_hbm, wi, wo, in_sem, out_sem):
    halves = wi.shape[0]
    inward = pltpu.make_async_copy(w_in_hbm, wi, in_sem)
    outward = pltpu.make_async_copy(
        w_out_hbm.at[pl.ds(place_ref[2] * halves, halves)], wo, out_sem
    )
    inward.start()
    outward.start()
    inward.wait()
    outward.wait()


def fetched(w_in_own, w_out, place):
    halves = w_in_own.shape[0]
    whole = pl.BlockSpec(memory_space=pltpu.VMEM)
    scalar = pl.BlockSpec(memory_space=pltpu.SMEM)
    anywhere = pl.BlockSpec(memory_space=pl.ANY)
    return pl.pallas_call(
        fetch_kernel,
        out_shape=[
            jax.ShapeDtypeStruct(w_in_own.shape, w_in_own.dtype),
            jax.ShapeDtypeStruct((halves,) + w_out.shape[1:], w_out.dtype),
        ],
        in_specs=[scalar, anywhere, anywhere],
        out_specs=[whole] * 2,
        scratch_shapes=[pltpu.SemaphoreType.DMA, pltpu.SemaphoreType.DMA],
        compiler_params=pltpu.CompilerParams(vmem_limit_bytes=SOME_VMEM),
        name="fetch",
    )(place, w_in_own, w_out)


def expert_kernel(place_ref, wi, wo, *rest):
    *row_refs, out_ref, rows = rest
    share = row_refs[0].shape[0]
    for step, row_ref in zip(TURNS, row_refs):
        start = pl.multiple_of((place_ref[4] ^ step) * share, share)
        rows[pl.ds(start, share)] = row_ref[...]
    taken = rows[...]
    acts = []
    for half in range(wi.shape[0]):
        gate = jnp.dot(taken, wi[half, 0], preferred_element_type=jnp.float32)
        upper = jnp.dot(taken, wi[half, 1], preferred_element_type=jnp.float32)
        acts.append((jnp.maximum(gate, 0.0) * upper).astype(jnp.bfloat16))
    acts = jnp.concatenate(acts, axis=1)
    groups, ranks, sides, _, quarter = out_ref.shape
    for rank in range(ranks):
        columns = slice(rank * quarter, (rank + 1) * quarter)
        made = jnp.dot(acts, wo[:, columns], preferred_element_type=jnp.float32)
        made = made.astype(jnp.bfloat16).reshape(sides, groups, share, quarter)
        for side in range(sides):
            out_ref[:, rank, side] = made[side]


def expert_rows(rows, w_in_own, w_out_own, place, ranks):
    share, width = rows[0].shape
    groups = len(rows)
    whole = pl.BlockSpec(memory_space=pltpu.VMEM)
    scalar = pl.BlockSpec(memory_space=pltpu.SMEM)
    return pl.pallas_call(
        expert_kernel,
        out_shape=jax.ShapeDtypeStruct(
            (groups // 2, ranks, 2, share, width // ranks), jnp.bfloat16
        ),
        in_specs=[scalar] + [whole] * (2 + groups),
        out_specs=whole,
        scratch_shapes=[pltpu.VMEM((groups * share, width), jnp.bfloat16)],
        compiler_params=pltpu.CompilerParams(vmem_limit_bytes=SOME_VMEM),
        name="experts",
    )(place, w_in_own, w_out_own, *[rows[step] for step in TURNS])


def combine_kernel(
    order_ref, rows_ref, targets_ref, gates_ref, resid_ref, slots_ref, tree_ref, posted_ref
):
    req_dev, tree, quarter = tree_ref.shape
    keep = posted_ref.shape[1]
    tokens = req_dev * tree
    places = lax.broadcasted_iota(jnp.int32, (tokens, rows_ref.shape[0]), 1)
    matrix = jnp.zeros(places.shape, jnp.float32)
    for pick in range(targets_ref.shape[1]):
        matrix = matrix + jnp.where(
            places == targets_ref[:, pick : pick + 1], gates_ref[:, pick : pick + 1], 0.0
        )
    mixture = jnp.dot(
        matrix.astype(jnp.bfloat16), rows_ref[...], preferred_element_type=jnp.float32
    )
    done = (resid_ref[...] + mixture).astype(jnp.bfloat16)
    tree_ref[...] = done.reshape(tree_ref.shape)
    posted_ref[...] = jnp.zeros_like(posted_ref)
    for request in range(req_dev):
        wanted = lax.broadcasted_iota(jnp.int32, (keep, tree), 0)
        chosen = (slots_ref[request : request + 1, :] == wanted).astype(jnp.bfloat16)
        kept = jnp.dot(
            chosen, done[request * tree : (request + 1) * tree], preferred_element_type=jnp.float32
        )
        posted_ref[pl.ds(order_ref[request], 1)] = kept.astype(jnp.bfloat16)[None]


def combine_rows(rows, targets, gates, resid, slots, order, requests):
    tokens, quarter = resid.shape
    req_dev, tree = slots.shape
    whole = pl.BlockSpec(memory_space=pltpu.VMEM)
    scalar = pl.BlockSpec(memory_space=pltpu.SMEM)
    return pl.pallas_call(
        combine_kernel,
        out_shape=[
            jax.ShapeDtypeStruct((req_dev, tree, quarter), jnp.bfloat16),
            jax.ShapeDtypeStruct((requests, KEEP, quarter), jnp.bfloat16),
        ],
        in_specs=[scalar] + [whole] * 5,
        out_specs=[whole] * 2,
        compiler_params=pltpu.CompilerParams(vmem_limit_bytes=SOME_VMEM),
        name="combine",
    )(order, rows, targets, gates, resid, slots)


def mixture(place_ref, rows_ref, pack_ref, side):
    experts, _, quarter = rows_ref.shape
    pack = jnp.transpose(pack_ref[...])
    first = place_ref[5] * (experts * CAP)
    places = lax.broadcasted_iota(jnp.int32, (pack.shape[0], experts * CAP), 1) + first
    matrix = jnp.zeros(places.shape, jnp.float32)
    for pick in range(TOPK):
        target = pack[:, pick : pick + 1].astype(jnp.int32)
        gate = pack[:, TOPK + pick : TOPK + pick + 1]
        matrix = matrix + jnp.where(places == target, gate, 0.0)
    rows = rows_ref[:, side * CAP : (side + 1) * CAP].reshape(experts * CAP, quarter)
    return jnp.dot(matrix.astype(jnp.bfloat16), rows, preferred_element_type=jnp.float32)


def gather_kernel(
    place_ref, rows_ref, own_ref, partner_ref, resid_ref, relay_ref, sum_ref, posted_ref
):
    requests, keep, quarter = posted_ref.shape
    tokens = own_ref.shape[1]
    tree = tokens // REQ_DEV
    relay = mixture(place_ref, rows_ref, partner_ref, 1).astype(jnp.bfloat16)
    relay_ref[...] = relay
    own_sum = resid_ref[...] + mixture(place_ref, rows_ref, own_ref, 0)
    sum_ref[...] = own_sum
    posted = [jnp.zeros((keep, quarter), jnp.float32)] * requests
    for pack_ref, done in (
        (own_ref, own_sum.astype(jnp.bfloat16)),
        (partner_ref, relay),
    ):
        slots = pack_ref[2 * TOPK : 2 * TOPK + 1, :].astype(jnp.int32)
        chosen = lax.broadcasted_iota(jnp.int32, (keep, tokens), 0) == slots
        homes = pack_ref[2 * TOPK + 1 : 2 * TOPK + 2, :].astype(jnp.int32)
        for request in range(REQ_DEV):
            start = request * tree
            rows = jnp.dot(
                chosen[:, start : start + tree].astype(jnp.bfloat16),
                done[start : start + tree],
                preferred_element_type=jnp.float32,
            )
            home = homes[:, start : start + 1]
            posted = [jnp.where(home == place, rows, held) for place, held in enumerate(posted)]
    for place in range(requests):
        posted_ref[place] = posted[place].astype(jnp.bfloat16)


def gathered(place, rows, own, partner, resid, requests):
    tokens, quarter = resid.shape
    whole = pl.BlockSpec(memory_space=pltpu.VMEM)
    scalar = pl.BlockSpec(memory_space=pltpu.SMEM)
    return pl.pallas_call(
        gather_kernel,
        out_shape=[
            jax.ShapeDtypeStruct((tokens, quarter), jnp.bfloat16),
            jax.ShapeDtypeStruct((tokens, quarter), jnp.float32),
            jax.ShapeDtypeStruct((requests, KEEP, quarter), jnp.bfloat16),
        ],
        in_specs=[scalar] + [whole] * 4,
        out_specs=[whole] * 3,
        compiler_params=pltpu.CompilerParams(vmem_limit_bytes=SOME_VMEM),
        name="gather",
    )(place, rows, own, partner, resid)


def finish_kernel(sum_ref, other_ref, received_ref, tree_ref, accepted_ref):
    done = (sum_ref[...] + other_ref[...].astype(jnp.float32)).astype(jnp.bfloat16)
    tree_ref[...] = done.reshape(tree_ref.shape)
    total = received_ref[0].astype(jnp.float32)
    for source in range(1, received_ref.shape[0]):
        total = total + received_ref[source].astype(jnp.float32)
    accepted_ref[...] = total.astype(jnp.bfloat16)


def finished(own_sum, other_sum, received):
    tokens, quarter = own_sum.shape
    req_dev = received.shape[1]
    whole = pl.BlockSpec(memory_space=pltpu.VMEM)
    return pl.pallas_call(
        finish_kernel,
        out_shape=[
            jax.ShapeDtypeStruct((req_dev, tokens // req_dev, quarter), jnp.bfloat16),
            jax.ShapeDtypeStruct(received.shape[1:], jnp.bfloat16),
        ],
        in_specs=[whole] * 3,
        out_specs=[whole] * 2,
        compiler_params=pltpu.CompilerParams(vmem_limit_bytes=SOME_VMEM),
        name="finish",
    )(own_sum, other_sum, received)


def on_device(
    drafts,
    gain_attn,
    w_query,
    key_value_weight,
    w_output,
    cache,
    lengths,
    tree_mask,
    depths,
    gain_moe,
    w_router,
    expert_ids,
    w_in,
    w_out,
    slots,
    order,
):
    req_dev, draft_tree, width = drafts.shape
    head_dim = cache.shape[-1]
    kv_heads = cache.shape[2]
    local_heads = w_query.shape[1] // head_dim
    tp_count = lax.axis_size("tp")
    req_count = lax.axis_size("req")
    tp_rank = lax.axis_index("tp")
    head_group = local_heads * tp_count // kv_heads
    kv_head = tp_rank * local_heads // head_group
    tokens = req_dev * draft_tree
    experts = w_router.shape[1]
    pieces = w_in.shape[0]
    quarter = width // tp_count
    first = tp_rank % 2
    req_rank = lax.axis_index("req")
    side = req_count // 2
    place = jnp.stack(
        [kv_head, first, tp_rank, req_rank, req_rank % side, req_rank // side]
    ).astype(jnp.int32)

    ids = expert_ids.reshape(tokens, -1)
    picks = ids[:, :, None] == jnp.arange(experts)[None, None, :]
    counts = jnp.sum(picks.astype(jnp.int32), axis=1)
    slot_expert = jnp.cumsum(counts, axis=0) - counts
    slot_pick = jnp.sum(jnp.where(picks, slot_expert[:, None, :], 0), axis=-1)
    held = jnp.where(counts == 1, slot_expert, -1).T
    by_expert = pieces == 2 * tp_count and req_count == 8 and req_dev == REQ_DEV
    if by_expert:
        share = CAP
        held = lax.dynamic_index_in_dim(
            held.reshape(req_count, tp_count, tokens), tp_rank, 1, keepdims=False
        )
        targets = ids * CAP + slot_pick
    else:
        share = CAP // tp_count
        held = jnp.repeat(held, 2, axis=0)
        slot_ids = tp_rank * share + jnp.arange(share)
        piece = 2 * ids[:, :, None] + jnp.arange(2)
        lane = (piece // pieces) * tp_count + (slot_pick // share)[:, :, None]
        targets = (lane * pieces + piece % pieces) * share + (slot_pick % share)[:, :, None]
        targets = targets.reshape(tokens, -1)
        matrix = (held[:, None, :] == slot_ids[None, :, None]).astype(jnp.bfloat16)
        matrix = matrix.reshape(-1, tokens)

    mine, theirs = attention_part(
        drafts,
        gain_attn,
        w_query,
        key_value_weight,
        w_output,
        cache,
        lengths,
        tree_mask,
        depths,
        tp_count,
    )
    near = [(i, i ^ 1) for i in range(tp_count)]
    far = [(i, i ^ 2) for i in range(tp_count)]

    def added(left, right):
        return (left.astype(jnp.float32) + right.astype(jnp.float32)).astype(jnp.bfloat16)

    chip = added(mine, lax.ppermute(theirs, "tp", near))
    half = added(chip, lax.ppermute(chip, "tp", far))
    other = lax.ppermute(half, "tp", near)

    if by_expert:
        logits, sent = dispatch_rows(
            half, other, drafts, gain_moe, held, w_router.T, place
        )
        arrived = [sent[0]] + [
            lax.ppermute(sent[step], "req", [(i, i ^ step) for i in range(req_count)])
            for step in range(1, req_count)
        ]
    else:
        resid = jnp.where(first == 0, jnp.stack([half, other]), jnp.stack([other, half]))
        resid = (drafts.astype(jnp.float32) + resid.astype(jnp.float32)).reshape(tokens, width)
        normed2 = rms_norm(resid, gain_moe).astype(jnp.bfloat16)
        logits = jnp.dot(normed2, w_router, preferred_element_type=jnp.float32)
        sent = jnp.dot(matrix, normed2, preferred_element_type=jnp.float32).astype(jnp.bfloat16)
        arrived = lax.all_to_all(
            sent.reshape(req_count, -1, width), "req", split_axis=0, concat_axis=0, tiled=True
        )

    chosen = jax.nn.sigmoid(jnp.sum(jnp.where(picks, logits[:, None, :], 0.0), axis=-1))
    gates = (chosen / jnp.sum(chosen, axis=1, keepdims=True)).astype(jnp.bfloat16)
    gates = gates.astype(jnp.float32)
    start = tp_rank * quarter
    own_attn = jnp.where(
        first == 0,
        jnp.concatenate([half, other], axis=0),
        jnp.concatenate([other, half], axis=0),
    )
    own_resid = lax.dynamic_slice_in_dim(
        drafts.reshape(tokens, width), start, quarter, 1
    ).astype(jnp.float32) + lax.dynamic_slice_in_dim(own_attn, start, quarter, 1).astype(
        jnp.float32
    )

    if by_expert:
        own_in = lax.dynamic_slice_in_dim(w_in, tp_rank * 2, 2, 0).transpose(0, 2, 1, 3)
        own_in, own_out = fetched(own_in, w_out, place)
        produced = expert_rows(arrived, own_in, own_out.reshape(-1, width), place, tp_count)
    else:
        gates = jnp.repeat(gates, 2, axis=1)
        rows_in = arrived.reshape(req_count, pieces, share, width)
        rows_in = rows_in.transpose(1, 0, 2, 3).reshape(pieces, req_count * share, width)
        gate_up = jnp.einsum("prd,pdgf->prgf", rows_in, w_in, preferred_element_type=jnp.float32)
        act = (jax.nn.relu(gate_up[:, :, 0]) * gate_up[:, :, 1]).astype(jnp.bfloat16)
        produced = jnp.einsum(
            "prf,pfd->prd", act, w_out, preferred_element_type=jnp.float32
        ).astype(jnp.bfloat16)
        produced = produced.reshape(pieces, req_count, share, tp_count, quarter)
        produced = produced.transpose(1, 3, 0, 2, 4)
    if by_expert:
        across = [(i, i ^ side) for i in range(req_count)]
        halves = [
            list(range(i * side * tp_count, (i + 1) * side * tp_count)) for i in range(2)
        ]
        own = jnp.concatenate(
            [
                targets.astype(jnp.float32).T,
                gates.T,
                slots.reshape(1, tokens).astype(jnp.float32),
                jnp.repeat(order, draft_tree).reshape(1, tokens).astype(jnp.float32),
                jnp.zeros((6, tokens), jnp.float32),
            ],
            axis=0,
        )
        partner = lax.ppermute(own, "req", across)
        returned = lax.all_to_all(
            produced.reshape(side * tp_count, -1, quarter),
            ("req", "tp"),
            split_axis=0,
            concat_axis=0,
            axis_index_groups=halves,
            tiled=True,
        )
        relay, own_sum, posted = gathered(
            place, returned, own, partner, own_resid, req_count * req_dev
        )
        other_sum = lax.ppermute(relay, "req", across)
    else:
        returned = lax.all_to_all(
            produced.reshape(req_count * tp_count, -1, quarter),
            ("req", "tp"),
            split_axis=0,
            concat_axis=0,
            tiled=True,
        )
        tree_out, posted = combine_rows(
            returned.reshape(-1, quarter),
            targets,
            gates,
            own_resid,
            slots,
            order,
            req_count * req_dev,
        )
    received = lax.all_to_all(
        posted.reshape(req_count, req_dev, KEEP, quarter),
        "req",
        split_axis=0,
        concat_axis=0,
        tiled=True,
    )
    if by_expert:
        tree_out, accepted = finished(own_sum, other_sum, received)
    else:
        accepted = jnp.sum(received.astype(jnp.float32), axis=0).astype(jnp.bfloat16)
    return (tree_out, accepted)


def solution(mesh):
    placed = (
        P("req", None, None),
        P(),
        P(None, "tp"),
        P(),
        P("tp", None),
        P("req", None, None, None, None),
        P("req"),
        P("req", None, None),
        P("req", None),
        P(),
        P(),
        P("req", None, None),
        P("req", None, None, None),
        P("req", None, None),
        P("req", None),
        P("req"),
    )
    return jax.shard_map(
        on_device,
        mesh=mesh,
        in_specs=placed,
        out_specs=(P("req", None, "tp"), P("req", None, "tp")),
        check_vma=False,
    )
```

```python
import functools

import jax
import jax.numpy as jnp
from jax import lax
from jax.experimental import pallas as pl
from jax.experimental.pallas import tpu as pltpu
from jax.sharding import PartitionSpec as P

KEEP = 16
CAP = 32
REQ_DEV = 2
TOPK = 4
TURNS = (1, 2, 4, 5, 6, 7, 3, 0)


EPSILON = 1e-06
THETA = 1000000.0
LOG2E = 1.4426950408889634
BLOCK = 1536
WHOLE_VMEM = 60 * 1024 * 1024
SOME_VMEM = 20 * 1024 * 1024


def rms_norm(values, gain_vec):
    return (
        values * lax.rsqrt(jnp.mean(values * values, axis=-1, keepdims=True) + EPSILON) * gain_vec
    )


def column_of(row):
    count = row.shape[1]
    at_row = lax.broadcasted_iota(jnp.int32, (count, count), 0)
    at_col = lax.broadcasted_iota(jnp.int32, (count, count), 1)
    return jnp.sum(jnp.where(at_row == at_col, row, 0.0), axis=1, keepdims=True)


def attention_kernel(
    tp_count,
    lengths_ref,
    gain_hbm,
    depths_hbm,
    mask_hbm,
    drafts_hbm,
    wq_hbm,
    wkv_hbm,
    wo_hbm,
    cache_hbm,
    mine_ref,
    theirs_ref,
    gain_ref,
    depths_ref,
    mask_ref,
    drafts,
    wq,
    wk,
    wv,
    wo,
    keys,
    vals,
    scores,
    weight_sem,
    cache_sem,
):
    req_dev, tree, width = drafts.shape
    head_dim = cache_hbm.shape[-1]
    kv_heads = cache_hbm.shape[2]
    local_heads = wq.shape[1] // head_dim
    block = scores.shape[2]
    tp_rank = lax.axis_index("tp")
    kv_head = tp_rank * local_heads // (local_heads * tp_count // kv_heads)
    first = lax.rem(tp_rank, 2)

    def column_copy(target, which, sem):
        start = pl.multiple_of((which * kv_heads + kv_head) * head_dim, head_dim)
        return pltpu.make_async_copy(wkv_hbm.at[:, pl.ds(start, head_dim)], target, sem)

    def cache_copy(request, which, index):
        rows = pl.ds(pl.multiple_of(index * block, block), block)
        target = vals if which else keys
        return pltpu.make_async_copy(
            cache_hbm.at[request, which, kv_head, rows],
            target.at[request, rows],
            cache_sem.at[request, which, index],
        )

    copy_d = pltpu.make_async_copy(drafts_hbm, drafts, weight_sem.at[4])
    copy_d.start()
    small = [
        pltpu.make_async_copy(gain_hbm, gain_ref, weight_sem.at[5]),
        pltpu.make_async_copy(depths_hbm, depths_ref, weight_sem.at[6]),
        pltpu.make_async_copy(mask_hbm, mask_ref, weight_sem.at[7]),
    ]
    for copy in small:
        copy.start()
    copy_q = pltpu.make_async_copy(wq_hbm, wq, weight_sem.at[0])
    copy_k = column_copy(wk, 0, weight_sem.at[1])
    copy_v = column_copy(wv, 1, weight_sem.at[2])
    copy_o = pltpu.make_async_copy(wo_hbm, wo, weight_sem.at[3])
    copy_q.start()
    copy_k.start()
    copy_v.start()
    limits = [lengths_ref[request] for request in range(req_dev)]
    counts = [(limit + block - 1) // block for limit in limits]
    for request in range(req_dev):
        for which in range(2):

            @pl.loop(0, counts[request])
            def _(index, request=request, which=which):
                cache_copy(request, which, index).start()

    copy_o.start()

    copy_d.wait()
    small[0].wait()
    inputs = drafts[...].astype(jnp.float32).reshape(req_dev * tree, width)
    normed = rms_norm(inputs, gain_ref[...][None, :]).astype(jnp.bfloat16)
    small[1].wait()
    small[2].wait()
    at = [
        column_of(depths_ref[request : request + 1, :].astype(jnp.float32))
        + limits[request].astype(jnp.float32)
        for request in range(req_dev)
    ]
    lane = lax.broadcasted_iota(jnp.int32, (req_dev * tree, head_dim), 1)
    half_dim = head_dim // 2
    freqs = jnp.exp(
        -jnp.log(THETA) * lax.rem(lane, half_dim).astype(jnp.float32) / half_dim
    )
    angles = jnp.concatenate(at, axis=0) * freqs
    cosine = jnp.cos(angles)
    sine = jnp.sin(angles) * jnp.where(lane < head_dim // 2, -1.0, 1.0)

    def turned(vectors):
        return (vectors * cosine + pltpu.roll(vectors, head_dim // 2, 1) * sine).astype(jnp.bfloat16)

    copy_q.wait()
    query_all = jnp.dot(normed, wq[...], preferred_element_type=jnp.float32)
    queries = [
        turned(query_all[:, head * head_dim : (head + 1) * head_dim]) for head in range(local_heads)
    ]
    copy_k.wait()
    key_new = turned(jnp.dot(normed, wk[...], preferred_element_type=jnp.float32))
    copy_v.wait()
    val_new = jnp.dot(normed, wv[...], preferred_element_type=jnp.float32).astype(jnp.bfloat16)
    slope = LOG2E * head_dim ** (-0.5)
    rows = local_heads * tree
    contract = (((1,), (1,)), ((), ()))

    def lanes_down(values, step):
        parts = [values[:, i : i + 128] for i in range(0, values.shape[1], 128)]
        return functools.reduce(step, parts)

    mixed = []
    for request in range(req_dev):
        span = slice(request * tree, (request + 1) * tree)
        own = jnp.concatenate([q[span] for q in queries], axis=0)
        allowed = jnp.concatenate([mask_ref[request]] * local_heads, axis=0) > 0
        tree_scores = lax.dot_general(
            own, key_new[span], contract, preferred_element_type=jnp.float32
        )
        tree_scores = jnp.where(allowed, tree_scores, -jnp.inf)
        limit = limits[request]

        def score_step(index, best, request=request, own=own, limit=limit):
            cache_copy(request, 0, index).wait()
            offset = pl.multiple_of(index * block, block)
            found = lax.dot_general(
                own,
                keys[request, pl.ds(offset, block)],
                contract,
                preferred_element_type=jnp.float32,
            )
            inside = offset + lax.broadcasted_iota(jnp.int32, found.shape, 1) < limit
            found = jnp.where(inside, found, -jnp.inf)
            scores[index] = found
            return jnp.maximum(best, lanes_down(found, jnp.maximum))

        best = lax.fori_loop(
            0, counts[request], score_step, jnp.full((rows, 128), -jnp.inf, jnp.float32)
        )
        peak = jnp.maximum(
            jnp.max(best, axis=1, keepdims=True), jnp.max(tree_scores, axis=1, keepdims=True)
        )
        tree_weights = jnp.exp2((tree_scores - peak) * slope)
        start = (
            jnp.zeros((rows, 128), jnp.float32),
            jnp.dot(
                tree_weights.astype(jnp.bfloat16), val_new[span], preferred_element_type=jnp.float32
            ),
        )

        def sum_step(index, carry, request=request, peak=peak):
            total, accum = carry
            cache_copy(request, 1, index).wait()
            offset = pl.multiple_of(index * block, block)
            weights = jnp.exp2((scores[index] - peak) * slope)
            accum = accum + jnp.dot(
                weights.astype(jnp.bfloat16),
                vals[request, pl.ds(offset, block)],
                preferred_element_type=jnp.float32,
            )
            return total + lanes_down(weights, jnp.add), accum

        total, accum = lax.fori_loop(0, counts[request], sum_step, start)
        total = jnp.sum(total, axis=1, keepdims=True) + jnp.sum(tree_weights, axis=1, keepdims=True)
        mixed.append((accum / total).astype(jnp.bfloat16))

    copy_o.wait()
    heads = jnp.concatenate(
        [
            jnp.concatenate(
                [found[head * tree : (head + 1) * tree] for head in range(local_heads)], axis=1
            )
            for found in mixed
        ],
        axis=0,
    )
    part = jnp.dot(heads, wo[...], preferred_element_type=jnp.float32).astype(jnp.bfloat16)
    part = part.reshape(req_dev, tree, width)
    for request in range(req_dev):

        @pl.when(first == request)
        def _(request=request):
            mine_ref[...] = part[request]

        @pl.when(first != request)
        def _(request=request):
            theirs_ref[...] = part[request]


def attention_part(
    drafts, gain, w_query, key_value_weight, w_output, cache, lengths, tree_mask, depths, tp_count
):
    req_dev, tree, width = drafts.shape
    head_dim = cache.shape[-1]
    longest = cache.shape[3]
    block = min(BLOCK, longest)
    local = w_query.shape[1]
    whole = pl.BlockSpec(memory_space=pltpu.VMEM)
    scalar = pl.BlockSpec(memory_space=pltpu.SMEM)
    anywhere = pl.BlockSpec(memory_space=pl.ANY)
    bf16 = jnp.bfloat16
    return pl.pallas_call(
        functools.partial(attention_kernel, tp_count),
        out_shape=[jax.ShapeDtypeStruct((tree, width), bf16)] * 2,
        in_specs=[scalar] + [anywhere] * 8,
        out_specs=[whole] * 2,
        scratch_shapes=[
            pltpu.VMEM((width,), jnp.float32),
            pltpu.VMEM((req_dev, tree), jnp.int32),
            pltpu.VMEM((req_dev, tree, tree), jnp.int32),
            pltpu.VMEM((req_dev, tree, width), bf16),
            pltpu.VMEM((width, local), bf16),
            pltpu.VMEM((width, head_dim), bf16),
            pltpu.VMEM((width, head_dim), bf16),
            pltpu.VMEM((local, width), bf16),
            pltpu.VMEM((req_dev, longest, head_dim), bf16),
            pltpu.VMEM((req_dev, longest, head_dim), bf16),
            pltpu.VMEM((longest // block, local // head_dim * tree, block), jnp.float32),
            pltpu.SemaphoreType.DMA((8,)),
            pltpu.SemaphoreType.DMA((req_dev, 2, longest // block)),
        ],
        compiler_params=pltpu.CompilerParams(vmem_limit_bytes=WHOLE_VMEM),
        name="attention",
    )(
        lengths,
        gain,
        depths,
        tree_mask,
        drafts,
        w_query,
        key_value_weight,
        w_output,
        cache,
    )


def dispatch_kernel(
    place_ref,
    half_ref,
    other_ref,
    drafts_ref,
    gain_ref,
    held_ref,
    router_ref,
    logits_ref,
    *rest,
):
    sent_refs, resid = rest[:-1], rest[-1]
    first = place_ref[1]
    resid[pl.ds(first, 1)] = half_ref[...].astype(jnp.float32)[None]
    resid[pl.ds(1 - first, 1)] = other_ref[...].astype(jnp.float32)[None]
    values = drafts_ref[...].astype(jnp.float32) + resid[...]
    normed = rms_norm(values, gain_ref[...][None, None, :]).astype(jnp.bfloat16)
    normed = normed.reshape(-1, normed.shape[-1])
    for step, sent_ref in enumerate(sent_refs):
        slots = lax.broadcasted_iota(
            jnp.int32, (sent_ref.shape[0], held_ref.shape[1]), 0
        )
        row = held_ref[pl.ds(place_ref[3] ^ step, 1), :]
        matrix = (row == slots).astype(jnp.bfloat16)
        sent_ref[...] = jnp.dot(matrix, normed, preferred_element_type=jnp.float32).astype(
            jnp.bfloat16
        )
    logits_ref[...] = lax.dot_general(
        normed, router_ref[...], (((1,), (1,)), ((), ())), preferred_element_type=jnp.float32
    )


def dispatch_rows(half, other, drafts, gain, held, router, place):
    req_dev, tree, width = drafts.shape
    tokens = req_dev * tree
    whole = pl.BlockSpec(memory_space=pltpu.VMEM)
    scalar = pl.BlockSpec(memory_space=pltpu.SMEM)
    logits, *sent = pl.pallas_call(
        dispatch_kernel,
        out_shape=[jax.ShapeDtypeStruct((tokens, router.shape[0]), jnp.float32)]
        + [jax.ShapeDtypeStruct((CAP, width), jnp.bfloat16)] * held.shape[0],
        in_specs=[scalar] + [whole] * 6,
        out_specs=[whole] * (1 + held.shape[0]),
        scratch_shapes=[pltpu.VMEM((req_dev, tree, width), jnp.float32)],
        compiler_params=pltpu.CompilerParams(vmem_limit_bytes=SOME_VMEM),
        name="dispatch",
    )(place, half, other, drafts, gain, held, router)
    return logits, sent


def fetch_kernel(place_ref, w_in_hbm, w_out_hbm, wi, wo, in_sem, out_sem):
    halves = wi.shape[0]
    inward = pltpu.make_async_copy(w_in_hbm, wi, in_sem)
    outward = pltpu.make_async_copy(
        w_out_hbm.at[pl.ds(place_ref[2] * halves, halves)], wo, out_sem
    )
    inward.start()
    outward.start()
    inward.wait()
    outward.wait()


def fetched(w_in_own, w_out, place):
    halves = w_in_own.shape[0]
    whole = pl.BlockSpec(memory_space=pltpu.VMEM)
    scalar = pl.BlockSpec(memory_space=pltpu.SMEM)
    anywhere = pl.BlockSpec(memory_space=pl.ANY)
    return pl.pallas_call(
        fetch_kernel,
        out_shape=[
            jax.ShapeDtypeStruct(w_in_own.shape, w_in_own.dtype),
            jax.ShapeDtypeStruct((halves,) + w_out.shape[1:], w_out.dtype),
        ],
        in_specs=[scalar, anywhere, anywhere],
        out_specs=[whole] * 2,
        scratch_shapes=[pltpu.SemaphoreType.DMA, pltpu.SemaphoreType.DMA],
        compiler_params=pltpu.CompilerParams(vmem_limit_bytes=SOME_VMEM),
        name="fetch",
    )(place, w_in_own, w_out)


def expert_kernel(place_ref, wi, wo, *rest):
    *row_refs, out_ref, rows = rest
    share = row_refs[0].shape[0]
    for step, row_ref in zip(TURNS, row_refs):
        start = pl.multiple_of((place_ref[4] ^ step) * share, share)
        rows[pl.ds(start, share)] = row_ref[...]
    taken = rows[...]
    acts = []
    for half in range(wi.shape[0]):
        gate = jnp.dot(taken, wi[half, 0], preferred_element_type=jnp.float32)
        upper = jnp.dot(taken, wi[half, 1], preferred_element_type=jnp.float32)
        acts.append((jnp.maximum(gate, 0.0) * upper).astype(jnp.bfloat16))
    acts = jnp.concatenate(acts, axis=1)
    groups, ranks, sides, _, quarter = out_ref.shape
    for rank in range(ranks):
        columns = slice(rank * quarter, (rank + 1) * quarter)
        made = jnp.dot(acts, wo[:, columns], preferred_element_type=jnp.float32)
        made = made.astype(jnp.bfloat16).reshape(sides, groups, share, quarter)
        for side in range(sides):
            out_ref[:, rank, side] = made[side]


def expert_rows(rows, w_in_own, w_out_own, place, ranks):
    share, width = rows[0].shape
    groups = len(rows)
    whole = pl.BlockSpec(memory_space=pltpu.VMEM)
    scalar = pl.BlockSpec(memory_space=pltpu.SMEM)
    return pl.pallas_call(
        expert_kernel,
        out_shape=jax.ShapeDtypeStruct(
            (groups // 2, ranks, 2, share, width // ranks), jnp.bfloat16
        ),
        in_specs=[scalar] + [whole] * (2 + groups),
        out_specs=whole,
        scratch_shapes=[pltpu.VMEM((groups * share, width), jnp.bfloat16)],
        compiler_params=pltpu.CompilerParams(vmem_limit_bytes=SOME_VMEM),
        name="experts",
    )(place, w_in_own, w_out_own, *[rows[step] for step in TURNS])


def combine_kernel(
    order_ref, rows_ref, targets_ref, gates_ref, resid_ref, slots_ref, tree_ref, posted_ref
):
    req_dev, tree, quarter = tree_ref.shape
    keep = posted_ref.shape[1]
    tokens = req_dev * tree
    places = lax.broadcasted_iota(jnp.int32, (tokens, rows_ref.shape[0]), 1)
    matrix = jnp.zeros(places.shape, jnp.float32)
    for pick in range(targets_ref.shape[1]):
        matrix = matrix + jnp.where(
            places == targets_ref[:, pick : pick + 1], gates_ref[:, pick : pick + 1], 0.0
        )
    mixture = jnp.dot(
        matrix.astype(jnp.bfloat16), rows_ref[...], preferred_element_type=jnp.float32
    )
    done = (resid_ref[...] + mixture).astype(jnp.bfloat16)
    tree_ref[...] = done.reshape(tree_ref.shape)
    posted_ref[...] = jnp.zeros_like(posted_ref)
    for request in range(req_dev):
        wanted = lax.broadcasted_iota(jnp.int32, (keep, tree), 0)
        chosen = (slots_ref[request : request + 1, :] == wanted).astype(jnp.bfloat16)
        kept = jnp.dot(
            chosen, done[request * tree : (request + 1) * tree], preferred_element_type=jnp.float32
        )
        posted_ref[pl.ds(order_ref[request], 1)] = kept.astype(jnp.bfloat16)[None]


def combine_rows(rows, targets, gates, resid, slots, order, requests):
    tokens, quarter = resid.shape
    req_dev, tree = slots.shape
    whole = pl.BlockSpec(memory_space=pltpu.VMEM)
    scalar = pl.BlockSpec(memory_space=pltpu.SMEM)
    return pl.pallas_call(
        combine_kernel,
        out_shape=[
            jax.ShapeDtypeStruct((req_dev, tree, quarter), jnp.bfloat16),
            jax.ShapeDtypeStruct((requests, KEEP, quarter), jnp.bfloat16),
        ],
        in_specs=[scalar] + [whole] * 5,
        out_specs=[whole] * 2,
        compiler_params=pltpu.CompilerParams(vmem_limit_bytes=SOME_VMEM),
        name="combine",
    )(order, rows, targets, gates, resid, slots)


def weighted(rows_ref, matrix_ref, side):
    experts, _, quarter = rows_ref.shape
    rows = rows_ref[:, side * CAP : (side + 1) * CAP].reshape(experts * CAP, quarter)
    return jnp.dot(matrix_ref[...], rows, preferred_element_type=jnp.float32)


def gather_kernel(
    rows_ref,
    own_ref,
    partner_ref,
    own_matrix_ref,
    partner_matrix_ref,
    resid_ref,
    relay_ref,
    sum_ref,
    posted_ref,
):
    requests, keep, quarter = posted_ref.shape
    tokens = own_ref.shape[1]
    tree = tokens // REQ_DEV
    relay = weighted(rows_ref, partner_matrix_ref, 1).astype(jnp.bfloat16)
    relay_ref[...] = relay
    own_sum = resid_ref[...] + weighted(rows_ref, own_matrix_ref, 0)
    sum_ref[...] = own_sum
    posted = [jnp.zeros((keep, quarter), jnp.float32)] * requests
    for pack_ref, done in (
        (own_ref, own_sum.astype(jnp.bfloat16)),
        (partner_ref, relay),
    ):
        slots = pack_ref[2 * TOPK : 2 * TOPK + 1, :].astype(jnp.int32)
        chosen = lax.broadcasted_iota(jnp.int32, (keep, tokens), 0) == slots
        homes = pack_ref[2 * TOPK + 1 : 2 * TOPK + 2, :].astype(jnp.int32)
        for request in range(REQ_DEV):
            start = request * tree
            rows = jnp.dot(
                chosen[:, start : start + tree].astype(jnp.bfloat16),
                done[start : start + tree],
                preferred_element_type=jnp.float32,
            )
            home = homes[:, start : start + 1]
            posted = [jnp.where(home == place, rows, held) for place, held in enumerate(posted)]
    for place in range(requests):
        posted_ref[place] = posted[place].astype(jnp.bfloat16)


def gathered(rows, own, partner, matrices, resid, requests):
    tokens, quarter = resid.shape
    whole = pl.BlockSpec(memory_space=pltpu.VMEM)
    return pl.pallas_call(
        gather_kernel,
        out_shape=[
            jax.ShapeDtypeStruct((tokens, quarter), jnp.bfloat16),
            jax.ShapeDtypeStruct((tokens, quarter), jnp.float32),
            jax.ShapeDtypeStruct((requests, KEEP, quarter), jnp.bfloat16),
        ],
        in_specs=[whole] * 6,
        out_specs=[whole] * 3,
        compiler_params=pltpu.CompilerParams(vmem_limit_bytes=SOME_VMEM),
        name="gather",
    )(rows, own, partner, *matrices, resid)


def finish_kernel(sum_ref, other_ref, received_ref, tree_ref, accepted_ref):
    done = (sum_ref[...] + other_ref[...].astype(jnp.float32)).astype(jnp.bfloat16)
    tree_ref[...] = done.reshape(tree_ref.shape)
    total = received_ref[0].astype(jnp.float32)
    for source in range(1, received_ref.shape[0]):
        total = total + received_ref[source].astype(jnp.float32)
    accepted_ref[...] = total.astype(jnp.bfloat16)


def finished(own_sum, other_sum, received):
    tokens, quarter = own_sum.shape
    req_dev = received.shape[1]
    whole = pl.BlockSpec(memory_space=pltpu.VMEM)
    return pl.pallas_call(
        finish_kernel,
        out_shape=[
            jax.ShapeDtypeStruct((req_dev, tokens // req_dev, quarter), jnp.bfloat16),
            jax.ShapeDtypeStruct(received.shape[1:], jnp.bfloat16),
        ],
        in_specs=[whole] * 3,
        out_specs=[whole] * 2,
        compiler_params=pltpu.CompilerParams(vmem_limit_bytes=SOME_VMEM),
        name="finish",
    )(own_sum, other_sum, received)


def on_device(
    drafts,
    gain_attn,
    w_query,
    key_value_weight,
    w_output,
    cache,
    lengths,
    tree_mask,
    depths,
    gain_moe,
    w_router,
    expert_ids,
    w_in,
    w_out,
    slots,
    order,
):
    req_dev, draft_tree, width = drafts.shape
    head_dim = cache.shape[-1]
    kv_heads = cache.shape[2]
    local_heads = w_query.shape[1] // head_dim
    tp_count = lax.axis_size("tp")
    req_count = lax.axis_size("req")
    tp_rank = lax.axis_index("tp")
    head_group = local_heads * tp_count // kv_heads
    kv_head = tp_rank * local_heads // head_group
    tokens = req_dev * draft_tree
    experts = w_router.shape[1]
    pieces = w_in.shape[0]
    quarter = width // tp_count
    first = tp_rank % 2
    req_rank = lax.axis_index("req")
    side = req_count // 2
    place = jnp.stack(
        [kv_head, first, tp_rank, req_rank, req_rank % side, req_rank // side]
    ).astype(jnp.int32)

    ids = expert_ids.reshape(tokens, -1)
    picks = ids[:, :, None] == jnp.arange(experts)[None, None, :]
    counts = jnp.sum(picks.astype(jnp.int32), axis=1)
    slot_expert = jnp.cumsum(counts, axis=0) - counts
    slot_pick = jnp.sum(jnp.where(picks, slot_expert[:, None, :], 0), axis=-1)
    held = jnp.where(counts == 1, slot_expert, -1).T
    by_expert = pieces == 2 * tp_count and req_count == 8 and req_dev == REQ_DEV
    if by_expert:
        share = CAP
        held = lax.dynamic_index_in_dim(
            held.reshape(req_count, tp_count, tokens), tp_rank, 1, keepdims=False
        )
        targets = ids * CAP + slot_pick
    else:
        share = CAP // tp_count
        held = jnp.repeat(held, 2, axis=0)
        slot_ids = tp_rank * share + jnp.arange(share)
        piece = 2 * ids[:, :, None] + jnp.arange(2)
        lane = (piece // pieces) * tp_count + (slot_pick // share)[:, :, None]
        targets = (lane * pieces + piece % pieces) * share + (slot_pick % share)[:, :, None]
        targets = targets.reshape(tokens, -1)
        matrix = (held[:, None, :] == slot_ids[None, :, None]).astype(jnp.bfloat16)
        matrix = matrix.reshape(-1, tokens)

    mine, theirs = attention_part(
        drafts,
        gain_attn,
        w_query,
        key_value_weight,
        w_output,
        cache,
        lengths,
        tree_mask,
        depths,
        tp_count,
    )
    near = [(i, i ^ 1) for i in range(tp_count)]
    far = [(i, i ^ 2) for i in range(tp_count)]

    def added(left, right):
        return (left.astype(jnp.float32) + right.astype(jnp.float32)).astype(jnp.bfloat16)

    chip = added(mine, lax.ppermute(theirs, "tp", near))
    half = added(chip, lax.ppermute(chip, "tp", far))
    other = lax.ppermute(half, "tp", near)

    if by_expert:
        logits, sent = dispatch_rows(
            half, other, drafts, gain_moe, held, w_router.T, place
        )
        arrived = [sent[0]] + [
            lax.ppermute(sent[step], "req", [(i, i ^ step) for i in range(req_count)])
            for step in range(1, req_count)
        ]
    else:
        resid = jnp.where(first == 0, jnp.stack([half, other]), jnp.stack([other, half]))
        resid = (drafts.astype(jnp.float32) + resid.astype(jnp.float32)).reshape(tokens, width)
        normed2 = rms_norm(resid, gain_moe).astype(jnp.bfloat16)
        logits = jnp.dot(normed2, w_router, preferred_element_type=jnp.float32)
        sent = jnp.dot(matrix, normed2, preferred_element_type=jnp.float32).astype(jnp.bfloat16)
        arrived = lax.all_to_all(
            sent.reshape(req_count, -1, width), "req", split_axis=0, concat_axis=0, tiled=True
        )

    chosen = jax.nn.sigmoid(jnp.sum(jnp.where(picks, logits[:, None, :], 0.0), axis=-1))
    gates = (chosen / jnp.sum(chosen, axis=1, keepdims=True)).astype(jnp.bfloat16)
    gates = gates.astype(jnp.float32)
    start = tp_rank * quarter
    own_attn = jnp.where(
        first == 0,
        jnp.concatenate([half, other], axis=0),
        jnp.concatenate([other, half], axis=0),
    )
    own_resid = lax.dynamic_slice_in_dim(
        drafts.reshape(tokens, width), start, quarter, 1
    ).astype(jnp.float32) + lax.dynamic_slice_in_dim(own_attn, start, quarter, 1).astype(
        jnp.float32
    )

    if by_expert:
        begin = lax.optimization_barrier((tp_rank * 2, arrived[1]))[0]
        own_in = lax.dynamic_slice_in_dim(w_in, begin, 2, 0).transpose(0, 2, 1, 3)
        own_in, own_out = fetched(own_in, w_out, place)
        produced = expert_rows(arrived, own_in, own_out.reshape(-1, width), place, tp_count)
    else:
        gates = jnp.repeat(gates, 2, axis=1)
        rows_in = arrived.reshape(req_count, pieces, share, width)
        rows_in = rows_in.transpose(1, 0, 2, 3).reshape(pieces, req_count * share, width)
        gate_up = jnp.einsum("prd,pdgf->prgf", rows_in, w_in, preferred_element_type=jnp.float32)
        act = (jax.nn.relu(gate_up[:, :, 0]) * gate_up[:, :, 1]).astype(jnp.bfloat16)
        produced = jnp.einsum(
            "prf,pfd->prd", act, w_out, preferred_element_type=jnp.float32
        ).astype(jnp.bfloat16)
        produced = produced.reshape(pieces, req_count, share, tp_count, quarter)
        produced = produced.transpose(1, 3, 0, 2, 4)
    if by_expert:
        across = [(i, i ^ side) for i in range(req_count)]
        halves = [
            list(range(i * side * tp_count, (i + 1) * side * tp_count)) for i in range(2)
        ]
        own = jnp.concatenate(
            [
                targets.astype(jnp.float32).T,
                gates.T,
                slots.reshape(1, tokens).astype(jnp.float32),
                jnp.repeat(order, draft_tree).reshape(1, tokens).astype(jnp.float32),
                jnp.zeros((6, tokens), jnp.float32),
            ],
            axis=0,
        )
        partner = lax.ppermute(own, "req", across)
        places = jnp.arange(side * tp_count * CAP) + req_rank // side * (side * tp_count * CAP)

        def combining(pack):
            hits = [
                jnp.where(
                    pack[pick][:, None].astype(jnp.int32) == places[None, :],
                    pack[TOPK + pick][:, None],
                    0.0,
                )
                for pick in range(TOPK)
            ]
            return functools.reduce(jnp.add, hits).astype(jnp.bfloat16)

        returned = lax.all_to_all(
            produced.reshape(side * tp_count, -1, quarter),
            ("req", "tp"),
            split_axis=0,
            concat_axis=0,
            axis_index_groups=halves,
            tiled=True,
        )
        relay, own_sum, posted = gathered(
            returned,
            own,
            partner,
            [combining(own), combining(partner)],
            own_resid,
            req_count * req_dev,
        )
        other_sum = lax.ppermute(relay, "req", across)
    else:
        returned = lax.all_to_all(
            produced.reshape(req_count * tp_count, -1, quarter),
            ("req", "tp"),
            split_axis=0,
            concat_axis=0,
            tiled=True,
        )
        tree_out, posted = combine_rows(
            returned.reshape(-1, quarter),
            targets,
            gates,
            own_resid,
            slots,
            order,
            req_count * req_dev,
        )
    received = lax.all_to_all(
        posted.reshape(req_count, req_dev, KEEP, quarter),
        "req",
        split_axis=0,
        concat_axis=0,
        tiled=True,
    )
    if by_expert:
        tree_out, accepted = finished(own_sum, other_sum, received)
    else:
        accepted = jnp.sum(received.astype(jnp.float32), axis=0).astype(jnp.bfloat16)
    return (tree_out, accepted)


def solution(mesh):
    placed = (
        P("req", None, None),
        P(),
        P(None, "tp"),
        P(),
        P("tp", None),
        P("req", None, None, None, None),
        P("req"),
        P("req", None, None),
        P("req", None),
        P(),
        P(),
        P("req", None, None),
        P("req", None, None, None),
        P("req", None, None),
        P("req", None),
        P("req"),
    )
    return jax.shard_map(
        on_device,
        mesh=mesh,
        in_specs=placed,
        out_specs=(P("req", None, "tp"), P("req", None, "tp")),
        check_vma=False,
    )
```

```python
import functools

import jax
import jax.numpy as jnp
from jax import lax
from jax.experimental import pallas as pl
from jax.experimental.pallas import tpu as pltpu
from jax.sharding import PartitionSpec as P

KEEP = 16
CAP = 32
REQ_DEV = 2
TOPK = 4
TURNS = (1, 2, 4, 5, 6, 7, 3, 0)


EPSILON = 1e-06
THETA = 1000000.0
LOG2E = 1.4426950408889634
BLOCK = 1536
WHOLE_VMEM = 60 * 1024 * 1024
SOME_VMEM = 12 * 1024 * 1024


def rms_norm(values, gain_vec):
    return (
        values * lax.rsqrt(jnp.mean(values * values, axis=-1, keepdims=True) + EPSILON) * gain_vec
    )


def column_of(row):
    count = row.shape[1]
    at_row = lax.broadcasted_iota(jnp.int32, (count, count), 0)
    at_col = lax.broadcasted_iota(jnp.int32, (count, count), 1)
    return jnp.sum(jnp.where(at_row == at_col, row, 0.0), axis=1, keepdims=True)


def attention_kernel(
    tp_count,
    lengths_ref,
    gain_hbm,
    depths_hbm,
    mask_hbm,
    drafts_hbm,
    wq_hbm,
    wkv_hbm,
    wo_hbm,
    cache_hbm,
    mine_ref,
    theirs_ref,
    gain_ref,
    depths_ref,
    mask_ref,
    drafts,
    wq,
    wk,
    wv,
    wo,
    keys,
    vals,
    scores,
    weight_sem,
    cache_sem,
):
    req_dev, tree, width = drafts.shape
    head_dim = cache_hbm.shape[-1]
    kv_heads = cache_hbm.shape[2]
    local_heads = wq.shape[1] // head_dim
    block = scores.shape[2]
    tp_rank = lax.axis_index("tp")
    kv_head = tp_rank * local_heads // (local_heads * tp_count // kv_heads)
    first = lax.rem(tp_rank, 2)

    def column_copy(target, which, sem):
        start = pl.multiple_of((which * kv_heads + kv_head) * head_dim, head_dim)
        return pltpu.make_async_copy(wkv_hbm.at[:, pl.ds(start, head_dim)], target, sem)

    def cache_copy(request, which, index):
        rows = pl.ds(pl.multiple_of(index * block, block), block)
        target = vals if which else keys
        return pltpu.make_async_copy(
            cache_hbm.at[request, which, kv_head, rows],
            target.at[request, rows],
            cache_sem.at[request, which, index],
        )

    copy_d = pltpu.make_async_copy(drafts_hbm, drafts, weight_sem.at[4])
    copy_d.start()
    small = [
        pltpu.make_async_copy(gain_hbm, gain_ref, weight_sem.at[5]),
        pltpu.make_async_copy(depths_hbm, depths_ref, weight_sem.at[6]),
        pltpu.make_async_copy(mask_hbm, mask_ref, weight_sem.at[7]),
    ]
    for copy in small:
        copy.start()
    copy_q = pltpu.make_async_copy(wq_hbm, wq, weight_sem.at[0])
    copy_k = column_copy(wk, 0, weight_sem.at[1])
    copy_v = column_copy(wv, 1, weight_sem.at[2])
    copy_o = pltpu.make_async_copy(wo_hbm, wo, weight_sem.at[3])
    copy_q.start()
    copy_k.start()
    copy_v.start()
    limits = [lengths_ref[request] for request in range(req_dev)]
    counts = [(limit + block - 1) // block for limit in limits]
    for request in range(req_dev):
        for which in range(2):

            @pl.loop(0, counts[request])
            def _(index, request=request, which=which):
                cache_copy(request, which, index).start()

    copy_o.start()

    copy_d.wait()
    small[0].wait()
    inputs = drafts[...].astype(jnp.float32).reshape(req_dev * tree, width)
    normed = rms_norm(inputs, gain_ref[...][None, :]).astype(jnp.bfloat16)
    small[1].wait()
    small[2].wait()
    at = [
        column_of(depths_ref[request : request + 1, :].astype(jnp.float32))
        + limits[request].astype(jnp.float32)
        for request in range(req_dev)
    ]
    lane = lax.broadcasted_iota(jnp.int32, (req_dev * tree, head_dim), 1)
    half_dim = head_dim // 2
    freqs = jnp.exp(
        -jnp.log(THETA) * lax.rem(lane, half_dim).astype(jnp.float32) / half_dim
    )
    angles = jnp.concatenate(at, axis=0) * freqs
    cosine = jnp.cos(angles)
    sine = jnp.sin(angles) * jnp.where(lane < head_dim // 2, -1.0, 1.0)

    def turned(vectors):
        return (vectors * cosine + pltpu.roll(vectors, head_dim // 2, 1) * sine).astype(jnp.bfloat16)

    copy_q.wait()
    query_all = jnp.dot(normed, wq[...], preferred_element_type=jnp.float32)
    queries = [
        turned(query_all[:, head * head_dim : (head + 1) * head_dim]) for head in range(local_heads)
    ]
    copy_k.wait()
    key_new = turned(jnp.dot(normed, wk[...], preferred_element_type=jnp.float32))
    copy_v.wait()
    val_new = jnp.dot(normed, wv[...], preferred_element_type=jnp.float32).astype(jnp.bfloat16)
    slope = LOG2E * head_dim ** (-0.5)
    rows = local_heads * tree
    contract = (((1,), (1,)), ((), ()))

    def lanes_down(values, step):
        parts = [values[:, i : i + 128] for i in range(0, values.shape[1], 128)]
        return functools.reduce(step, parts)

    mixed = []
    for request in range(req_dev):
        span = slice(request * tree, (request + 1) * tree)
        own = jnp.concatenate([q[span] for q in queries], axis=0)
        allowed = jnp.concatenate([mask_ref[request]] * local_heads, axis=0) > 0
        tree_scores = lax.dot_general(
            own, key_new[span], contract, preferred_element_type=jnp.float32
        )
        tree_scores = jnp.where(allowed, tree_scores, -jnp.inf)
        limit = limits[request]

        def score_step(index, best, request=request, own=own, limit=limit):
            cache_copy(request, 0, index).wait()
            offset = pl.multiple_of(index * block, block)
            found = lax.dot_general(
                own,
                keys[request, pl.ds(offset, block)],
                contract,
                preferred_element_type=jnp.float32,
            )
            inside = offset + lax.broadcasted_iota(jnp.int32, found.shape, 1) < limit
            found = jnp.where(inside, found, -jnp.inf)
            scores[index] = found
            return jnp.maximum(best, lanes_down(found, jnp.maximum))

        best = lax.fori_loop(
            0, counts[request], score_step, jnp.full((rows, 128), -jnp.inf, jnp.float32)
        )
        peak = jnp.maximum(
            jnp.max(best, axis=1, keepdims=True), jnp.max(tree_scores, axis=1, keepdims=True)
        )
        tree_weights = jnp.exp2((tree_scores - peak) * slope)
        start = (
            jnp.zeros((rows, 128), jnp.float32),
            jnp.dot(
                tree_weights.astype(jnp.bfloat16), val_new[span], preferred_element_type=jnp.float32
            ),
        )

        def sum_step(index, carry, request=request, peak=peak):
            total, accum = carry
            cache_copy(request, 1, index).wait()
            offset = pl.multiple_of(index * block, block)
            weights = jnp.exp2((scores[index] - peak) * slope)
            accum = accum + jnp.dot(
                weights.astype(jnp.bfloat16),
                vals[request, pl.ds(offset, block)],
                preferred_element_type=jnp.float32,
            )
            return total + lanes_down(weights, jnp.add), accum

        total, accum = lax.fori_loop(0, counts[request], sum_step, start)
        total = jnp.sum(total, axis=1, keepdims=True) + jnp.sum(tree_weights, axis=1, keepdims=True)
        mixed.append((accum / total).astype(jnp.bfloat16))

    copy_o.wait()
    heads = jnp.concatenate(
        [
            jnp.concatenate(
                [found[head * tree : (head + 1) * tree] for head in range(local_heads)], axis=1
            )
            for found in mixed
        ],
        axis=0,
    )
    part = jnp.dot(heads, wo[...], preferred_element_type=jnp.float32).astype(jnp.bfloat16)
    part = part.reshape(req_dev, tree, width)
    for request in range(req_dev):

        @pl.when(first == request)
        def _(request=request):
            mine_ref[...] = part[request]

        @pl.when(first != request)
        def _(request=request):
            theirs_ref[...] = part[request]


def attention_part(
    drafts, gain, w_query, key_value_weight, w_output, cache, lengths, tree_mask, depths, tp_count
):
    req_dev, tree, width = drafts.shape
    head_dim = cache.shape[-1]
    longest = cache.shape[3]
    block = min(BLOCK, longest)
    local = w_query.shape[1]
    whole = pl.BlockSpec(memory_space=pltpu.VMEM)
    scalar = pl.BlockSpec(memory_space=pltpu.SMEM)
    anywhere = pl.BlockSpec(memory_space=pl.ANY)
    bf16 = jnp.bfloat16
    return pl.pallas_call(
        functools.partial(attention_kernel, tp_count),
        out_shape=[jax.ShapeDtypeStruct((tree, width), bf16)] * 2,
        in_specs=[scalar] + [anywhere] * 8,
        out_specs=[whole] * 2,
        scratch_shapes=[
            pltpu.VMEM((width,), jnp.float32),
            pltpu.VMEM((req_dev, tree), jnp.int32),
            pltpu.VMEM((req_dev, tree, tree), jnp.int32),
            pltpu.VMEM((req_dev, tree, width), bf16),
            pltpu.VMEM((width, local), bf16),
            pltpu.VMEM((width, head_dim), bf16),
            pltpu.VMEM((width, head_dim), bf16),
            pltpu.VMEM((local, width), bf16),
            pltpu.VMEM((req_dev, longest, head_dim), bf16),
            pltpu.VMEM((req_dev, longest, head_dim), bf16),
            pltpu.VMEM((longest // block, local // head_dim * tree, block), jnp.float32),
            pltpu.SemaphoreType.DMA((8,)),
            pltpu.SemaphoreType.DMA((req_dev, 2, longest // block)),
        ],
        compiler_params=pltpu.CompilerParams(vmem_limit_bytes=WHOLE_VMEM),
        name="attention",
    )(
        lengths,
        gain,
        depths,
        tree_mask,
        drafts,
        w_query,
        key_value_weight,
        w_output,
        cache,
    )


def dispatch_kernel(
    place_ref,
    half_ref,
    other_ref,
    drafts_ref,
    gain_ref,
    held_ref,
    router_ref,
    logits_ref,
    *rest,
):
    sent_refs, resid = rest[:-1], rest[-1]
    first = place_ref[1]
    resid[pl.ds(first, 1)] = half_ref[...].astype(jnp.float32)[None]
    resid[pl.ds(1 - first, 1)] = other_ref[...].astype(jnp.float32)[None]
    values = drafts_ref[...].astype(jnp.float32) + resid[...]
    normed = rms_norm(values, gain_ref[...][None, None, :]).astype(jnp.bfloat16)
    normed = normed.reshape(-1, normed.shape[-1])
    for step, sent_ref in enumerate(sent_refs):
        slots = lax.broadcasted_iota(
            jnp.int32, (sent_ref.shape[0], held_ref.shape[1]), 0
        )
        row = held_ref[pl.ds(place_ref[3] ^ step, 1), :]
        matrix = (row == slots).astype(jnp.bfloat16)
        sent_ref[...] = jnp.dot(matrix, normed, preferred_element_type=jnp.float32).astype(
            jnp.bfloat16
        )
    logits_ref[...] = lax.dot_general(
        normed, router_ref[...], (((1,), (1,)), ((), ())), preferred_element_type=jnp.float32
    )


def dispatch_rows(half, other, drafts, gain, held, router, place):
    req_dev, tree, width = drafts.shape
    tokens = req_dev * tree
    whole = pl.BlockSpec(memory_space=pltpu.VMEM)
    scalar = pl.BlockSpec(memory_space=pltpu.SMEM)
    logits, *sent = pl.pallas_call(
        dispatch_kernel,
        out_shape=[jax.ShapeDtypeStruct((tokens, router.shape[0]), jnp.float32)]
        + [jax.ShapeDtypeStruct((CAP, width), jnp.bfloat16)] * held.shape[0],
        in_specs=[scalar] + [whole] * 6,
        out_specs=[whole] * (1 + held.shape[0]),
        scratch_shapes=[pltpu.VMEM((req_dev, tree, width), jnp.float32)],
        compiler_params=pltpu.CompilerParams(vmem_limit_bytes=SOME_VMEM),
        name="dispatch",
    )(place, half, other, drafts, gain, held, router)
    return logits, sent


def fetch_kernel(place_ref, w_in_hbm, w_out_hbm, wi, wo, in_sem, out_sem):
    halves = wi.shape[0]
    inward = pltpu.make_async_copy(w_in_hbm, wi, in_sem)
    outward = pltpu.make_async_copy(
        w_out_hbm.at[pl.ds(place_ref[2] * halves, halves)], wo, out_sem
    )
    inward.start()
    outward.start()
    inward.wait()
    outward.wait()


def fetched(w_in_own, w_out, place):
    halves = w_in_own.shape[0]
    whole = pl.BlockSpec(memory_space=pltpu.VMEM)
    scalar = pl.BlockSpec(memory_space=pltpu.SMEM)
    anywhere = pl.BlockSpec(memory_space=pl.ANY)
    return pl.pallas_call(
        fetch_kernel,
        out_shape=[
            jax.ShapeDtypeStruct(w_in_own.shape, w_in_own.dtype),
            jax.ShapeDtypeStruct((halves,) + w_out.shape[1:], w_out.dtype),
        ],
        in_specs=[scalar, anywhere, anywhere],
        out_specs=[whole] * 2,
        scratch_shapes=[pltpu.SemaphoreType.DMA, pltpu.SemaphoreType.DMA],
        compiler_params=pltpu.CompilerParams(vmem_limit_bytes=SOME_VMEM),
        name="fetch",
    )(place, w_in_own, w_out)


def expert_kernel(place_ref, wi, wo, *rest):
    *row_refs, out_ref, rows = rest
    share = row_refs[0].shape[0]
    for step, row_ref in zip(TURNS, row_refs):
        start = pl.multiple_of((place_ref[4] ^ step) * share, share)
        rows[pl.ds(start, share)] = row_ref[...]
    taken = rows[...]
    acts = []
    for half in range(wi.shape[0]):
        gate = jnp.dot(taken, wi[half, 0], preferred_element_type=jnp.float32)
        upper = jnp.dot(taken, wi[half, 1], preferred_element_type=jnp.float32)
        acts.append((jnp.maximum(gate, 0.0) * upper).astype(jnp.bfloat16))
    acts = jnp.concatenate(acts, axis=1)
    groups, ranks, sides, _, quarter = out_ref.shape
    for rank in range(ranks):
        columns = slice(rank * quarter, (rank + 1) * quarter)
        made = jnp.dot(acts, wo[:, columns], preferred_element_type=jnp.float32)
        made = made.astype(jnp.bfloat16).reshape(sides, groups, share, quarter)
        for side in range(sides):
            out_ref[:, rank, side] = made[side]


def expert_rows(rows, w_in_own, w_out_own, place, ranks):
    share, width = rows[0].shape
    groups = len(rows)
    whole = pl.BlockSpec(memory_space=pltpu.VMEM)
    scalar = pl.BlockSpec(memory_space=pltpu.SMEM)
    return pl.pallas_call(
        expert_kernel,
        out_shape=jax.ShapeDtypeStruct(
            (groups // 2, ranks, 2, share, width // ranks), jnp.bfloat16
        ),
        in_specs=[scalar] + [whole] * (2 + groups),
        out_specs=whole,
        scratch_shapes=[pltpu.VMEM((groups * share, width), jnp.bfloat16)],
        compiler_params=pltpu.CompilerParams(vmem_limit_bytes=SOME_VMEM),
        name="experts",
    )(place, w_in_own, w_out_own, *[rows[step] for step in TURNS])


def combine_kernel(
    order_ref, rows_ref, targets_ref, gates_ref, resid_ref, slots_ref, tree_ref, posted_ref
):
    req_dev, tree, quarter = tree_ref.shape
    keep = posted_ref.shape[1]
    tokens = req_dev * tree
    places = lax.broadcasted_iota(jnp.int32, (tokens, rows_ref.shape[0]), 1)
    matrix = jnp.zeros(places.shape, jnp.float32)
    for pick in range(targets_ref.shape[1]):
        matrix = matrix + jnp.where(
            places == targets_ref[:, pick : pick + 1], gates_ref[:, pick : pick + 1], 0.0
        )
    mixture = jnp.dot(
        matrix.astype(jnp.bfloat16), rows_ref[...], preferred_element_type=jnp.float32
    )
    done = (resid_ref[...] + mixture).astype(jnp.bfloat16)
    tree_ref[...] = done.reshape(tree_ref.shape)
    posted_ref[...] = jnp.zeros_like(posted_ref)
    for request in range(req_dev):
        wanted = lax.broadcasted_iota(jnp.int32, (keep, tree), 0)
        chosen = (slots_ref[request : request + 1, :] == wanted).astype(jnp.bfloat16)
        kept = jnp.dot(
            chosen, done[request * tree : (request + 1) * tree], preferred_element_type=jnp.float32
        )
        posted_ref[pl.ds(order_ref[request], 1)] = kept.astype(jnp.bfloat16)[None]


def combine_rows(rows, targets, gates, resid, slots, order, requests):
    tokens, quarter = resid.shape
    req_dev, tree = slots.shape
    whole = pl.BlockSpec(memory_space=pltpu.VMEM)
    scalar = pl.BlockSpec(memory_space=pltpu.SMEM)
    return pl.pallas_call(
        combine_kernel,
        out_shape=[
            jax.ShapeDtypeStruct((req_dev, tree, quarter), jnp.bfloat16),
            jax.ShapeDtypeStruct((requests, KEEP, quarter), jnp.bfloat16),
        ],
        in_specs=[scalar] + [whole] * 5,
        out_specs=[whole] * 2,
        compiler_params=pltpu.CompilerParams(vmem_limit_bytes=SOME_VMEM),
        name="combine",
    )(order, rows, targets, gates, resid, slots)


def weighted(rows_ref, matrix_ref, side):
    experts, _, quarter = rows_ref.shape
    rows = rows_ref[:, side * CAP : (side + 1) * CAP].reshape(experts * CAP, quarter)
    return jnp.dot(matrix_ref[...], rows, preferred_element_type=jnp.float32)


def gather_kernel(
    rows_ref,
    own_ref,
    partner_ref,
    own_matrix_ref,
    partner_matrix_ref,
    resid_ref,
    relay_ref,
    sum_ref,
    posted_ref,
):
    requests, keep, quarter = posted_ref.shape
    tokens = own_ref.shape[1]
    tree = tokens // REQ_DEV
    relay = weighted(rows_ref, partner_matrix_ref, 1).astype(jnp.bfloat16)
    relay_ref[...] = relay
    own_sum = resid_ref[...] + weighted(rows_ref, own_matrix_ref, 0)
    sum_ref[...] = own_sum
    posted = [jnp.zeros((keep, quarter), jnp.float32)] * requests
    for pack_ref, done in (
        (own_ref, own_sum.astype(jnp.bfloat16)),
        (partner_ref, relay),
    ):
        slots = pack_ref[2 * TOPK : 2 * TOPK + 1, :].astype(jnp.int32)
        chosen = lax.broadcasted_iota(jnp.int32, (keep, tokens), 0) == slots
        homes = pack_ref[2 * TOPK + 1 : 2 * TOPK + 2, :].astype(jnp.int32)
        for request in range(REQ_DEV):
            start = request * tree
            rows = jnp.dot(
                chosen[:, start : start + tree].astype(jnp.bfloat16),
                done[start : start + tree],
                preferred_element_type=jnp.float32,
            )
            home = homes[:, start : start + 1]
            posted = [jnp.where(home == place, rows, held) for place, held in enumerate(posted)]
    for place in range(requests):
        posted_ref[place] = posted[place].astype(jnp.bfloat16)


def gathered(rows, own, partner, matrices, resid, requests):
    tokens, quarter = resid.shape
    whole = pl.BlockSpec(memory_space=pltpu.VMEM)
    return pl.pallas_call(
        gather_kernel,
        out_shape=[
            jax.ShapeDtypeStruct((tokens, quarter), jnp.bfloat16),
            jax.ShapeDtypeStruct((tokens, quarter), jnp.float32),
            jax.ShapeDtypeStruct((requests, KEEP, quarter), jnp.bfloat16),
        ],
        in_specs=[whole] * 6,
        out_specs=[whole] * 3,
        compiler_params=pltpu.CompilerParams(vmem_limit_bytes=SOME_VMEM),
        name="gather",
    )(rows, own, partner, *matrices, resid)


def finish_kernel(sum_ref, other_ref, received_ref, tree_ref, accepted_ref):
    done = (sum_ref[...] + other_ref[...].astype(jnp.float32)).astype(jnp.bfloat16)
    tree_ref[...] = done.reshape(tree_ref.shape)
    total = received_ref[0].astype(jnp.float32)
    for source in range(1, received_ref.shape[0]):
        total = total + received_ref[source].astype(jnp.float32)
    accepted_ref[...] = total.astype(jnp.bfloat16)


def finished(own_sum, other_sum, received):
    tokens, quarter = own_sum.shape
    req_dev = received.shape[1]
    whole = pl.BlockSpec(memory_space=pltpu.VMEM)
    return pl.pallas_call(
        finish_kernel,
        out_shape=[
            jax.ShapeDtypeStruct((req_dev, tokens // req_dev, quarter), jnp.bfloat16),
            jax.ShapeDtypeStruct(received.shape[1:], jnp.bfloat16),
        ],
        in_specs=[whole] * 3,
        out_specs=[whole] * 2,
        compiler_params=pltpu.CompilerParams(vmem_limit_bytes=SOME_VMEM),
        name="finish",
    )(own_sum, other_sum, received)


def on_device(
    drafts,
    gain_attn,
    w_query,
    key_value_weight,
    w_output,
    cache,
    lengths,
    tree_mask,
    depths,
    gain_moe,
    w_router,
    expert_ids,
    w_in,
    w_out,
    slots,
    order,
):
    req_dev, draft_tree, width = drafts.shape
    head_dim = cache.shape[-1]
    kv_heads = cache.shape[2]
    local_heads = w_query.shape[1] // head_dim
    tp_count = lax.axis_size("tp")
    req_count = lax.axis_size("req")
    tp_rank = lax.axis_index("tp")
    head_group = local_heads * tp_count // kv_heads
    kv_head = tp_rank * local_heads // head_group
    tokens = req_dev * draft_tree
    experts = w_router.shape[1]
    pieces = w_in.shape[0]
    quarter = width // tp_count
    first = tp_rank % 2
    req_rank = lax.axis_index("req")
    side = req_count // 2
    place = jnp.stack(
        [kv_head, first, tp_rank, req_rank, req_rank % side, req_rank // side]
    ).astype(jnp.int32)

    ids = expert_ids.reshape(tokens, -1)
    picks = ids[:, :, None] == jnp.arange(experts)[None, None, :]
    counts = jnp.sum(picks.astype(jnp.int32), axis=1)
    slot_expert = jnp.cumsum(counts, axis=0) - counts
    slot_pick = jnp.sum(jnp.where(picks, slot_expert[:, None, :], 0), axis=-1)
    held = jnp.where(counts == 1, slot_expert, -1).T
    by_expert = pieces == 2 * tp_count and req_count == 8 and req_dev == REQ_DEV
    if by_expert:
        share = CAP
        held = lax.dynamic_index_in_dim(
            held.reshape(req_count, tp_count, tokens), tp_rank, 1, keepdims=False
        )
        targets = ids * CAP + slot_pick
    else:
        share = CAP // tp_count
        held = jnp.repeat(held, 2, axis=0)
        slot_ids = tp_rank * share + jnp.arange(share)
        piece = 2 * ids[:, :, None] + jnp.arange(2)
        lane = (piece // pieces) * tp_count + (slot_pick // share)[:, :, None]
        targets = (lane * pieces + piece % pieces) * share + (slot_pick % share)[:, :, None]
        targets = targets.reshape(tokens, -1)
        matrix = (held[:, None, :] == slot_ids[None, :, None]).astype(jnp.bfloat16)
        matrix = matrix.reshape(-1, tokens)

    mine, theirs = attention_part(
        drafts,
        gain_attn,
        w_query,
        key_value_weight,
        w_output,
        cache,
        lengths,
        tree_mask,
        depths,
        tp_count,
    )
    near = [(i, i ^ 1) for i in range(tp_count)]
    far = [(i, i ^ 2) for i in range(tp_count)]

    def added(left, right):
        return (left.astype(jnp.float32) + right.astype(jnp.float32)).astype(jnp.bfloat16)

    chip = added(mine, lax.ppermute(theirs, "tp", near))
    half = added(chip, lax.ppermute(chip, "tp", far))
    other = lax.ppermute(half, "tp", near)

    if by_expert:
        logits, sent = dispatch_rows(
            half, other, drafts, gain_moe, held, w_router.T, place
        )
        arrived = [sent[0]] + [
            lax.ppermute(sent[step], "req", [(i, i ^ step) for i in range(req_count)])
            for step in range(1, req_count)
        ]
    else:
        resid = jnp.where(first == 0, jnp.stack([half, other]), jnp.stack([other, half]))
        resid = (drafts.astype(jnp.float32) + resid.astype(jnp.float32)).reshape(tokens, width)
        normed2 = rms_norm(resid, gain_moe).astype(jnp.bfloat16)
        logits = jnp.dot(normed2, w_router, preferred_element_type=jnp.float32)
        sent = jnp.dot(matrix, normed2, preferred_element_type=jnp.float32).astype(jnp.bfloat16)
        arrived = lax.all_to_all(
            sent.reshape(req_count, -1, width), "req", split_axis=0, concat_axis=0, tiled=True
        )

    chosen = jax.nn.sigmoid(jnp.sum(jnp.where(picks, logits[:, None, :], 0.0), axis=-1))
    gates = (chosen / jnp.sum(chosen, axis=1, keepdims=True)).astype(jnp.bfloat16)
    gates = gates.astype(jnp.float32)
    start = tp_rank * quarter
    own_attn = jnp.where(
        first == 0,
        jnp.concatenate([half, other], axis=0),
        jnp.concatenate([other, half], axis=0),
    )
    own_resid = lax.dynamic_slice_in_dim(
        drafts.reshape(tokens, width), start, quarter, 1
    ).astype(jnp.float32) + lax.dynamic_slice_in_dim(own_attn, start, quarter, 1).astype(
        jnp.float32
    )

    if by_expert:
        begin = lax.optimization_barrier((tp_rank * 2, arrived[1]))[0]
        own_in = lax.dynamic_slice_in_dim(w_in, begin, 2, 0).transpose(0, 2, 1, 3)
        own_in, own_out = fetched(own_in, w_out, place)
        produced = expert_rows(arrived, own_in, own_out.reshape(-1, width), place, tp_count)
    else:
        gates = jnp.repeat(gates, 2, axis=1)
        rows_in = arrived.reshape(req_count, pieces, share, width)
        rows_in = rows_in.transpose(1, 0, 2, 3).reshape(pieces, req_count * share, width)
        gate_up = jnp.einsum("prd,pdgf->prgf", rows_in, w_in, preferred_element_type=jnp.float32)
        act = (jax.nn.relu(gate_up[:, :, 0]) * gate_up[:, :, 1]).astype(jnp.bfloat16)
        produced = jnp.einsum(
            "prf,pfd->prd", act, w_out, preferred_element_type=jnp.float32
        ).astype(jnp.bfloat16)
        produced = produced.reshape(pieces, req_count, share, tp_count, quarter)
        produced = produced.transpose(1, 3, 0, 2, 4)
    if by_expert:
        across = [(i, i ^ side) for i in range(req_count)]
        halves = [
            list(range(i * side * tp_count, (i + 1) * side * tp_count)) for i in range(2)
        ]
        own = jnp.concatenate(
            [
                targets.astype(jnp.float32).T,
                gates.T,
                slots.reshape(1, tokens).astype(jnp.float32),
                jnp.repeat(order, draft_tree).reshape(1, tokens).astype(jnp.float32),
                jnp.zeros((6, tokens), jnp.float32),
            ],
            axis=0,
        )
        partner = lax.ppermute(own, "req", across)
        places = jnp.arange(side * tp_count * CAP) + req_rank // side * (side * tp_count * CAP)

        def combining(pack):
            hits = [
                jnp.where(
                    pack[pick][:, None].astype(jnp.int32) == places[None, :],
                    pack[TOPK + pick][:, None],
                    0.0,
                )
                for pick in range(TOPK)
            ]
            return functools.reduce(jnp.add, hits).astype(jnp.bfloat16)

        returned = lax.all_to_all(
            produced.reshape(side * tp_count, -1, quarter),
            ("req", "tp"),
            split_axis=0,
            concat_axis=0,
            axis_index_groups=halves,
            tiled=True,
        )
        relay, own_sum, posted = gathered(
            returned,
            own,
            partner,
            [combining(own), combining(partner)],
            own_resid,
            req_count * req_dev,
        )
        other_sum = lax.ppermute(relay, "req", across)
    else:
        returned = lax.all_to_all(
            produced.reshape(req_count * tp_count, -1, quarter),
            ("req", "tp"),
            split_axis=0,
            concat_axis=0,
            tiled=True,
        )
        tree_out, posted = combine_rows(
            returned.reshape(-1, quarter),
            targets,
            gates,
            own_resid,
            slots,
            order,
            req_count * req_dev,
        )
    received = lax.all_to_all(
        posted.reshape(req_count, req_dev, KEEP, quarter),
        "req",
        split_axis=0,
        concat_axis=0,
        tiled=True,
    )
    if by_expert:
        tree_out, accepted = finished(own_sum, other_sum, received)
    else:
        accepted = jnp.sum(received.astype(jnp.float32), axis=0).astype(jnp.bfloat16)
    return (tree_out, accepted)


def solution(mesh):
    placed = (
        P("req", None, None),
        P(),
        P(None, "tp"),
        P(),
        P("tp", None),
        P("req", None, None, None, None),
        P("req"),
        P("req", None, None),
        P("req", None),
        P(),
        P(),
        P("req", None, None),
        P("req", None, None, None),
        P("req", None, None),
        P("req", None),
        P("req"),
    )
    return jax.shard_map(
        on_device,
        mesh=mesh,
        in_specs=placed,
        out_specs=(P("req", None, "tp"), P("req", None, "tp")),
        check_vma=False,
    )
```
